128 devices in a mesh: dev: 128 (over y, z, x, core).
Axes of the slice: x: 4, y: 4, z: 4, core: 2. Of those that a mesh axis runs over, the one named last changes fastest.
Arguments:
- dynamics: float32 [2, 72, 65536], P(None, None, 'dev'), may hold values from -6 to 6
- adjacency: int32 [2, 16384], P(None, 'dev'), may hold values from 0 to 4095, as said below
- cloud_state: float32 [2, 58, 64, 16384], P(None, None, None, 'dev'), may hold values from -6 to 6
- span_source: int32 [16384], P('dev'), may hold values from 0 to 16383, as said below
- substeps: int32 [1024], P('dev'), may hold values from 1 to 12
Outputs:
- dynamics_summed: float32 [2, 72, 65536], P(None, None, 'dev')
- tendency: float32 [2, 58, 16384], P(None, None, 'dev')
- cloud_new: float32 [2, 58, 64, 16384], P(None, None, None, 'dev')
The draws below stay inside these ranges and needn't reach their ends.
Inputs may be any that keep to these rules, and one draw needn't show every extreme that they name: `adjacency`: edges match in pairs: edge k of e faces edge m of f exactly when edge m of f faces edge k of e. The element across an edge belongs to the same block of 32 elements or to the block just below or above, cyclically. `span_source`: A permutation of the columns. Each block of 128 slots holds exactly 1 column of each block of 128 columns.
All inputs are finite; a program needn't handle non-finite values.
Results may differ from the reference program's by a relative error of at most 0.0003.
Values sent between devices are 32-bit elements; how exact they have to be, the bound alone decides.
A program may use at most 128 MiB of HBM per device.

```python
import jax
import jax.numpy as jnp
from jax import lax

EL_DEV = 32
ELEMS = 4096
NODES = 16
FIELDS = 2
LEV = 72
CRM_Z = 58
CRM_X = 64
COLS_DEV = 128
COLS = 16384
SPAN = 16
SPANS = 1024
PER_PEER = 1
SUB_MAX = 12


def heavy_spans(key):
    per_device = COLS_DEV // SPAN
    blocks = COLS // COLS_DEV
    return jax.random.randint(jax.random.fold_in(key, 901), (blocks,), 0, per_device).astype(jnp.int32)


def draw_adjacency(key, part):
    key = jax.random.fold_in(key, 10)
    grid_rows = ELEMS // EL_DEV
    key_one, key_two = jax.random.split(key)
    row_keys = jax.random.split(key_one, grid_rows)
    shuffles = jax.vmap(lambda k: jax.random.permutation(k, EL_DEV))(row_keys)
    element_id = (jnp.arange(grid_rows, dtype=jnp.int32)[:, None] * EL_DEV + shuffles).astype(jnp.int32)
    rotation = jax.random.randint(key_two, (grid_rows, EL_DEV), 0, 4)
    direction = (jnp.arange(4, dtype=jnp.int32)[None, None, :] + rotation[:, :, None]) % 4
    row_step = jnp.array([-1, 0, 1, 0], jnp.int32)[direction]
    col_step = jnp.array([0, 1, 0, -1], jnp.int32)[direction]
    near_row = (jnp.arange(grid_rows, dtype=jnp.int32)[:, None, None] + row_step) % grid_rows
    near_col = (jnp.arange(EL_DEV, dtype=jnp.int32)[None, :, None] + col_step) % EL_DEV
    neighbour = element_id[near_row, near_col]
    facing = (direction + 2 - rotation[near_row, near_col]) % 4
    flat_id = element_id.reshape(-1)
    first = jnp.zeros((ELEMS, 4), jnp.int32).at[flat_id].set(neighbour.reshape(-1, 4))
    second = jnp.zeros((ELEMS, 4), jnp.int32).at[flat_id].set(facing.reshape(-1, 4))
    return jnp.stack([first.reshape(-1), second.reshape(-1)]).astype(jnp.int32)


def draw_span_source(key, part):
    heavy = heavy_spans(key)
    key = jax.random.fold_in(key, 11)
    blocks = COLS // COLS_DEV
    per_device = COLS_DEV // SPAN
    key_one, key_two, key_three, key_four = jax.random.split(key, 4)
    shuffles = jax.vmap(lambda k: jax.random.permutation(k, COLS_DEV))(jax.random.split(key_one, blocks))
    grouped = (shuffles + jnp.arange(blocks, dtype=jnp.int32)[:, None] * COLS_DEV).reshape(blocks, blocks, PER_PEER)
    offsets = jax.random.randint(key_two, (blocks,), 0, blocks)
    hot_start = jax.random.randint(key_three, (), 0, blocks).astype(jnp.int32)
    target = jnp.arange(blocks, dtype=jnp.int32)[:, None]
    source = jnp.broadcast_to(jnp.arange(blocks, dtype=jnp.int32)[None, :], (blocks, blocks))
    owner = (source + hot_start) % blocks
    group = (target - offsets[owner]) % blocks
    chosen = grouped[owner, group].reshape(blocks, per_device, SPAN)
    mixing = jax.vmap(lambda k: jax.random.permutation(k, SPAN))(jax.random.split(key_four, blocks * per_device))
    rows = jnp.take_along_axis(chosen, mixing.reshape(blocks, per_device, SPAN), axis=2)
    from_row = (jnp.arange(per_device, dtype=jnp.int32)[None, :] - heavy[:, None]) % per_device
    slots = jnp.take_along_axis(rows, jnp.broadcast_to(from_row[:, :, None], rows.shape), axis=1)
    return slots.reshape(-1).astype(jnp.int32)


def draw_substeps(key, part):
    heavy = heavy_spans(key)
    key = jax.random.fold_in(key, 12)
    per_device = COLS_DEV // SPAN
    blocks = SPANS // per_device
    key_one, key_two, key_three = jax.random.split(key, 3)
    index = jnp.arange(SPANS, dtype=jnp.int32)
    owner_block = index // per_device
    local = index % per_device
    is_heavy = local == heavy[owner_block]
    high = jax.random.randint(key_one, (SPANS,), SUB_MAX - 2, SUB_MAX + 1)
    low = jax.random.randint(key_two, (SPANS,), 1, 3)
    counts = jnp.where(is_heavy, high, low)
    picked = jax.random.randint(key_three, (), 0, blocks).astype(jnp.int32)
    stiffest = picked * per_device + heavy[picked]
    return jnp.where(index == stiffest, SUB_MAX, counts).astype(jnp.int32)


def steps_of(own_key, extent, cuts, least, largest):
    factor_of, own = 1.0, jax.random.fold_in(own_key, 6)
    for dim, shards_of in cuts:
        steps = jnp.exp(jax.random.uniform(jax.random.fold_in(own, dim), (shards_of,), jnp.float32, least / len(cuts), largest / len(cuts)))
        factor_of = factor_of * jnp.repeat(steps, extent[dim] // shards_of).reshape([-1 if axis == dim else 1 for axis in range(len(extent))])
    return factor_of


def gaussian(stream_key, extent, width, bound, pieces=(), kind=jnp.bfloat16):
    result = jax.random.normal(stream_key, extent, jnp.float32) * width
    if len(pieces) > 0:
        result = steps_of(stream_key, extent, pieces, -0.22, 0.18) * result
    return jnp.clip(result, min=-bound, max=bound).astype(kind)


def setup_inputs(seed: int = 0) -> dict:
    splits = jax.random.split(jax.random.key(seed), 6)
    return {
        "dynamics": gaussian(splits[0], (FIELDS, LEV, ELEMS * NODES), 1.0, 6.0, ((2, 128),), jnp.float32),
        "adjacency": draw_adjacency(jax.random.fold_in(splits[5], 71), 0),
        "cloud_state": gaussian(splits[2], (FIELDS, CRM_Z, CRM_X, COLS), 1.0, 6.0, ((3, 128),), jnp.float32),
        "span_source": draw_span_source(jax.random.fold_in(splits[5], 71), 0),
        "substeps": draw_substeps(jax.random.fold_in(splits[5], 71), 0),
    }


edge_nodes = ((1, 2), (7, 11), (14, 13), (8, 4))
relax_rate = 0.3
diffusion = 0.1
latent_heat = 1.0


def edge_sum(node_values, adjacency):
    elements = node_values.shape[2]
    edge_index = jnp.array(edge_nodes, jnp.int32).reshape(8)
    edge_values = node_values[..., edge_index].reshape(node_values.shape[0], node_values.shape[1], elements * 8)
    neighbour = adjacency[0].reshape(elements, 4)
    facing = adjacency[1].reshape(elements, 4)
    partner = (neighbour * 8 + facing * 2)[:, :, None] + jnp.array([1, 0], jnp.int32)[None, None, :]
    opposite = edge_values[..., partner.reshape(-1)]
    averaged = 0.5 * (edge_values + opposite)
    return node_values.at[..., edge_index].set(averaged.reshape(node_values.shape[0], node_values.shape[1], elements, 8))


def column_means(node_values):
    fields, levels, elements = node_values.shape[0], node_values.shape[1], node_values.shape[2]
    blocks = node_values.reshape(fields, levels, elements, 2, 2, 2, 2)
    return jnp.mean(blocks, axis=(4, 6)).reshape(fields, levels, elements * 4)


def cloud_step(state, forcing, counts, trip_count):
    depth = state.shape[1]
    heights = jnp.arange(depth).astype(jnp.float32)
    saturation = (0.8 * jnp.exp(-2.0 * heights / depth))[:, None, None]
    start_mean = jnp.mean(state, axis=2)

    def substep(step_index, current):
        average = jnp.mean(current, axis=2)
        relaxed = current + relax_rate * (forcing - average)[:, :, None, :]
        above = jnp.concatenate([relaxed[:, 1:], relaxed[:, -1:]], axis=1)
        below = jnp.concatenate([relaxed[:, :1], relaxed[:, :-1]], axis=1)
        laplace = jnp.roll(relaxed, 1, axis=2) + jnp.roll(relaxed, -1, axis=2) + above + below - 4.0 * relaxed
        diffused = relaxed + diffusion * laplace
        condensed = 0.5 * jnp.maximum(diffused[1] - saturation - 0.5 * diffused[0], 0.0)
        stepped = jnp.stack([diffused[0] + latent_heat * condensed, diffused[1] - condensed])
        active = (step_index < counts)[None, None, None, :]
        return jnp.where(active, stepped, current)

    final = lax.fori_loop(0, trip_count, substep, state)
    return final, jnp.mean(final, axis=2) - start_mean


def reference(dynamics, adjacency, cloud_state, span_source, substeps):
    fields, levels, node_count = dynamics.shape
    elements = node_count // 16
    node_values = edge_sum(dynamics.reshape(fields, levels, elements, 16), adjacency)
    dynamics_summed = node_values.reshape(fields, levels, node_count)
    forcing = column_means(node_values)[:, :CRM_Z]
    slot_state = cloud_state[..., span_source]
    slot_forcing = forcing[..., span_source]
    slot_counts = jnp.repeat(substeps, SPAN)

    def one_span(index):
        start = (index * SPAN).astype(jnp.int32)
        state = lax.dynamic_slice_in_dim(slot_state, start, SPAN, 3)
        force = lax.dynamic_slice_in_dim(slot_forcing, start, SPAN, 2)
        counts = lax.dynamic_slice_in_dim(slot_counts, start, SPAN, 0)
        return cloud_step(state, force, counts, SUB_MAX)

    new_blocks, tend_blocks = lax.map(one_span, jnp.arange(SPANS, dtype=jnp.int32))
    new_slots = jnp.moveaxis(new_blocks, 0, 3).reshape(fields, CRM_Z, CRM_X, COLS)
    tend_slots = jnp.moveaxis(tend_blocks, 0, 2).reshape(fields, CRM_Z, COLS)
    cloud_new = jnp.zeros_like(cloud_state).at[..., span_source].set(new_slots)
    tendency = jnp.zeros((fields, CRM_Z, COLS), jnp.float32).at[..., span_source].set(tend_slots)
    return dynamics_summed, tendency, cloud_new
```

```python
import functools

import jax
import jax.numpy as jnp
from jax import lax
from jax.experimental import pallas as pl
from jax.experimental.pallas import tpu as pltpu
from jax.sharding import PartitionSpec as P

LANES = 128
ROWS = 8
GROUP = 8
PAD = 8
CHUNKS = 6
UNROLL = 58


def odious(node):
    return ((node ^ (node >> 1) ^ (node >> 2) ^ (node >> 3)) & 1) == 1


def edge_of(node):
    return jnp.where(
        (node == 1) | (node == 2), 0, jnp.where((node == 7) | (node == 11), 1, jnp.where((node == 14) | (node == 13), 2, 3))
    )


def which_of(node):
    return jnp.where((node == 2) | (node == 11) | (node == 13) | (node == 4), 1, 0)


def lanes(shape=(ROWS, LANES)):
    return lax.broadcasted_iota(jnp.int32, shape, len(shape) - 1)


def total_of(parts):
    while len(parts) > 1:
        parts = [a + b for a, b in zip(parts[::2], parts[1::2])] + ([parts[-1]] if len(parts) % 2 else [])
    return parts[0]


def exchange_kernel(
    devices, span, dyn_ref, source_ref, sub_ref, halo_ref, count_ref, edges, outgoing, arrived, second, arrived2,
    halo_send, halo_recv, own_sem, one_send, one_recv, two_send, two_recv,
):
    me = lax.axis_index("dev")
    groups = devices // GROUP
    group = me // GROUP
    member = me % GROUP
    above = (me + 1) % devices
    below = (me + devices - 1) % devices

    barrier = pltpu.get_barrier_semaphore()
    for step in range(1, groups):
        pl.semaphore_signal(barrier, inc=1, device_id=(((group + step) % groups) * GROUP + member,), device_id_type=pl.DeviceIdType.MESH)
    for step in range(1, GROUP):
        pl.semaphore_signal(barrier, inc=1, device_id=(group * GROUP + (member + step) % GROUP,), device_id_type=pl.DeviceIdType.MESH)
    pl.semaphore_signal(barrier, inc=1, device_id=(above,), device_id_type=pl.DeviceIdType.MESH)
    pl.semaphore_signal(barrier, inc=1, device_id=(below,), device_id_type=pl.DeviceIdType.MESH)

    fields, levels, _ = dyn_ref.shape
    on_edge = odious(lanes((levels, LANES)) % 16)
    for f in range(fields):
        for j in range(2):
            first = dyn_ref[f, :, 2 * j * LANES : (2 * j + 1) * LANES]
            later = dyn_ref[f, :, (2 * j + 1) * LANES : (2 * j + 2) * LANES]
            edges[f, :, j * LANES : (j + 1) * LANES] = jnp.where(on_edge, first, pltpu.roll(later, 8, axis=1))

    spans = sub_ref.shape[0]
    slot = lanes((1, LANES))
    counts = jnp.zeros((1, LANES), jnp.int32)
    for i in range(spans):
        counts = jnp.where(slot // span == i, sub_ref[i], counts)
    source = source_ref[...]
    target = lax.broadcasted_iota(jnp.int32, (devices, LANES), 0)
    to_device = jnp.where(source // LANES == target, counts, 0).astype(jnp.float32).astype(jnp.bfloat16)
    row = lax.broadcasted_iota(jnp.int32, (LANES, LANES), 0)
    to_lane = jnp.where(source % LANES == row, 1.0, 0.0).astype(jnp.bfloat16)
    message = lax.dot_general(to_device, to_lane, (((1,), (1,)), ((), ())), preferred_element_type=jnp.float32)
    outgoing[...] = message.astype(jnp.int32).reshape(groups, GROUP, LANES)

    pl.semaphore_wait(barrier, groups - 1 + GROUP - 1 + 2)

    copies = []

    def send(src, dst, send_sem, recv_sem, device):
        copy = pltpu.make_async_remote_copy(
            src_ref=src, dst_ref=dst, send_sem=send_sem, recv_sem=recv_sem, device_id=(device,), device_id_type=pl.DeviceIdType.MESH
        )
        copy.start()
        return copy

    copies.append(send(edges, halo_ref.at[1], halo_send.at[0], halo_recv.at[0], above))
    copies.append(send(edges, halo_ref.at[2], halo_send.at[1], halo_recv.at[1], below))
    own = pltpu.make_async_copy(edges, halo_ref.at[0], own_sem)
    own.start()
    firsts = []
    for step in range(1, groups):
        to = (group + step) % groups
        firsts.append(send(outgoing.at[to], arrived.at[step], one_send.at[step], one_recv.at[step], to * GROUP + member))
    for copy in firsts:
        copy.wait_recv()
    merged = outgoing[group]
    for step in range(1, groups):
        merged = merged + arrived[step]
    for q in range(GROUP):
        second[q] = jnp.broadcast_to(merged[q : q + 1, :], (ROWS, LANES))
    seconds = []
    for step in range(1, GROUP):
        to = (member + step) % GROUP
        seconds.append(send(second.at[to], arrived2.at[step], two_send.at[step], two_recv.at[step], group * GROUP + to))
    for copy in seconds:
        copy.wait_recv()
    mine = second[member]
    for step in range(1, GROUP):
        mine = mine + arrived2[step]
    count_ref[...] = mine
    for copy in firsts + seconds:
        copy.wait_send()
    for copy in copies:
        copy.wait()
    own.wait()


def exchange(dynamics, span_source, substeps, devices):
    fields, levels, nodes = dynamics.shape
    groups = devices // GROUP
    span = span_source.shape[0] // substeps.shape[0]
    return pl.pallas_call(
        functools.partial(exchange_kernel, devices, span),
        out_shape=(
            jax.ShapeDtypeStruct((3, fields, levels, nodes // 2), jnp.float32),
            jax.ShapeDtypeStruct((ROWS, LANES), jnp.int32),
        ),
        in_specs=[
            pl.BlockSpec(memory_space=pltpu.VMEM),
            pl.BlockSpec(memory_space=pltpu.VMEM),
            pl.BlockSpec(memory_space=pltpu.SMEM),
        ],
        out_specs=(pl.BlockSpec(memory_space=pl.ANY), pl.BlockSpec(memory_space=pltpu.VMEM)),
        scratch_shapes=[
            pltpu.VMEM((fields, levels, nodes // 2), jnp.float32),
            pltpu.VMEM((groups, GROUP, LANES), jnp.int32),
            pltpu.VMEM((groups, GROUP, LANES), jnp.int32),
            pltpu.VMEM((GROUP, ROWS, LANES), jnp.int32),
            pltpu.VMEM((GROUP, ROWS, LANES), jnp.int32),
            pltpu.SemaphoreType.DMA((2,)),
            pltpu.SemaphoreType.DMA((2,)),
            pltpu.SemaphoreType.DMA,
            pltpu.SemaphoreType.DMA((groups,)),
            pltpu.SemaphoreType.DMA((groups,)),
            pltpu.SemaphoreType.DMA((GROUP,)),
            pltpu.SemaphoreType.DMA((GROUP,)),
        ],
        compiler_params=pltpu.CompilerParams(collective_id=0, has_side_effects=True, vmem_limit_bytes=8 * 2**20),
        name="exchange",
    )(dynamics, span_source.reshape(1, -1), substeps)


def split_dot(values, weights):
    upper = values.astype(jnp.bfloat16)
    lower = (values - upper.astype(jnp.float32)).astype(jnp.bfloat16)
    return jnp.dot(upper, weights, preferred_element_type=jnp.float32) + jnp.dot(lower, weights, preferred_element_type=jnp.float32)


def edge_sum(me, devices, dyn_ref, halo, adj_ref, dsum_ref, force_ref):
    fields, levels, nodes = dyn_ref.shape
    rows = fields * levels
    half = nodes // 2
    elements = nodes // 16
    across = jnp.broadcast_to(adj_ref[0:1, :], (ROWS, LANES))
    facing = jnp.broadcast_to(adj_ref[1:2, :], (ROWS, LANES))
    block = (across // elements - me + devices) % devices
    part = jnp.where(block == 0, 0, jnp.where(block == 1, 2, 1))
    positions = []
    for t in range(2):
        other = ((2, 1), (11, 7), (13, 14), (4, 8))
        node = jnp.where(
            facing == 0, other[0][t], jnp.where(facing == 1, other[1][t], jnp.where(facing == 2, other[2][t], other[3][t]))
        )
        place = (across % elements) * 16 + node
        in_pair = place % 256
        lane = jnp.where(in_pair < LANES, in_pair, (in_pair - LANES + 8) % LANES)
        positions.append(part * half + (place // 256) * LANES + lane)

    lane = lanes()
    node = lane % 16
    on_edge = odious(node)
    landing = []
    for v in range(nodes // LANES):
        index = 32 * v + 4 * (lane // 16) + edge_of(node)
        picked = [jnp.take_along_axis(p, index, axis=1, mode="promise_in_bounds") for p in positions]
        landing.append(jnp.where(on_edge, jnp.where(which_of(node) == 0, picked[0], picked[1]), -1)[0:1])
    landing = jnp.concatenate(landing, axis=1)
    row = lax.broadcasted_iota(jnp.int32, (3 * half, nodes), 0)
    weights = jnp.where(row == landing, 1.0, 0.0).astype(jnp.bfloat16)

    edge_values = jnp.concatenate([halo[i].reshape(rows, half) for i in range(3)], axis=1)
    own = dyn_ref[...].reshape(rows, nodes)

    quarter = lane % 4
    base = lane - quarter

    def pick(t, edge):
        return jnp.take_along_axis(positions[t], base + edge, axis=1, mode="promise_in_bounds")

    def by_quarter(options):
        a, b, c, d = options
        return jnp.where(quarter == 0, a, jnp.where(quarter == 1, b, jnp.where(quarter == 2, c, d)))[0:1]

    one = by_quarter([pick(0, 0), pick(1, 0), pick(0, 3), pick(1, 1)])
    two = by_quarter([pick(1, 3), pick(0, 1), pick(1, 2), pick(0, 2)])
    row = lax.broadcasted_iota(jnp.int32, (3 * half, LANES), 0)
    across_weights = jnp.where((row == one) | (row == two), 0.125, 0.0).astype(jnp.bfloat16)
    row = lax.broadcasted_iota(jnp.int32, (nodes, LANES), 0)
    inner = row % 16
    column = 4 * (row // 16) + 2 * (inner // 8) + (inner % 4) // 2
    own_weights = jnp.where(
        column == lax.broadcasted_iota(jnp.int32, (nodes, LANES), 1), jnp.where(odious(inner), 0.125, 0.25), 0.0
    ).astype(jnp.bfloat16)
    force_ref[...] = split_dot(own, own_weights) + split_dot(edge_values, across_weights)

    opposite = split_dot(edge_values, weights)
    edge_lane = odious(lanes((rows, nodes)) % 16)
    dsum_ref[...] = jnp.where(edge_lane, 0.5 * (own + opposite), own).reshape(fields, levels, nodes)


def columns_kernel(
    devices, bounds, dyn_ref, halo_ref, adj_ref, count_ref, cloud_ref, dsum_ref, tend_ref, new_ref,
    state, halo, force, sums, mean_e, mean_a, term_e, term_a, bias, bias_a, old_e, old_a, in_sems, out_sems, halo_sem,
):
    depth = cloud_ref.shape[1]
    levels = dyn_ref.shape[1]
    width = cloud_ref.shape[2]
    parts = width // ROWS
    top = mean_e.shape[0] - 2 * PAD
    me = lax.axis_index("dev")

    loads = []
    halo_copy = pltpu.make_async_copy(halo_ref, halo, halo_sem)
    halo_copy.start()
    for i, (lo, hi) in enumerate(bounds):
        copy = pltpu.make_async_copy(cloud_ref.at[:, lo:hi], state.at[:, lo:hi], in_sems.at[i])
        copy.start()
        loads.append(copy)
    halo_copy.wait()
    edge_sum(me, devices, dyn_ref, halo, adj_ref, dsum_ref, force)

    height = lax.broadcasted_iota(jnp.int32, (top, LANES), 0).astype(jnp.float32)
    saturation = 0.8 * jnp.exp(-2.0 * height / depth)
    force_0 = force[0:top]
    force_1 = force[levels : levels + top]
    force_e = force_1 - 0.5 * force_0
    force_a = force_0 + force_1

    def begin(z, carry):
        total_a, total_e = [], []
        for k in range(parts):
            u0 = state[0, z, pl.ds(k, ROWS, stride=parts), :]
            u1 = state[1, z, pl.ds(k, ROWS, stride=parts), :]
            total_a.append(u0 + u1)
            total_e.append(u1 - 0.5 * u0)
        for k in range(parts):
            state[0, z, k * ROWS : (k + 1) * ROWS, :] = total_a[k]
            state[1, z, k * ROWS : (k + 1) * ROWS, :] = total_e[k]
        at = pl.multiple_of(z * ROWS, ROWS)
        sums[0, pl.ds(at, ROWS), :] = total_of(total_a)
        sums[1, pl.ds(at, ROWS), :] = total_of(total_e)
        return carry

    for (lo, hi), copy in zip(bounds, loads):
        copy.wait()
        lax.fori_loop(lo, hi, begin, 0, unroll=2)

    def mean_of(which):
        blocks = []
        for block in range(top // ROWS):
            start = block * ROWS * ROWS
            blocks.append(total_of([sums[which, pl.ds(start + j, ROWS, stride=ROWS), :] for j in range(ROWS)]))
        return jnp.concatenate(blocks, axis=0) * (1.0 / width)

    def spread(ref, values):
        ref[PAD : PAD + top, :] = values
        ref[PAD - 1 : PAD, :] = values[0:1]
        ref[PAD + depth : PAD + depth + 1, :] = values[depth - 1 : depth]
        return 8.0 * values + ref[PAD - 1 : PAD - 1 + top, :] + ref[PAD + 1 : PAD + 1 + top, :]

    def sweep(which, active, with_bias, with_sum, limit, unroll):
        def load(z):
            return [state[which, z, k * ROWS : (k + 1) * ROWS, :] for k in range(parts)]

        def level(z, before, here):
            after = load(jnp.minimum(z + 1, depth - 1) if not isinstance(z, int) else min(z + 1, depth - 1))
            left = pltpu.roll(here[parts - 1], 1, axis=0)
            right = pltpu.roll(here[0], ROWS - 1, axis=0)
            if with_bias is not None:
                shift = jnp.broadcast_to(with_bias[pl.ds(z, 1), :], (ROWS, LANES))
            stepped = []
            for k in range(parts):
                beside = (here[k - 1] if k > 0 else left) + (here[k + 1] if k < parts - 1 else right)
                value = 6.0 * here[k] + (beside + (before[k] + after[k]))
                if with_bias is not None:
                    value = value + shift
                if limit:
                    value = jnp.minimum(value, 0.25 * value)
                if active is not None:
                    value = jnp.where(active, value, here[k])
                stepped.append(value)
                state[which, z, k * ROWS : (k + 1) * ROWS, :] = value
            if with_sum:
                at = z * ROWS if isinstance(z, int) else pl.multiple_of(z * ROWS, ROWS)
                sums[which, pl.ds(at, ROWS), :] = total_of(stepped)
            return here, after

        before = here = load(0)
        if unroll >= depth:
            for z in range(depth):
                before, here = level(z, before, here)
            return
        whole = depth // unroll

        def several(i, carry):
            before, here = carry
            for j in range(unroll):
                before, here = level(i * unroll + j, before, here)
            return before, here

        before, here = lax.fori_loop(0, whole, several, (before, here))
        for z in range(whole * unroll, depth):
            before, here = level(z, before, here)

    counts = count_ref[...]
    least = jnp.min(counts)
    most = jnp.max(counts)

    start_a = mean_of(0)
    start_e = mean_of(1)
    old_a[...] = start_a
    old_e[...] = start_e
    term_e[...] = spread(mean_e, saturation + 0.3 * (force_e - saturation)) - 10.0 * saturation
    bias[...] = spread(mean_e, 0.3 * (force_e - start_e)) - 10.0 * saturation
    bias_a[...] = -spread(mean_a, start_a)
    term_a[...] = 0.3 * force_a
    mean_a_now = 0.1 * spread(mean_a, 0.7 * start_a + 0.3 * force_a)
    mean_a[PAD : PAD + top, :] = mean_a_now
    sweep(0, None, bias_a, False, False, UNROLL)
    sweep(1, None, bias, True, True, UNROLL)

    def profiles(scale, active):
        bias[...] = scale * term_e[...] - 0.3 * spread(mean_e, mean_of(1))
        now = mean_a[PAD : PAD + top, :]
        later = 0.1 * spread(mean_a, 0.7 * now + term_a[...])
        if active is not None:
            later = jnp.where(active, later, now)
        mean_a[PAD : PAD + top, :] = later

    def plain(step, scale):
        profiles(scale, None)
        sweep(0, None, None, False, False, UNROLL)
        sweep(1, None, bias, True, True, UNROLL)
        return scale * 10.0

    def masked(step, scale):
        active = counts > step
        profiles(scale, jnp.broadcast_to(active[0:1], (top, LANES)))
        sweep(0, active, None, False, False, UNROLL)
        sweep(1, active, bias, True, True, UNROLL)
        return scale * 10.0

    scale = lax.fori_loop(1, least, plain, jnp.float32(10.0))
    lax.fori_loop(least, most, masked, scale)

    shrink = jnp.ones((ROWS, LANES), jnp.float32)
    for step in range(12):
        shrink = jnp.where(counts > step, shrink * 0.1, shrink)
    across = shrink[0:1]
    new_a = mean_a[PAD : PAD + top, :]
    new_e = mean_of(1) * across + saturation
    tend_0 = (2.0 / 3.0) * ((new_a - new_e) - (old_a[...] - old_e[...]))
    tend_1 = (new_a - old_a[...]) - tend_0
    tend_ref[0] = tend_0[0:depth]
    tend_ref[1] = tend_1[0:depth]
    bias[...] = (2.0 / 3.0) * (new_a - saturation)
    bias_a[...] = new_a
    shrink_0 = (2.0 / 3.0) * shrink

    def finish(z, carry):
        add_0 = jnp.broadcast_to(bias[pl.ds(z, 1), :], (ROWS, LANES))
        add_a = jnp.broadcast_to(bias_a[pl.ds(z, 1), :], (ROWS, LANES))
        new_0, new_1 = [], []
        for k in range(parts):
            a = state[0, z, k * ROWS : (k + 1) * ROWS, :]
            e = state[1, z, k * ROWS : (k + 1) * ROWS, :]
            u0 = (a - e) * shrink_0 + add_0
            new_0.append(u0)
            new_1.append((a * shrink + add_a) - u0)
        for k in range(parts):
            state[0, z, pl.ds(k, ROWS, stride=parts), :] = new_0[k]
            state[1, z, pl.ds(k, ROWS, stride=parts), :] = new_1[k]
        return carry

    stores = []
    for i, (lo, hi) in enumerate(bounds):
        lax.fori_loop(lo, hi, finish, 0, unroll=2)
        copy = pltpu.make_async_copy(state.at[:, lo:hi], new_ref.at[:, lo:hi], out_sems.at[i])
        copy.start()
        stores.append(copy)
    for copy in stores:
        copy.wait()


def columns(dynamics, halo, adjacency, counts, cloud_state, devices):
    fields, levels, nodes = dynamics.shape
    depth, width = cloud_state.shape[1], cloud_state.shape[2]
    top = -(-depth // ROWS) * ROWS
    cuts = [round(i * depth / CHUNKS) for i in range(CHUNKS + 1)]
    bounds = tuple(zip(cuts[:-1], cuts[1:]))
    vmem = pl.BlockSpec(memory_space=pltpu.VMEM)
    anywhere = pl.BlockSpec(memory_space=pl.ANY)
    profile = pltpu.VMEM((top, LANES), jnp.float32)
    padded = pltpu.VMEM((top + 2 * PAD, LANES), jnp.float32)
    return pl.pallas_call(
        functools.partial(columns_kernel, devices, bounds),
        out_shape=(
            jax.ShapeDtypeStruct(dynamics.shape, jnp.float32),
            jax.ShapeDtypeStruct((fields, depth, LANES), jnp.float32),
            jax.ShapeDtypeStruct(cloud_state.shape, jnp.float32),
        ),
        in_specs=[vmem, anywhere, vmem, vmem, anywhere],
        out_specs=(vmem, vmem, anywhere),
        scratch_shapes=[
            pltpu.VMEM(cloud_state.shape, jnp.float32),
            pltpu.VMEM(halo.shape, jnp.float32),
            pltpu.VMEM((fields * levels, LANES), jnp.float32),
            pltpu.VMEM((2, top * ROWS, LANES), jnp.float32),
            padded, padded, profile, profile, profile, profile, profile, profile,
            pltpu.SemaphoreType.DMA((CHUNKS,)),
            pltpu.SemaphoreType.DMA((CHUNKS,)),
            pltpu.SemaphoreType.DMA,
        ],
        compiler_params=pltpu.CompilerParams(vmem_limit_bytes=40 * 2**20),
        name="columns",
    )(dynamics, halo, adjacency, counts, cloud_state)


def on_device(dynamics, adjacency, cloud_state, span_source, substeps):
    devices = lax.axis_size("dev")
    halo, counts = exchange(dynamics, span_source, substeps, devices)
    return columns(dynamics, halo, adjacency, counts, cloud_state, devices)


def solution(mesh):
    in_specs = (
        P(None, None, "dev"),
        P(None, "dev"),
        P(None, None, None, "dev"),
        P("dev"),
        P("dev"),
    )
    out_specs = (P(None, None, "dev"), P(None, None, "dev"), P(None, None, None, "dev"))
    return jax.shard_map(on_device, mesh=mesh, in_specs=in_specs, out_specs=out_specs, check_vma=False)
```

```python
import functools

import jax
import jax.numpy as jnp
from jax import lax
from jax.experimental import pallas as pl
from jax.experimental.pallas import tpu as pltpu
from jax.sharding import PartitionSpec as P

LANES = 128
ROWS = 8
GROUP = 8
PAD = 8
CHUNKS = 6
UNROLL = 58
SHORT = 2


def odious(node):
    return ((node ^ (node >> 1) ^ (node >> 2) ^ (node >> 3)) & 1) == 1


def edge_of(node):
    return jnp.where(
        (node == 1) | (node == 2), 0, jnp.where((node == 7) | (node == 11), 1, jnp.where((node == 14) | (node == 13), 2, 3))
    )


def which_of(node):
    return jnp.where((node == 2) | (node == 11) | (node == 13) | (node == 4), 1, 0)


def lanes(shape=(ROWS, LANES)):
    return lax.broadcasted_iota(jnp.int32, shape, len(shape) - 1)


def total_of(parts):
    while len(parts) > 1:
        parts = [a + b for a, b in zip(parts[::2], parts[1::2])] + ([parts[-1]] if len(parts) % 2 else [])
    return parts[0]


def mean_of(sums, width):
    blocks = []
    for start in range(0, sums.shape[0], ROWS * ROWS):
        blocks.append(total_of([sums[pl.ds(start + j, ROWS, stride=ROWS), :] for j in range(ROWS)]))
    return jnp.concatenate(blocks, axis=0) * (1.0 / width)


def spread(ref, values, depth):
    top = values.shape[0]
    ref[PAD : PAD + top, :] = values
    ref[PAD - 1 : PAD, :] = values[0:1]
    ref[PAD + depth : PAD + depth + 1, :] = values[depth - 1 : depth]
    return 8.0 * values + ref[PAD - 1 : PAD - 1 + top, :] + ref[PAD + 1 : PAD + 1 + top, :]


def saturation_of(top, depth):
    height = lax.broadcasted_iota(jnp.int32, (top, LANES), 0).astype(jnp.float32)
    return 0.8 * jnp.exp(-2.0 * height / depth)


def sweep(src, dst, which, active, bias, sums, limit, unroll):
    depth = src.shape[1]
    parts = src.shape[2] // ROWS

    def load(z):
        return [src[which, z, k * ROWS : (k + 1) * ROWS, :] for k in range(parts)]

    def level(z, before, here):
        known = isinstance(z, int)
        after = load(min(z + 1, depth - 1) if known else jnp.minimum(z + 1, depth - 1))
        left = pltpu.roll(here[parts - 1], 1, axis=0)
        right = pltpu.roll(here[0], ROWS - 1, axis=0)
        if bias is not None:
            shift = jnp.broadcast_to(bias[pl.ds(z, 1), :], (ROWS, LANES))
        stepped = []
        for k in range(parts):
            beside = (here[k - 1] if k > 0 else left) + (here[k + 1] if k < parts - 1 else right)
            value = 6.0 * here[k] + (beside + (before[k] + after[k]))
            if bias is not None:
                value = value + shift
            if limit:
                value = jnp.minimum(value, 0.25 * value)
            if active is not None:
                value = jnp.where(active, value, here[k])
            stepped.append(value)
            dst[which, z, k * ROWS : (k + 1) * ROWS, :] = value
        if sums is not None:
            at = z * ROWS if known else pl.multiple_of(z * ROWS, ROWS)
            sums[pl.ds(at, ROWS), :] = total_of(stepped)
        return here, after

    before = here = load(0)
    if unroll >= depth:
        for z in range(depth):
            before, here = level(z, before, here)
        return
    whole = depth // unroll

    def several(i, carry):
        before, here = carry
        for j in range(unroll):
            before, here = level(i * unroll + j, before, here)
        return before, here

    before, here = lax.fori_loop(0, whole, several, (before, here))
    for z in range(whole * unroll, depth):
        before, here = level(z, before, here)


def split_dot(values, weights):
    upper = values.astype(jnp.bfloat16)
    lower = (values - upper.astype(jnp.float32)).astype(jnp.bfloat16)
    return jnp.dot(upper, weights, preferred_element_type=jnp.float32) + jnp.dot(lower, weights, preferred_element_type=jnp.float32)


def partner_places(me, devices, adjacency, elements, half):
    across = jnp.broadcast_to(adjacency[0:1, :], (ROWS, LANES))
    facing = jnp.broadcast_to(adjacency[1:2, :], (ROWS, LANES))
    block = (across // elements - me + devices) % devices
    part = jnp.where(block == 0, 0, jnp.where(block == 1, 2, 1))
    places = []
    for t in range(2):
        other = ((2, 1), (11, 7), (13, 14), (4, 8))
        node = jnp.where(
            facing == 0, other[0][t], jnp.where(facing == 1, other[1][t], jnp.where(facing == 2, other[2][t], other[3][t]))
        )
        place = (across % elements) * 16 + node
        in_pair = place % 256
        lane = jnp.where(in_pair < LANES, in_pair, (in_pair - LANES + 8) % LANES)
        places.append(part * half + (place // 256) * LANES + lane)
    return places


def node_weights(places, nodes, half):
    lane = lanes()
    node = lane % 16
    landing = []
    for v in range(nodes // LANES):
        index = 32 * v + 4 * (lane // 16) + edge_of(node)
        picked = [jnp.take_along_axis(p, index, axis=1, mode="promise_in_bounds") for p in places]
        landing.append(jnp.where(odious(node), jnp.where(which_of(node) == 0, picked[0], picked[1]), -1)[0:1])
    landing = jnp.concatenate(landing, axis=1)
    row = lax.broadcasted_iota(jnp.int32, (3 * half, nodes), 0)
    return jnp.where(row == landing, 1.0, 0.0).astype(jnp.bfloat16)


def column_weights(places, nodes, half):
    lane = lanes()
    quarter = lane % 4

    def pick(t, edge):
        return jnp.take_along_axis(places[t], lane - quarter + edge, axis=1, mode="promise_in_bounds")

    def by_quarter(a, b, c, d):
        return jnp.where(quarter == 0, a, jnp.where(quarter == 1, b, jnp.where(quarter == 2, c, d)))[0:1]

    one = by_quarter(pick(0, 0), pick(1, 0), pick(0, 3), pick(1, 1))
    two = by_quarter(pick(1, 3), pick(0, 1), pick(1, 2), pick(0, 2))
    row = lax.broadcasted_iota(jnp.int32, (3 * half, LANES), 0)
    across = jnp.where((row == one) | (row == two), 0.125, 0.0).astype(jnp.bfloat16)
    row = lax.broadcasted_iota(jnp.int32, (nodes, LANES), 0)
    inner = row % 16
    column = 4 * (row // 16) + 2 * (inner // 8) + (inner % 4) // 2
    here = column == lax.broadcasted_iota(jnp.int32, (nodes, LANES), 1)
    own = jnp.where(here, jnp.where(odious(inner), 0.125, 0.25), 0.0).astype(jnp.bfloat16)
    return own, across


def first_kernel(
    devices, span, bounds, dyn_hbm, adj_hbm, cloud_hbm, source_hbm, sub_hbm,
    state, dsum_ref, count_ref, sums_e, profiles,
    dyn, adj, source_ref, sub_ref, edges, halo, outgoing, arrived, second, arrived2, sums_a, padded, bias, bias_a,
    local_sems, in_sems, halo_send, halo_recv, one_send, one_recv, two_send, two_recv,
):
    me = lax.axis_index("dev")
    groups = devices // GROUP
    group = me // GROUP
    member = me % GROUP
    above = (me + 1) % devices
    below = (me + devices - 1) % devices
    fields, levels, nodes = dyn.shape
    half = nodes // 2
    depth, width = state.shape[1], state.shape[2]
    parts = width // ROWS
    top = profiles.shape[1]

    barrier = pltpu.get_barrier_semaphore()

    def greet(device):
        pl.semaphore_signal(barrier, inc=1, device_id=(device,), device_id_type=pl.DeviceIdType.MESH)

    for step in range(1, groups):
        greet(((group + step) % groups) * GROUP + member)
    for step in range(1, GROUP):
        greet(group * GROUP + (member + step) % GROUP)
    greet(above)
    greet(below)

    local = []
    for i, (src, dst) in enumerate(((dyn_hbm, dyn), (source_hbm, source_ref), (sub_hbm, sub_ref), (adj_hbm, adj))):
        local.append(pltpu.make_async_copy(src, dst, local_sems.at[i]))
        local[-1].start()
    loads = []
    for i, (lo, hi) in enumerate(bounds):
        loads.append(pltpu.make_async_copy(cloud_hbm.at[:, lo:hi], state.at[:, lo:hi], in_sems.at[i]))
        loads[-1].start()

    local[0].wait()
    on_edge = odious(lanes((levels, LANES)) % 16)
    for f in range(fields):
        for j in range(2):
            first = dyn[f, :, 2 * j * LANES : (2 * j + 1) * LANES]
            later = dyn[f, :, (2 * j + 1) * LANES : (2 * j + 2) * LANES]
            edges[f, :, j * LANES : (j + 1) * LANES] = jnp.where(on_edge, first, pltpu.roll(later, 8, axis=1))

    local[1].wait()
    local[2].wait()
    slot = lanes((1, LANES))
    counts = jnp.zeros((1, LANES), jnp.int32)
    for i in range(LANES // span):
        counts = jnp.where(slot // span == i, sub_ref[0:1, i : i + 1], counts)
    source = source_ref[...]
    target = lax.broadcasted_iota(jnp.int32, (devices, LANES), 0)
    to_device = jnp.where(source // LANES == target, counts, 0).astype(jnp.float32).astype(jnp.bfloat16)
    row = lax.broadcasted_iota(jnp.int32, (LANES, LANES), 0)
    to_lane = jnp.where(source % LANES == row, 1.0, 0.0).astype(jnp.bfloat16)
    message = lax.dot_general(to_device, to_lane, (((1,), (1,)), ((), ())), preferred_element_type=jnp.float32)
    outgoing[...] = message.astype(jnp.int32).reshape(groups, GROUP, LANES)

    pl.semaphore_wait(barrier, groups - 1 + GROUP - 1 + 2)

    def send(src, dst, send_sem, recv_sem, device):
        copy = pltpu.make_async_remote_copy(
            src_ref=src, dst_ref=dst, send_sem=send_sem, recv_sem=recv_sem, device_id=(device,), device_id_type=pl.DeviceIdType.MESH
        )
        copy.start()
        return copy

    firsts = []
    for step in range(1, groups):
        to = (group + step) % groups
        firsts.append(send(outgoing.at[to], arrived.at[step], one_send.at[step], one_recv.at[step], to * GROUP + member))
    up = send(edges, halo.at[0], halo_send.at[0], halo_recv.at[0], above)
    down = send(edges, halo.at[1], halo_send.at[1], halo_recv.at[1], below)

    def begin(z, carry):
        all_a, all_e = [], []
        for k in range(parts):
            u0 = state[0, z, pl.ds(k, ROWS, stride=parts), :]
            u1 = state[1, z, pl.ds(k, ROWS, stride=parts), :]
            all_a.append(u0 + u1)
            all_e.append(u1 - 0.5 * u0)
        for k in range(parts):
            state[0, z, k * ROWS : (k + 1) * ROWS, :] = all_a[k]
            state[1, z, k * ROWS : (k + 1) * ROWS, :] = all_e[k]
        at = pl.multiple_of(z * ROWS, ROWS)
        sums_a[pl.ds(at, ROWS), :] = total_of(all_a)
        sums_e[pl.ds(at, ROWS), :] = total_of(all_e)
        return carry

    for (lo, hi), copy in zip(bounds, loads):
        copy.wait()
        lax.fori_loop(lo, hi, begin, 0)

    local[3].wait()
    places = partner_places(me, devices, adj, nodes // 16, half)
    own_weights, across_weights = column_weights(places, nodes, half)
    own = dyn[...].reshape(fields * levels, nodes)
    force_own = split_dot(own, own_weights)
    start_a = mean_of(sums_a, width)
    start_e = mean_of(sums_e, width)
    saturation = saturation_of(top, depth)
    bias_a[...] = -spread(padded, start_a, depth)

    for copy in firsts:
        copy.wait_recv()
    merged = outgoing[group]
    for step in range(1, groups):
        merged = merged + arrived[step]
    for q in range(GROUP):
        second[q] = jnp.broadcast_to(merged[q : q + 1, :], (ROWS, LANES))
    seconds = []
    for step in range(1, GROUP):
        to = (member + step) % GROUP
        seconds.append(send(second.at[to], arrived2.at[step], two_send.at[step], two_recv.at[step], group * GROUP + to))

    sweep(state, state, 0, None, bias_a, None, False, SHORT)
    weights = node_weights(places, nodes, half)

    up.wait()
    down.wait()
    values = [edges[...].reshape(fields * levels, half)] + [halo[i].reshape(fields * levels, half) for i in range(2)]
    values = jnp.concatenate(values, axis=1)
    force = force_own + split_dot(values, across_weights)
    force_0 = force[0:top]
    force_1 = force[levels : levels + top]
    force_e = force_1 - 0.5 * force_0
    force_a = force_0 + force_1
    bias[...] = spread(padded, 0.3 * (force_e - start_e), depth) - 10.0 * saturation
    sweep(state, state, 1, None, bias, sums_e, True, SHORT)

    profiles[0] = start_a
    profiles[1] = start_e
    profiles[2] = 0.3 * force_a
    profiles[3] = spread(padded, saturation + 0.3 * (force_e - saturation), depth) - 10.0 * saturation
    profiles[4] = 0.1 * spread(padded, 0.7 * start_a + 0.3 * force_a, depth)

    opposite = split_dot(values, weights)
    edge_lane = odious(lanes((fields * levels, nodes)) % 16)
    dsum_ref[...] = jnp.where(edge_lane, 0.5 * (own + opposite), own).reshape(fields, levels, nodes)

    for copy in seconds:
        copy.wait_recv()
    mine = second[member]
    for step in range(1, GROUP):
        mine = mine + arrived2[step]
    count_ref[...] = mine
    for copy in firsts + seconds:
        copy.wait_send()


def cut(depth):
    cuts = [round(i * depth / CHUNKS) for i in range(CHUNKS + 1)]
    return tuple(zip(cuts[:-1], cuts[1:]))


def first(dynamics, adjacency, cloud_state, span_source, substeps, devices):
    fields, levels, nodes = dynamics.shape
    depth, width = cloud_state.shape[1], cloud_state.shape[2]
    top = -(-depth // ROWS) * ROWS
    groups = devices // GROUP
    span = span_source.shape[0] // substeps.shape[0]
    vmem = pl.BlockSpec(memory_space=pltpu.VMEM)
    hbm = pl.BlockSpec(memory_space=pltpu.HBM)
    profile = pltpu.VMEM((top, LANES), jnp.float32)
    return pl.pallas_call(
        functools.partial(first_kernel, devices, span, cut(depth)),
        out_shape=(
            jax.ShapeDtypeStruct(cloud_state.shape, jnp.float32),
            jax.ShapeDtypeStruct(dynamics.shape, jnp.float32),
            jax.ShapeDtypeStruct((ROWS, LANES), jnp.int32),
            jax.ShapeDtypeStruct((top * ROWS, LANES), jnp.float32),
            jax.ShapeDtypeStruct((5, top, LANES), jnp.float32),
        ),
        in_specs=[hbm] * 5,
        out_specs=(vmem,) * 5,
        scratch_shapes=[
            pltpu.VMEM(dynamics.shape, jnp.float32),
            pltpu.VMEM(adjacency.shape, jnp.int32),
            pltpu.VMEM((1, LANES), jnp.int32),
            pltpu.VMEM((1, substeps.shape[0]), jnp.int32),
            pltpu.VMEM((fields, levels, nodes // 2), jnp.float32),
            pltpu.VMEM((2, fields, levels, nodes // 2), jnp.float32),
            pltpu.VMEM((groups, GROUP, LANES), jnp.int32),
            pltpu.VMEM((groups, GROUP, LANES), jnp.int32),
            pltpu.VMEM((GROUP, ROWS, LANES), jnp.int32),
            pltpu.VMEM((GROUP, ROWS, LANES), jnp.int32),
            pltpu.VMEM((top * ROWS, LANES), jnp.float32),
            pltpu.VMEM((top + 2 * PAD, LANES), jnp.float32),
            profile,
            profile,
            pltpu.SemaphoreType.DMA((4,)),
            pltpu.SemaphoreType.DMA((CHUNKS,)),
            pltpu.SemaphoreType.DMA((2,)),
            pltpu.SemaphoreType.DMA((2,)),
            pltpu.SemaphoreType.DMA((groups,)),
            pltpu.SemaphoreType.DMA((groups,)),
            pltpu.SemaphoreType.DMA((GROUP,)),
            pltpu.SemaphoreType.DMA((GROUP,)),
        ],
        compiler_params=pltpu.CompilerParams(collective_id=0, has_side_effects=True, vmem_limit_bytes=20 * 2**20),
        name="first",
    )(*[
        pltpu.with_memory_space_constraint(x, pltpu.HBM)
        for x in (dynamics, adjacency, cloud_state, span_source.reshape(1, -1), substeps.reshape(1, -1))
    ])


def rest_kernel(
    bounds, given, dsum_ref, count_ref, given_sums, profiles, dsum_out, tend_ref, new_ref,
    state, sums, mean_e, mean_a, bias, out_sems, dsum_sem,
):
    depth, width = state.shape[1], state.shape[2]
    parts = width // ROWS
    top = bias.shape[0]
    dsum_copy = pltpu.make_async_copy(dsum_ref, dsum_out, dsum_sem)
    dsum_copy.start()

    counts = count_ref[...]
    least = jnp.min(counts)
    most = jnp.max(counts)
    saturation = saturation_of(top, depth)

    def advance(scale, source_sums, active):
        bias[...] = scale * profiles[3] - 0.3 * spread(mean_e, mean_of(source_sums, width), depth)
        now = mean_a[PAD : PAD + top, :]
        later = 0.1 * spread(mean_a, 0.7 * now + profiles[2], depth)
        if active is not None:
            later = jnp.where(jnp.broadcast_to(active[0:1], (top, LANES)), later, now)
        mean_a[PAD : PAD + top, :] = later

    def plain(step, scale):
        advance(scale, sums, None)
        sweep(state, state, 0, None, None, None, False, UNROLL)
        sweep(state, state, 1, None, bias, sums, True, UNROLL)
        return scale * 10.0

    def masked(step, scale):
        active = counts > step
        advance(scale, sums, active)
        sweep(state, state, 0, active, None, None, False, UNROLL)
        sweep(state, state, 1, active, bias, sums, True, UNROLL)
        return scale * 10.0

    mean_a[PAD : PAD + top, :] = profiles[4]
    active = counts > 1
    advance(10.0, given_sums, active)
    sweep(given, state, 0, active, None, None, False, UNROLL)
    sweep(given, state, 1, active, bias, sums, True, UNROLL)
    middle = jnp.maximum(least, 2)
    scale = lax.fori_loop(2, middle, plain, jnp.float32(100.0))
    lax.fori_loop(middle, most, masked, scale)

    shrink = jnp.ones((ROWS, LANES), jnp.float32)
    for step in range(12):
        shrink = jnp.where(counts > step, shrink * 0.1, shrink)
    new_a = mean_a[PAD : PAD + top, :]
    new_e = mean_of(sums, width) * shrink[0:1] + saturation
    old_a = profiles[0]
    old_e = profiles[1]
    tend_0 = (2.0 / 3.0) * ((new_a - new_e) - (old_a - old_e))
    tend_1 = (new_a - old_a) - tend_0
    tend_ref[:, 0, :] = tend_0[0:depth]
    tend_ref[:, 1, :] = tend_1[0:depth]
    bias[...] = (2.0 / 3.0) * (new_a - saturation)
    shrink_0 = (2.0 / 3.0) * shrink

    def finish(z, carry):
        add_0 = jnp.broadcast_to(bias[pl.ds(z, 1), :], (ROWS, LANES))
        add_a = jnp.broadcast_to(mean_a[pl.ds(PAD + z, 1), :], (ROWS, LANES))
        new_0, new_1 = [], []
        for k in range(parts):
            a = state[0, z, k * ROWS : (k + 1) * ROWS, :]
            e = state[1, z, k * ROWS : (k + 1) * ROWS, :]
            u0 = (a - e) * shrink_0 + add_0
            new_0.append(u0)
            new_1.append((a * shrink + add_a) - u0)
        for k in range(parts):
            state[0, z, pl.ds(k, ROWS, stride=parts), :] = new_0[k]
            state[1, z, pl.ds(k, ROWS, stride=parts), :] = new_1[k]
        return carry

    stores = []
    for i, (lo, hi) in enumerate(bounds):
        lax.fori_loop(lo, hi, finish, 0, unroll=2)
        copy = pltpu.make_async_copy(state.at[:, lo:hi], new_ref.at[:, lo:hi], out_sems.at[i])
        copy.start()
        stores.append(copy)
    for copy in stores:
        copy.wait()
    dsum_copy.wait()


def rest(state, dsum, counts, sums, profiles):
    fields, depth, width, _ = state.shape
    top = profiles.shape[1]
    vmem = pl.BlockSpec(memory_space=pltpu.VMEM)
    hbm = pl.BlockSpec(memory_space=pltpu.HBM)
    padded = pltpu.VMEM((top + 2 * PAD, LANES), jnp.float32)
    return pl.pallas_call(
        functools.partial(rest_kernel, cut(depth)),
        out_shape=(
            jax.ShapeDtypeStruct(dsum.shape, jnp.float32),
            jax.ShapeDtypeStruct((depth, fields, LANES), jnp.float32),
            jax.ShapeDtypeStruct(state.shape, jnp.float32),
        ),
        in_specs=[vmem] * 5,
        out_specs=(hbm, vmem, hbm),
        scratch_shapes=[
            pltpu.VMEM(state.shape, jnp.float32),
            pltpu.VMEM(sums.shape, jnp.float32),
            padded,
            padded,
            pltpu.VMEM((top, LANES), jnp.float32),
            pltpu.SemaphoreType.DMA((CHUNKS,)),
            pltpu.SemaphoreType.DMA,
        ],
        compiler_params=pltpu.CompilerParams(vmem_limit_bytes=20 * 2**20),
        name="rest",
    )(state, dsum, counts, sums, profiles)


def on_device(dynamics, adjacency, cloud_state, span_source, substeps):
    devices = lax.axis_size("dev")
    carried = first(dynamics, adjacency, cloud_state, span_source, substeps, devices)
    dynamics_summed, tendency, cloud_new = rest(*carried)
    return dynamics_summed, jnp.transpose(tendency, (1, 0, 2)), cloud_new


def solution(mesh):
    in_specs = (
        P(None, None, "dev"),
        P(None, "dev"),
        P(None, None, None, "dev"),
        P("dev"),
        P("dev"),
    )
    out_specs = (P(None, None, "dev"), P(None, None, "dev"), P(None, None, None, "dev"))
    return jax.shard_map(on_device, mesh=mesh, in_specs=in_specs, out_specs=out_specs, check_vma=False)
```

```python
import functools

import jax
import jax.numpy as jnp
from jax import lax
from jax.experimental import pallas as pl
from jax.experimental.pallas import tpu as pltpu
from jax.sharding import PartitionSpec as P

LANES = 128
ROWS = 8
PAD = 8
CHUNKS = 6
UNROLL = 58
AHEAD = 6


def odious(node):
    return ((node ^ (node >> 1) ^ (node >> 2) ^ (node >> 3)) & 1) == 1


def edge_of(node):
    return jnp.where(
        (node == 1) | (node == 2), 0, jnp.where((node == 7) | (node == 11), 1, jnp.where((node == 14) | (node == 13), 2, 3))
    )


def which_of(node):
    return jnp.where((node == 2) | (node == 11) | (node == 13) | (node == 4), 1, 0)


def lanes(shape=(ROWS, LANES)):
    return lax.broadcasted_iota(jnp.int32, shape, len(shape) - 1)


def total_of(parts):
    while len(parts) > 1:
        parts = [a + b for a, b in zip(parts[::2], parts[1::2])] + ([parts[-1]] if len(parts) % 2 else [])
    return parts[0]


def mean_of(sums, width):
    blocks = []
    for start in range(0, sums.shape[0], ROWS * ROWS):
        blocks.append(total_of([sums[pl.ds(start + j, ROWS, stride=ROWS), :] for j in range(ROWS)]))
    return jnp.concatenate(blocks, axis=0) * (1.0 / width)


def spread(ref, values, depth):
    top = values.shape[0]
    ref[PAD : PAD + top, :] = values
    ref[PAD - 1 : PAD, :] = values[0:1]
    ref[PAD + depth : PAD + depth + 1, :] = values[depth - 1 : depth]
    return 8.0 * values + ref[PAD - 1 : PAD - 1 + top, :] + ref[PAD + 1 : PAD + 1 + top, :]


def saturation_of(top, depth):
    height = lax.broadcasted_iota(jnp.int32, (top, LANES), 0).astype(jnp.float32)
    return 0.8 * jnp.exp(-2.0 * height / depth)


def sweep(src, dst, which, active, bias, sums, limit, unroll):
    depth = src.shape[1]
    parts = src.shape[2] // ROWS

    def load(z):
        return [src[which, z, k * ROWS : (k + 1) * ROWS, :] for k in range(parts)]

    def level(z, before, here):
        known = isinstance(z, int)
        after = load(min(z + 1, depth - 1) if known else jnp.minimum(z + 1, depth - 1))
        left = pltpu.roll(here[parts - 1], 1, axis=0)
        right = pltpu.roll(here[0], ROWS - 1, axis=0)
        if bias is not None:
            shift = jnp.broadcast_to(bias[pl.ds(z, 1), :], (ROWS, LANES))
        stepped = []
        for k in range(parts):
            beside = (here[k - 1] if k > 0 else left) + (here[k + 1] if k < parts - 1 else right)
            value = 6.0 * here[k] + (beside + (before[k] + after[k]))
            if bias is not None:
                value = value + shift
            if limit:
                value = jnp.minimum(value, 0.25 * value)
            if active is not None:
                value = jnp.where(active, value, here[k])
            stepped.append(value)
            dst[which, z, k * ROWS : (k + 1) * ROWS, :] = value
        if sums is not None:
            at = z * ROWS if known else pl.multiple_of(z * ROWS, ROWS)
            sums[pl.ds(at, ROWS), :] = total_of(stepped)
        return here, after

    before = here = load(0)
    if unroll >= depth:
        for z in range(depth):
            before, here = level(z, before, here)
        return
    whole = depth // unroll

    def several(i, carry):
        before, here = carry
        for j in range(unroll):
            before, here = level(i * unroll + j, before, here)
        return before, here

    before, here = lax.fori_loop(0, whole, several, (before, here))
    for z in range(whole * unroll, depth):
        before, here = level(z, before, here)


def split_dot(values, weights):
    upper = values.astype(jnp.bfloat16)
    lower = (values - upper.astype(jnp.float32)).astype(jnp.bfloat16)
    return jnp.dot(upper, weights, preferred_element_type=jnp.float32) + jnp.dot(lower, weights, preferred_element_type=jnp.float32)


def partner_places(me, devices, adjacency, elements, half):
    across = jnp.broadcast_to(adjacency[0:1, :], (ROWS, LANES))
    facing = jnp.broadcast_to(adjacency[1:2, :], (ROWS, LANES))
    block = (across // elements - me + devices) % devices
    part = jnp.where(block == 0, 0, jnp.where(block == 1, 2, 1))
    places = []
    for t in range(2):
        other = ((2, 1), (11, 7), (13, 14), (4, 8))
        node = jnp.where(
            facing == 0, other[0][t], jnp.where(facing == 1, other[1][t], jnp.where(facing == 2, other[2][t], other[3][t]))
        )
        place = (across % elements) * 16 + node
        in_pair = place % 256
        lane = jnp.where(in_pair < LANES, in_pair, (in_pair - LANES + 8) % LANES)
        places.append(part * half + (place // 256) * LANES + lane)
    return places


def packed_nodes(index):
    lane = index % LANES
    direct = odious(lane % 16)
    moved = (lane + LANES - 8) % LANES
    element = jnp.where(direct, lane // 16, 8 + moved // 16) + (index // LANES) * 16
    return element, jnp.where(direct, lane % 16, moved % 16)


def edge_weights(places, half):
    landing = []
    for v in range(half // LANES):
        element, node = packed_nodes(lanes() + v * LANES)
        index = 4 * element + edge_of(node)
        picked = [jnp.take_along_axis(p, index, axis=1, mode="promise_in_bounds") for p in places]
        landing.append(jnp.where(which_of(node) == 0, picked[0], picked[1])[0:1])
    landing = jnp.concatenate(landing, axis=1)
    row = lax.broadcasted_iota(jnp.int32, (3 * half, half), 0)
    return jnp.where(row == landing, 1.0, 0.0).astype(jnp.bfloat16)


def quarter_weights(element, node, keep):
    column = 4 * element + 2 * (node // 8) + (node % 4) // 2
    here = (column == lax.broadcasted_iota(jnp.int32, column.shape, 1)) & keep
    return jnp.where(here, 0.25, 0.0).astype(jnp.bfloat16)


def first_kernel(
    devices, span, bounds, dyn_hbm, adj_hbm, cloud_hbm, source_hbm, sub_hbm,
    history, dsum_ref, count_ref, sums_e, mean_a, profiles,
    loaded, dyn, adj, source_ref, sub_ref, edges, halo, outgoing, merged, arrived_y, arrived, sums, padded, bias, bias_a,
    local_sems, in_sems, halo_send, halo_recv, leg_send, leg_recv,
):
    me = lax.axis_index("dev")
    strides = (devices // 4, devices // 16, devices // 64)
    sibling = me + 1 - 2 * (me % 2)
    above = (me + 1) % devices
    below = (me + devices - 1) % devices

    def along(stride, step):
        at = (me // stride) % 4
        to = (at + step) % 4
        return to, me + (to - at) * stride

    fields, levels, nodes = dyn.shape
    half = nodes // 2
    depth, width = loaded.shape[1], loaded.shape[2]
    parts = width // ROWS
    top = profiles.shape[1]

    barrier = pltpu.get_barrier_semaphore()

    def greet(device):
        pl.semaphore_signal(barrier, inc=1, device_id=(device,), device_id_type=pl.DeviceIdType.MESH)

    greet(above)
    greet(below)
    greet(sibling)
    for stride in strides:
        for step in range(1, 4):
            greet(along(stride, step)[1])

    local = []
    for i, (src, dst) in enumerate(((dyn_hbm, dyn), (source_hbm, source_ref), (sub_hbm, sub_ref), (adj_hbm, adj))):
        local.append(pltpu.make_async_copy(src, dst, local_sems.at[i]))
        local[-1].start()
    loads = []
    for i, (lo, hi) in enumerate(bounds):
        loads.append(pltpu.make_async_copy(cloud_hbm.at[:, lo:hi], loaded.at[:, lo:hi], in_sems.at[i]))
        loads[-1].start()

    local[0].wait()
    on_edge = odious(lanes((levels, LANES)) % 16)
    for f in range(fields):
        for j in range(2):
            direct = dyn[f, :, 2 * j * LANES : (2 * j + 1) * LANES]
            later = dyn[f, :, (2 * j + 1) * LANES : (2 * j + 2) * LANES]
            edges[f, :, j * LANES : (j + 1) * LANES] = jnp.where(on_edge, direct, pltpu.roll(later, 8, axis=1))

    local[1].wait()
    local[2].wait()
    slot = lanes((1, LANES))
    counts = jnp.zeros((1, LANES), jnp.int32)
    for i in range(LANES // span):
        counts = jnp.where(slot // span == i, sub_ref[0:1, i : i + 1], counts)
    source = source_ref[...]
    target = lax.broadcasted_iota(jnp.int32, (devices, LANES), 0)
    to_device = jnp.where(source // LANES == target, counts, 0).astype(jnp.float32).astype(jnp.bfloat16)
    row = lax.broadcasted_iota(jnp.int32, (LANES, LANES), 0)
    to_lane = jnp.where(source % LANES == row, 1.0, 0.0).astype(jnp.bfloat16)
    message = lax.dot_general(to_device, to_lane, (((1,), (1,)), ((), ())), preferred_element_type=jnp.float32)
    outgoing[...] = message.astype(jnp.int32).reshape(outgoing.shape)

    pl.semaphore_wait(barrier, 12)

    def send(src, dst, send_sem, recv_sem, device):
        copy = pltpu.make_async_remote_copy(
            src_ref=src, dst_ref=dst, send_sem=send_sem, recv_sem=recv_sem, device_id=(device,), device_id_type=pl.DeviceIdType.MESH
        )
        copy.start()
        return copy

    rows_y = outgoing.shape[0] // 4
    leg_y, leg_z, leg_x = [], [], []
    for step in range(1, 4):
        to, device = along(strides[0], step)
        leg_y.append(send(outgoing.at[pl.ds(to * rows_y, rows_y)], arrived_y.at[step], leg_send.at[step], leg_recv.at[step], device))
    up = send(edges, halo.at[0], halo_send.at[0], halo_recv.at[0], above)
    down = send(edges, halo.at[1], halo_send.at[1], halo_recv.at[1], below)

    def begin(z, carry):
        all_a, all_e = [], []
        for k in range(parts):
            u0 = loaded[0, z, pl.ds(k, ROWS, stride=parts), :]
            u1 = loaded[1, z, pl.ds(k, ROWS, stride=parts), :]
            all_a.append(u0 + u1)
            all_e.append(u1 - 0.5 * u0)
        for k in range(parts):
            loaded[0, z, k * ROWS : (k + 1) * ROWS, :] = all_a[k]
            loaded[1, z, k * ROWS : (k + 1) * ROWS, :] = all_e[k]
        at = pl.multiple_of(z * ROWS, ROWS)
        sums[0, pl.ds(at, ROWS), :] = total_of(all_a)
        sums[1, pl.ds(at, ROWS), :] = total_of(all_e)
        return carry

    for (lo, hi), copy in zip(bounds, loads):
        copy.wait()
        lax.fori_loop(lo, hi, begin, 0)

    start_a = mean_of(sums.at[0], width)
    start_e = mean_of(sums.at[1], width)
    saturation = saturation_of(top, depth)
    bias_a[...] = -spread(padded, start_a, depth)
    sweep(loaded, history.at[0], 0, None, bias_a, None, False, UNROLL)

    local[3].wait()
    weights = edge_weights(partner_places(me, devices, adj, nodes // 16, half), half)
    row = lax.broadcasted_iota(jnp.int32, (nodes, LANES), 0)
    own_weights = quarter_weights(row // 16, row % 16, ~odious(row % 16))
    pool_weights = quarter_weights(*packed_nodes(lax.broadcasted_iota(jnp.int32, (half, LANES), 0)), True)
    rows = fields * levels
    force_own = split_dot(dyn[...].reshape(rows, nodes), own_weights)
    own_edges = edges[...].reshape(rows, half)
    opposite_own = split_dot(own_edges, weights[:half])

    for copy in leg_y:
        copy.wait_recv()
    at_y = (me // strides[0]) % 4
    merged[...] = outgoing[pl.ds(at_y * rows_y, rows_y)] + arrived_y[1] + arrived_y[2] + arrived_y[3]
    for step in range(1, 4):
        to, device = along(strides[1], step)
        leg_z.append(send(merged.at[to], arrived.at[step], leg_send.at[3 + step], leg_recv.at[3 + step], device))

    up.wait()
    down.wait()
    values = jnp.concatenate([halo[i].reshape(rows, half) for i in range(2)], axis=1)
    averaged = 0.5 * (own_edges + (opposite_own + split_dot(values, weights[half:])))
    force = force_own + split_dot(averaged, pool_weights)
    force_0 = force[0:top]
    force_1 = force[levels : levels + top]
    force_e = force_1 - 0.5 * force_0
    force_a = force_0 + force_1
    bias[...] = spread(padded, 0.3 * (force_e - start_e), depth) - 10.0 * saturation
    sweep(loaded, history.at[0], 1, None, bias, sums_e.at[0], True, UNROLL)

    profiles[0] = start_a
    profiles[1] = start_e
    profiles[2] = 0.3 * force_a
    profiles[3] = spread(padded, saturation + 0.3 * (force_e - saturation), depth) - 10.0 * saturation
    mean_a[0] = 0.1 * spread(padded, 0.7 * start_a + 0.3 * force_a, depth)

    def onward(step, scale):
        before, after = history.at[step - 1], history.at[step]
        bias[...] = scale * profiles[3] - 0.3 * spread(padded, mean_of(sums_e.at[step - 1], width), depth)
        mean_a[step] = 0.1 * spread(padded, 0.7 * mean_a[step - 1] + profiles[2], depth)
        sweep(before, after, 0, None, None, None, False, UNROLL)
        sweep(before, after, 1, None, bias, sums_e.at[step], True, UNROLL)
        return scale * 10.0

    scale = lax.fori_loop(1, AHEAD // 3, onward, jnp.float32(10.0))

    averaged = averaged.reshape(fields, levels, half)
    for f in range(fields):
        for j in range(2):
            part = averaged[f, :, j * LANES : (j + 1) * LANES]
            for v, moved in ((2 * j, part), (2 * j + 1, pltpu.roll(part, LANES - 8, axis=1))):
                at = slice(v * LANES, (v + 1) * LANES)
                dsum_ref[f, :, at] = jnp.where(on_edge, moved, dyn[f, :, at])

    for copy in leg_z:
        copy.wait_recv()
    at_z = (me // strides[1]) % 4
    arrived[0] = merged[at_z] + arrived[1] + arrived[2] + arrived[3]
    for step in range(1, 4):
        to, device = along(strides[2], step)
        leg_x.append(send(arrived.at[0], arrived.at[3 + step], leg_send.at[6 + step], leg_recv.at[6 + step], device))
    scale = lax.fori_loop(AHEAD // 3, 2 * AHEAD // 3, onward, scale)
    for copy in leg_x:
        copy.wait_recv()
    arrived[7] = arrived[0] + arrived[4] + arrived[5] + arrived[6]
    last = send(arrived.at[7], arrived.at[8], leg_send.at[0], leg_recv.at[0], sibling)
    lax.fori_loop(2 * AHEAD // 3, AHEAD, onward, scale)
    last.wait_recv()
    member = pl.ds(me % ROWS, 1)
    count_ref[...] = jnp.broadcast_to(arrived[7, member, :] + arrived[8, member, :], (ROWS, LANES))
    for copy in leg_y + leg_z + leg_x + [last]:
        copy.wait_send()


def cut(depth):
    cuts = [round(i * depth / CHUNKS) for i in range(CHUNKS + 1)]
    return tuple(zip(cuts[:-1], cuts[1:]))


def first(dynamics, adjacency, cloud_state, span_source, substeps, devices):
    fields, levels, nodes = dynamics.shape
    depth, width = cloud_state.shape[1], cloud_state.shape[2]
    top = -(-depth // ROWS) * ROWS
    tiles = devices // ROWS
    span = span_source.shape[0] // substeps.shape[0]
    vmem = pl.BlockSpec(memory_space=pltpu.VMEM)
    hbm = pl.BlockSpec(memory_space=pltpu.HBM)
    profile = pltpu.VMEM((top, LANES), jnp.float32)
    return pl.pallas_call(
        functools.partial(first_kernel, devices, span, cut(depth)),
        out_shape=(
            jax.ShapeDtypeStruct((AHEAD,) + cloud_state.shape, jnp.float32),
            jax.ShapeDtypeStruct(dynamics.shape, jnp.float32),
            jax.ShapeDtypeStruct((ROWS, LANES), jnp.int32),
            jax.ShapeDtypeStruct((AHEAD, top * ROWS, LANES), jnp.float32),
            jax.ShapeDtypeStruct((AHEAD, top, LANES), jnp.float32),
            jax.ShapeDtypeStruct((4, top, LANES), jnp.float32),
        ),
        in_specs=[hbm] * 5,
        out_specs=(vmem,) * 6,
        scratch_shapes=[
            pltpu.VMEM(cloud_state.shape, jnp.float32),
            pltpu.VMEM(dynamics.shape, jnp.float32),
            pltpu.VMEM(adjacency.shape, jnp.int32),
            pltpu.VMEM((1, LANES), jnp.int32),
            pltpu.VMEM((1, substeps.shape[0]), jnp.int32),
            pltpu.VMEM((fields, levels, nodes // 2), jnp.float32),
            pltpu.VMEM((2, fields, levels, nodes // 2), jnp.float32),
            pltpu.VMEM((tiles, ROWS, LANES), jnp.int32),
            pltpu.VMEM((tiles // 4, ROWS, LANES), jnp.int32),
            pltpu.VMEM((4, tiles // 4, ROWS, LANES), jnp.int32),
            pltpu.VMEM((9, ROWS, LANES), jnp.int32),
            pltpu.VMEM((2, top * ROWS, LANES), jnp.float32),
            pltpu.VMEM((top + 2 * PAD, LANES), jnp.float32),
            profile,
            profile,
            pltpu.SemaphoreType.DMA((4,)),
            pltpu.SemaphoreType.DMA((CHUNKS,)),
            pltpu.SemaphoreType.DMA((2,)),
            pltpu.SemaphoreType.DMA((2,)),
            pltpu.SemaphoreType.DMA((10,)),
            pltpu.SemaphoreType.DMA((10,)),
        ],
        compiler_params=pltpu.CompilerParams(collective_id=0, has_side_effects=True, vmem_limit_bytes=16 * 2**20),
        name="first",
    )(*[
        pltpu.with_memory_space_constraint(x, pltpu.HBM)
        for x in (dynamics, adjacency, cloud_state, span_source.reshape(1, -1), substeps.reshape(1, -1))
    ])


def rest_kernel(
    bounds, history, dsum_ref, count_ref, sums_e, means_a, profiles, dsum_out, tend_ref, new_ref,
    state, sums, mean_e, mean_a, bias, out_sems, dsum_sem,
):
    depth, width = state.shape[1], state.shape[2]
    parts = width // ROWS
    top = bias.shape[0]
    dsum_copy = pltpu.make_async_copy(dsum_ref, dsum_out, dsum_sem)
    dsum_copy.start()

    counts = count_ref[...]
    least = jnp.min(counts)
    most = jnp.max(counts)
    saturation = saturation_of(top, depth)

    def advance(scale, source_sums, active):
        bias[...] = scale * profiles[3] - 0.3 * spread(mean_e, mean_of(source_sums, width), depth)
        now = mean_a[PAD : PAD + top, :]
        later = 0.1 * spread(mean_a, 0.7 * now + profiles[2], depth)
        if active is not None:
            later = jnp.where(jnp.broadcast_to(active[0:1], (top, LANES)), later, now)
        mean_a[PAD : PAD + top, :] = later

    def plain(step, scale):
        advance(scale, sums, None)
        sweep(state, state, 0, None, None, None, False, UNROLL)
        sweep(state, state, 1, None, bias, sums, True, UNROLL)
        return scale * 10.0

    def masked(step, scale):
        active = counts > step
        advance(scale, sums, active)
        sweep(state, state, 0, active, None, None, False, UNROLL)
        sweep(state, state, 1, active, bias, sums, True, UNROLL)
        return scale * 10.0

    @pl.when(least > AHEAD)
    def _():
        mean_a[PAD : PAD + top, :] = means_a[AHEAD - 1]
        advance(10.0**AHEAD, sums_e.at[AHEAD - 1], None)
        sweep(history.at[AHEAD - 1], state, 0, None, None, None, False, UNROLL)
        sweep(history.at[AHEAD - 1], state, 1, None, bias, sums, True, UNROLL)

    @pl.when(least <= AHEAD)
    def _():
        def pick(step, carry):
            active = counts > step
            row = active[0:1]

            def level(z, carry):
                for f in range(2):
                    for k in range(parts):
                        at = slice(k * ROWS, (k + 1) * ROWS)
                        state[f, z, at, :] = jnp.where(active, history[step, f, z, at, :], state[f, z, at, :])
                at = pl.ds(pl.multiple_of(z * ROWS, ROWS), ROWS)
                sums[at, :] = jnp.where(active, sums_e[step, at, :], sums[at, :])
                return carry

            lax.fori_loop(0, depth, level, 0)
            here = slice(PAD, PAD + top)
            mean_a[here, :] = jnp.where(jnp.broadcast_to(row, (top, LANES)), means_a[step], mean_a[here, :])
            return carry

        lax.fori_loop(least - 1, jnp.minimum(most, AHEAD), pick, 0)

    done = jnp.where(least > AHEAD, AHEAD + 1, AHEAD)
    middle = jnp.maximum(least, done)
    scale = jnp.where(least > AHEAD, jnp.float32(10.0 ** (AHEAD + 1)), jnp.float32(10.0**AHEAD))
    scale = lax.fori_loop(done, middle, plain, scale)
    lax.fori_loop(middle, most, masked, scale)

    shrink = jnp.ones((ROWS, LANES), jnp.float32)
    for step in range(12):
        shrink = jnp.where(counts > step, shrink * 0.1, shrink)
    new_a = mean_a[PAD : PAD + top, :]
    new_e = mean_of(sums, width) * shrink[0:1] + saturation
    old_a = profiles[0]
    old_e = profiles[1]
    tend_0 = (2.0 / 3.0) * ((new_a - new_e) - (old_a - old_e))
    tend_1 = (new_a - old_a) - tend_0
    tend_ref[:, 0, :] = tend_0[0:depth]
    tend_ref[:, 1, :] = tend_1[0:depth]
    bias[...] = (2.0 / 3.0) * (new_a - saturation)
    shrink_0 = (2.0 / 3.0) * shrink

    def finish(z, carry):
        add_0 = jnp.broadcast_to(bias[pl.ds(z, 1), :], (ROWS, LANES))
        add_a = jnp.broadcast_to(mean_a[pl.ds(PAD + z, 1), :], (ROWS, LANES))
        new_0, new_1 = [], []
        for k in range(parts):
            a = state[0, z, k * ROWS : (k + 1) * ROWS, :]
            e = state[1, z, k * ROWS : (k + 1) * ROWS, :]
            u0 = (a - e) * shrink_0 + add_0
            new_0.append(u0)
            new_1.append((a * shrink + add_a) - u0)
        for k in range(parts):
            state[0, z, pl.ds(k, ROWS, stride=parts), :] = new_0[k]
            state[1, z, pl.ds(k, ROWS, stride=parts), :] = new_1[k]
        return carry

    stores = []
    for i, (lo, hi) in enumerate(bounds):
        lax.fori_loop(lo, hi, finish, 0, unroll=2)
        copy = pltpu.make_async_copy(state.at[:, lo:hi], new_ref.at[:, lo:hi], out_sems.at[i])
        copy.start()
        stores.append(copy)
    for copy in stores:
        copy.wait()
    dsum_copy.wait()


def rest(history, dsum, counts, sums_e, means_a, profiles):
    _, fields, depth, width, _ = history.shape
    top = profiles.shape[1]
    vmem = pl.BlockSpec(memory_space=pltpu.VMEM)
    hbm = pl.BlockSpec(memory_space=pltpu.HBM)
    padded = pltpu.VMEM((top + 2 * PAD, LANES), jnp.float32)
    return pl.pallas_call(
        functools.partial(rest_kernel, cut(depth)),
        out_shape=(
            jax.ShapeDtypeStruct(dsum.shape, jnp.float32),
            jax.ShapeDtypeStruct((depth, fields, LANES), jnp.float32),
            jax.ShapeDtypeStruct(history.shape[1:], jnp.float32),
        ),
        in_specs=[vmem] * 6,
        out_specs=(hbm, vmem, hbm),
        scratch_shapes=[
            pltpu.VMEM(history.shape[1:], jnp.float32),
            pltpu.VMEM(sums_e.shape[1:], jnp.float32),
            padded,
            padded,
            pltpu.VMEM((top, LANES), jnp.float32),
            pltpu.SemaphoreType.DMA((CHUNKS,)),
            pltpu.SemaphoreType.DMA,
        ],
        compiler_params=pltpu.CompilerParams(vmem_limit_bytes=12 * 2**20),
        name="rest",
    )(history, dsum, counts, sums_e, means_a, profiles)


def on_device(dynamics, adjacency, cloud_state, span_source, substeps):
    devices = lax.axis_size("dev")
    carried = first(dynamics, adjacency, cloud_state, span_source, substeps, devices)
    dynamics_summed, tendency, cloud_new = rest(*carried)
    return dynamics_summed, jnp.transpose(tendency, (1, 0, 2)), cloud_new


def solution(mesh):
    in_specs = (
        P(None, None, "dev"),
        P(None, "dev"),
        P(None, None, None, "dev"),
        P("dev"),
        P("dev"),
    )
    out_specs = (P(None, None, "dev"), P(None, None, "dev"), P(None, None, None, "dev"))
    return jax.shard_map(on_device, mesh=mesh, in_specs=in_specs, out_specs=out_specs, check_vma=False)
```

```python
import functools

import jax
import jax.numpy as jnp
from jax import lax
from jax.experimental import pallas as pl
from jax.experimental.pallas import tpu as pltpu
from jax.sharding import PartitionSpec as P

LANES = 128
ROWS = 8
PAD = 8
CHUNKS = 6
AHEAD = 7
READ_Z = 3


def odious(node):
    return ((node ^ (node >> 1) ^ (node >> 2) ^ (node >> 3)) & 1) == 1


def edge_of(node):
    return jnp.where(
        (node == 1) | (node == 2), 0, jnp.where((node == 7) | (node == 11), 1, jnp.where((node == 14) | (node == 13), 2, 3))
    )


def which_of(node):
    return jnp.where((node == 2) | (node == 11) | (node == 13) | (node == 4), 1, 0)


def lanes(shape=(ROWS, LANES)):
    return lax.broadcasted_iota(jnp.int32, shape, len(shape) - 1)


def total_of(parts):
    while len(parts) > 1:
        parts = [a + b for a, b in zip(parts[::2], parts[1::2])] + ([parts[-1]] if len(parts) % 2 else [])
    return parts[0]


def mean_of(sums, width):
    blocks = []
    for start in range(0, sums.shape[0], ROWS * ROWS):
        blocks.append(total_of([sums[pl.ds(start + j, ROWS, stride=ROWS), :] for j in range(ROWS)]))
    return jnp.concatenate(blocks, axis=0) * (1.0 / width)


def spread(ref, values, depth):
    top = values.shape[0]
    ref[PAD : PAD + top, :] = values
    ref[PAD - 1 : PAD, :] = values[0:1]
    ref[PAD + depth : PAD + depth + 1, :] = values[depth - 1 : depth]
    return 8.0 * values + ref[PAD - 1 : PAD - 1 + top, :] + ref[PAD + 1 : PAD + 1 + top, :]


def saturation_of(top, depth):
    height = lax.broadcasted_iota(jnp.int32, (top, LANES), 0).astype(jnp.float32)
    return 0.8 * jnp.exp(-2.0 * height / depth)


def sweep(src, dst, which, active, bias, sums, limit, between=()):
    depth = src.shape[1]
    parts = src.shape[2] // ROWS

    def load(z):
        return [src[which, z, k * ROWS : (k + 1) * ROWS, :] for k in range(parts)]

    def level(z, before, here):
        known = isinstance(z, int)
        after = load(min(z + 1, depth - 1) if known else jnp.minimum(z + 1, depth - 1))
        left = pltpu.roll(here[parts - 1], 1, axis=0)
        right = pltpu.roll(here[0], ROWS - 1, axis=0)
        if bias is not None:
            shift = jnp.broadcast_to(bias[pl.ds(z, 1), :], (ROWS, LANES))
        stepped = []
        for k in range(parts):
            beside = (here[k - 1] if k > 0 else left) + (here[k + 1] if k < parts - 1 else right)
            value = 6.0 * here[k] + (beside + (before[k] + after[k]))
            if bias is not None:
                value = value + shift
            if limit:
                value = jnp.minimum(value, 0.25 * value)
            if active is not None:
                value = jnp.where(active, value, here[k])
            stepped.append(value)
            dst[which, z, k * ROWS : (k + 1) * ROWS, :] = value
        if sums is not None:
            at = z * ROWS if known else pl.multiple_of(z * ROWS, ROWS)
            sums[pl.ds(at, ROWS), :] = total_of(stepped)
        return here, after

    before = here = load(0)
    between = list(between)
    for z in range(depth):
        before, here = level(z, before, here)
        if between:
            between.pop(0)()
    for piece in between:
        piece()


def advance(scale, sums, terms, bias, pad_e, pad_a, now, later, width, depth, active=None):
    top = bias.shape[0]
    blocks = [(at, at + ROWS) for at in range(0, top, ROWS)]

    def spread_of(pad, lo, hi):
        return 8.0 * pad[PAD + lo : PAD + hi, :] + pad[PAD - 1 + lo : PAD - 1 + hi, :] + pad[PAD + 1 + lo : PAD + 1 + hi, :]

    def ends(pad):
        pad[PAD - 1 : PAD, :] = pad[PAD : PAD + 1, :]
        pad[PAD + depth : PAD + depth + 1, :] = pad[PAD + depth - 1 : PAD + depth, :]

    def mean_e(lo, hi):
        rows = [sums[pl.ds(lo * ROWS + j, ROWS, stride=ROWS), :] for j in range(ROWS)]
        pad_e[PAD + lo : PAD + hi, :] = total_of(rows) * (1.0 / width)

    def bias_e(lo, hi):
        bias[lo:hi, :] = scale * terms[3, lo:hi, :] - 0.3 * spread_of(pad_e, lo, hi)

    def relaxed_a(lo, hi):
        pad_a[PAD + lo : PAD + hi, :] = 0.7 * now[lo:hi, :] + terms[2, lo:hi, :]

    def mean_a(lo, hi):
        value = 0.1 * spread_of(pad_a, lo, hi)
        if active is not None:
            value = jnp.where(active, value, now[lo:hi, :])
        later[lo:hi, :] = value

    pieces = [functools.partial(mean_e, *block) for block in blocks] + [functools.partial(ends, pad_e)]
    pieces += [functools.partial(bias_e, *block) for block in blocks]
    pieces += [functools.partial(relaxed_a, *block) for block in blocks] + [functools.partial(ends, pad_a)]
    return pieces + [functools.partial(mean_a, *block) for block in blocks]


def split_dot(values, weights):
    upper = values.astype(jnp.bfloat16)
    lower = (values - upper.astype(jnp.float32)).astype(jnp.bfloat16)
    return jnp.dot(upper, weights, preferred_element_type=jnp.float32) + jnp.dot(lower, weights, preferred_element_type=jnp.float32)


def partner_places(me, devices, adjacency, elements, half):
    across = jnp.broadcast_to(adjacency[0:1, :], (ROWS, LANES))
    facing = jnp.broadcast_to(adjacency[1:2, :], (ROWS, LANES))
    block = (across // elements - me + devices) % devices
    part = jnp.where(block == 0, 0, jnp.where(block == 1, 2, 1))
    places = []
    for t in range(2):
        other = ((2, 1), (11, 7), (13, 14), (4, 8))
        node = jnp.where(
            facing == 0, other[0][t], jnp.where(facing == 1, other[1][t], jnp.where(facing == 2, other[2][t], other[3][t]))
        )
        place = (across % elements) * 16 + node
        in_pair = place % 256
        lane = jnp.where(in_pair < LANES, in_pair, (in_pair - LANES + 8) % LANES)
        places.append(part * half + (place // 256) * LANES + lane)
    return places


def packed_nodes(index):
    lane = index % LANES
    direct = odious(lane % 16)
    moved = (lane + LANES - 8) % LANES
    element = jnp.where(direct, lane // 16, 8 + moved // 16) + (index // LANES) * 16
    return element, jnp.where(direct, lane % 16, moved % 16)


def edge_weights(places, half):
    landing = []
    for v in range(half // LANES):
        element, node = packed_nodes(lanes() + v * LANES)
        index = 4 * element + edge_of(node)
        picked = [jnp.take_along_axis(p, index, axis=1, mode="promise_in_bounds") for p in places]
        landing.append(jnp.where(which_of(node) == 0, picked[0], picked[1])[0:1])
    landing = jnp.concatenate(landing, axis=1)
    row = lax.broadcasted_iota(jnp.int32, (3 * half, half), 0)
    return jnp.where(row == landing, 1.0, 0.0).astype(jnp.bfloat16)


def quarter_weights(element, node, keep):
    column = 4 * element + 2 * (node // 8) + (node % 4) // 2
    here = (column == lax.broadcasted_iota(jnp.int32, column.shape, 1)) & keep
    return jnp.where(here, 0.25, 0.0).astype(jnp.bfloat16)


def first_kernel(
    devices, span, bounds, dyn_hbm, adj_hbm, cloud_hbm, source_hbm, sub_hbm,
    history, dsum_ref, count_ref, sums_e, mean_a, profiles,
    loaded, dyn, adj, source_ref, sub_ref, edges, halo, outgoing, merged, arrived_y, arrived_z, arrived_x,
    sums, padded, padded_a, bias, bias_a,
    local_sems, in_sems, halo_send, halo_recv, leg_send, leg_recv,
):
    me = lax.axis_index("dev")
    strides = (devices // 4, devices // 16)
    member = me % ROWS
    above = (me + 1) % devices
    below = (me + devices - 1) % devices

    def along(stride, step):
        at = (me // stride) % 4
        to = (at + step) % 4
        return to, me + (to - at) * stride

    fields, levels, nodes = dyn.shape
    half = nodes // 2
    depth, width = loaded.shape[1], loaded.shape[2]
    parts = width // ROWS
    top = profiles.shape[1]

    barrier = pltpu.get_barrier_semaphore()

    def greet(device):
        pl.semaphore_signal(barrier, inc=1, device_id=(device,), device_id_type=pl.DeviceIdType.MESH)

    greet(above)
    greet(below)
    for stride in strides:
        for step in range(1, 4):
            greet(along(stride, step)[1])
    for step in range(1, ROWS):
        greet(me - member + (member + step) % ROWS)

    local = []
    for i, (src, dst) in enumerate(((dyn_hbm, dyn), (source_hbm, source_ref), (sub_hbm, sub_ref), (adj_hbm, adj))):
        local.append(pltpu.make_async_copy(src, dst, local_sems.at[i]))
        local[-1].start()
    loads = []
    for i, (lo, hi) in enumerate(bounds):
        loads.append(pltpu.make_async_copy(cloud_hbm.at[:, lo:hi], loaded.at[:, lo:hi], in_sems.at[i]))
        loads[-1].start()

    local[0].wait()
    on_edge = odious(lanes((levels, LANES)) % 16)
    for f in range(fields):
        for j in range(2):
            direct = dyn[f, :, 2 * j * LANES : (2 * j + 1) * LANES]
            later = dyn[f, :, (2 * j + 1) * LANES : (2 * j + 2) * LANES]
            edges[f, :, j * LANES : (j + 1) * LANES] = jnp.where(on_edge, direct, pltpu.roll(later, 8, axis=1))

    local[1].wait()
    local[2].wait()
    slot = lanes((1, LANES))
    counts = jnp.zeros((1, LANES), jnp.int32)
    for i in range(LANES // span):
        counts = jnp.where(slot // span == i, sub_ref[0:1, i : i + 1], counts)
    source = source_ref[...]
    target = lax.broadcasted_iota(jnp.int32, (devices, LANES), 0)
    to_device = jnp.where(source // LANES == target, counts, 0).astype(jnp.float32).astype(jnp.bfloat16)
    row = lax.broadcasted_iota(jnp.int32, (LANES, LANES), 0)
    to_lane = jnp.where(source % LANES == row, 1.0, 0.0).astype(jnp.bfloat16)
    message = lax.dot_general(to_device, to_lane, (((1,), (1,)), ((), ())), preferred_element_type=jnp.float32)
    outgoing[...] = message.astype(jnp.int32).reshape(outgoing.shape)

    pl.semaphore_wait(barrier, 2 + 3 + 3 + ROWS - 1)

    def send(src, dst, send_sem, recv_sem, device):
        copy = pltpu.make_async_remote_copy(
            src_ref=src, dst_ref=dst, send_sem=send_sem, recv_sem=recv_sem, device_id=(device,), device_id_type=pl.DeviceIdType.MESH
        )
        copy.start()
        return copy

    rows_y = outgoing.shape[0] // 4
    leg_y, leg_z, leg_x = [], [], []
    for step in range(1, 4):
        to, device = along(strides[0], step)
        leg_y.append(send(outgoing.at[pl.ds(to * rows_y, rows_y)], arrived_y.at[step], leg_send.at[step], leg_recv.at[step], device))
    up = send(edges, halo.at[0], halo_send.at[0], halo_recv.at[0], above)
    down = send(edges, halo.at[1], halo_send.at[1], halo_recv.at[1], below)

    def begin(z, carry):
        all_a, all_e = [], []
        for k in range(parts):
            u0 = loaded[0, z, pl.ds(k, ROWS, stride=parts), :]
            u1 = loaded[1, z, pl.ds(k, ROWS, stride=parts), :]
            all_a.append(u0 + u1)
            all_e.append(u1 - 0.5 * u0)
        for k in range(parts):
            loaded[0, z, k * ROWS : (k + 1) * ROWS, :] = all_a[k]
            loaded[1, z, k * ROWS : (k + 1) * ROWS, :] = all_e[k]
        at = pl.multiple_of(z * ROWS, ROWS)
        sums[0, pl.ds(at, ROWS), :] = total_of(all_a)
        sums[1, pl.ds(at, ROWS), :] = total_of(all_e)
        return carry

    for (lo, hi), copy in zip(bounds, loads):
        copy.wait()
        lax.fori_loop(lo, hi, begin, 0)

    start_a = mean_of(sums.at[0], width)
    start_e = mean_of(sums.at[1], width)
    saturation = saturation_of(top, depth)
    bias_a[...] = -spread(padded, start_a, depth)
    sweep(loaded, history.at[0], 0, None, bias_a, None, False)

    local[3].wait()
    weights = edge_weights(partner_places(me, devices, adj, nodes // 16, half), half)
    row = lax.broadcasted_iota(jnp.int32, (nodes, LANES), 0)
    own_weights = quarter_weights(row // 16, row % 16, ~odious(row % 16))
    pool_weights = quarter_weights(*packed_nodes(lax.broadcasted_iota(jnp.int32, (half, LANES), 0)), True)
    rows = fields * levels
    force_own = split_dot(dyn[...].reshape(rows, nodes), own_weights)
    own_edges = edges[...].reshape(rows, half)
    opposite_own = split_dot(own_edges, weights[:half])

    for copy in leg_y:
        copy.wait_recv()
    at_y = (me // strides[0]) % 4
    merged[...] = outgoing[pl.ds(at_y * rows_y, rows_y)] + arrived_y[1] + arrived_y[2] + arrived_y[3]
    for step in range(1, 4):
        to, device = along(strides[1], step)
        leg_z.append(send(merged.at[to], arrived_z.at[step], leg_send.at[3 + step], leg_recv.at[3 + step], device))

    up.wait()
    down.wait()
    values = jnp.concatenate([halo[i].reshape(rows, half) for i in range(2)], axis=1)
    averaged = 0.5 * (own_edges + (opposite_own + split_dot(values, weights[half:])))
    force = force_own + split_dot(averaged, pool_weights)
    force_0 = force[0:top]
    force_1 = force[levels : levels + top]
    force_e = force_1 - 0.5 * force_0
    force_a = force_0 + force_1
    bias[...] = spread(padded, 0.3 * (force_e - start_e), depth) - 10.0 * saturation
    sweep(loaded, history.at[0], 1, None, bias, sums_e.at[0], True)

    profiles[0] = start_a
    profiles[1] = start_e
    profiles[2] = 0.3 * force_a
    profiles[3] = spread(padded, saturation + 0.3 * (force_e - saturation), depth) - 10.0 * saturation
    mean_a[0] = 0.1 * spread(padded, 0.7 * start_a + 0.3 * force_a, depth)

    def onward(step, scale):
        before, after = history.at[step - 1], history.at[step]
        pieces = advance(
            scale, sums_e.at[step - 1], profiles, bias, padded, padded_a, mean_a.at[step - 1], mean_a.at[step], width, depth
        )
        sweep(before, after, 0, None, None, None, False, pieces)
        sweep(before, after, 1, None, bias, sums_e.at[step], True)
        return scale * 10.0

    scale = lax.fori_loop(1, READ_Z, onward, jnp.float32(10.0))
    for copy in leg_z:
        copy.wait_recv()
    at_z = (me // strides[1]) % 4
    arrived_x[0] = merged[at_z] + arrived_z[1] + arrived_z[2] + arrived_z[3]
    for step in range(1, ROWS):
        device = me - member + (member + step) % ROWS
        leg_x.append(send(arrived_x.at[0], arrived_x.at[step], leg_send.at[6 + step], leg_recv.at[6 + step], device))
    lax.fori_loop(READ_Z, AHEAD, onward, scale)

    averaged = averaged.reshape(fields, levels, half)
    for f in range(fields):
        for j in range(2):
            part = averaged[f, :, j * LANES : (j + 1) * LANES]
            for v, moved in ((2 * j, part), (2 * j + 1, pltpu.roll(part, LANES - 8, axis=1))):
                at = slice(v * LANES, (v + 1) * LANES)
                dsum_ref[f, :, at] = jnp.where(on_edge, moved, dyn[f, :, at])

    for copy in leg_x:
        copy.wait_recv()
    mine = total_of([arrived_x[i, pl.ds(member, 1), :] for i in range(ROWS)])
    count_ref[...] = jnp.broadcast_to(mine, (ROWS, LANES))
    for copy in leg_y + leg_z + leg_x:
        copy.wait_send()


def cut(depth):
    cuts = [round(i * depth / CHUNKS) for i in range(CHUNKS + 1)]
    return tuple(zip(cuts[:-1], cuts[1:]))


def first(dynamics, adjacency, cloud_state, span_source, substeps, devices):
    fields, levels, nodes = dynamics.shape
    depth, width = cloud_state.shape[1], cloud_state.shape[2]
    top = -(-depth // ROWS) * ROWS
    tiles = devices // ROWS
    span = span_source.shape[0] // substeps.shape[0]
    vmem = pl.BlockSpec(memory_space=pltpu.VMEM)
    hbm = pl.BlockSpec(memory_space=pltpu.HBM)
    profile = pltpu.VMEM((top, LANES), jnp.float32)
    return pl.pallas_call(
        functools.partial(first_kernel, devices, span, cut(depth)),
        out_shape=(
            jax.ShapeDtypeStruct((AHEAD,) + cloud_state.shape, jnp.float32),
            jax.ShapeDtypeStruct(dynamics.shape, jnp.float32),
            jax.ShapeDtypeStruct((ROWS, LANES), jnp.int32),
            jax.ShapeDtypeStruct((AHEAD, top * ROWS, LANES), jnp.float32),
            jax.ShapeDtypeStruct((AHEAD, top, LANES), jnp.float32),
            jax.ShapeDtypeStruct((4, top, LANES), jnp.float32),
        ),
        in_specs=[hbm] * 5,
        out_specs=(vmem,) * 6,
        scratch_shapes=[
            pltpu.VMEM(cloud_state.shape, jnp.float32),
            pltpu.VMEM(dynamics.shape, jnp.float32),
            pltpu.VMEM(adjacency.shape, jnp.int32),
            pltpu.VMEM((1, LANES), jnp.int32),
            pltpu.VMEM((1, substeps.shape[0]), jnp.int32),
            pltpu.VMEM((fields, levels, nodes // 2), jnp.float32),
            pltpu.VMEM((2, fields, levels, nodes // 2), jnp.float32),
            pltpu.VMEM((tiles, ROWS, LANES), jnp.int32),
            pltpu.VMEM((tiles // 4, ROWS, LANES), jnp.int32),
            pltpu.VMEM((4, tiles // 4, ROWS, LANES), jnp.int32),
            pltpu.VMEM((4, ROWS, LANES), jnp.int32),
            pltpu.VMEM((ROWS, ROWS, LANES), jnp.int32),
            pltpu.VMEM((2, top * ROWS, LANES), jnp.float32),
            pltpu.VMEM((top + 2 * PAD, LANES), jnp.float32),
            pltpu.VMEM((top + 2 * PAD, LANES), jnp.float32),
            profile,
            profile,
            pltpu.SemaphoreType.DMA((4,)),
            pltpu.SemaphoreType.DMA((CHUNKS,)),
            pltpu.SemaphoreType.DMA((2,)),
            pltpu.SemaphoreType.DMA((2,)),
            pltpu.SemaphoreType.DMA((14,)),
            pltpu.SemaphoreType.DMA((14,)),
        ],
        compiler_params=pltpu.CompilerParams(collective_id=0, has_side_effects=True, vmem_limit_bytes=10 * 2**20),
        name="first",
    )(*[
        pltpu.with_memory_space_constraint(x, pltpu.HBM)
        for x in (dynamics, adjacency, cloud_state, span_source.reshape(1, -1), substeps.reshape(1, -1))
    ])


def rest_kernel(
    bounds, history, dsum_ref, count_ref, sums_e, means_a, profiles, dsum_out, tend_ref, new_ref,
    state, sums, padded, padded_a, mean_a, bias, out_sems, dsum_sem,
):
    depth, width = state.shape[1], state.shape[2]
    parts = width // ROWS
    top = bias.shape[0]
    dsum_copy = pltpu.make_async_copy(dsum_ref, dsum_out, dsum_sem)
    dsum_copy.start()

    counts = count_ref[...]
    least = jnp.min(counts)
    most = jnp.max(counts)
    saturation = saturation_of(top, depth)

    def substep(src, source_sums, source_mean, scale, active):
        pieces = advance(scale, source_sums, profiles, bias, padded, padded_a, source_mean, mean_a, width, depth, active)
        sweep(src, state, 0, active, None, None, False, pieces)
        sweep(src, state, 1, active, bias, sums, True)
        return scale * 10.0

    def plain(step, scale):
        return substep(state, sums, mean_a, scale, None)

    def masked(step, scale):
        return substep(state, sums, mean_a, scale, counts > step)

    @pl.when(least > AHEAD)
    def _():
        last = AHEAD - 1
        substep(history.at[last], sums_e.at[last], means_a.at[last], 10.0**AHEAD, None)

    @pl.when(least <= AHEAD)
    def _():
        def pick(step, carry):
            active = counts > step

            def level(z, carry):
                for f in range(2):
                    for k in range(parts):
                        at = slice(k * ROWS, (k + 1) * ROWS)
                        state[f, z, at, :] = jnp.where(active, history[step, f, z, at, :], state[f, z, at, :])
                at = pl.ds(pl.multiple_of(z * ROWS, ROWS), ROWS)
                sums[at, :] = jnp.where(active, sums_e[step, at, :], sums[at, :])
                return carry

            lax.fori_loop(0, depth, level, 0)
            mean_a[...] = jnp.where(jnp.broadcast_to(active[0:1], (top, LANES)), means_a[step], mean_a[...])
            return carry

        lax.fori_loop(least - 1, jnp.minimum(most, AHEAD), pick, 0)

    done = jnp.where(least > AHEAD, AHEAD + 1, AHEAD)
    middle = jnp.maximum(least, done)
    scale = jnp.where(least > AHEAD, jnp.float32(10.0 ** (AHEAD + 1)), jnp.float32(10.0**AHEAD))
    scale = lax.fori_loop(done, middle, plain, scale)
    lax.fori_loop(middle, most, masked, scale)

    shrink = jnp.ones((ROWS, LANES), jnp.float32)
    for step in range(12):
        shrink = jnp.where(counts > step, shrink * 0.1, shrink)
    new_a = mean_a[...]
    new_e = mean_of(sums, width) * shrink[0:1] + saturation
    old_a = profiles[0]
    old_e = profiles[1]
    tend_0 = (2.0 / 3.0) * ((new_a - new_e) - (old_a - old_e))
    tend_1 = (new_a - old_a) - tend_0
    tend_ref[:, 0, :] = tend_0[0:depth]
    tend_ref[:, 1, :] = tend_1[0:depth]
    bias[...] = (2.0 / 3.0) * (new_a - saturation)
    shrink_0 = (2.0 / 3.0) * shrink

    def finish(z):
        add_0 = jnp.broadcast_to(bias[pl.ds(z, 1), :], (ROWS, LANES))
        add_a = jnp.broadcast_to(mean_a[pl.ds(z, 1), :], (ROWS, LANES))
        new_0, new_1 = [], []
        for k in range(parts):
            a = state[0, z, k * ROWS : (k + 1) * ROWS, :]
            e = state[1, z, k * ROWS : (k + 1) * ROWS, :]
            u0 = (a - e) * shrink_0 + add_0
            new_0.append(u0)
            new_1.append((a * shrink + add_a) - u0)
        for k in range(parts):
            state[0, z, pl.ds(k, ROWS, stride=parts), :] = new_0[k]
            state[1, z, pl.ds(k, ROWS, stride=parts), :] = new_1[k]

    stores = []
    for i, (lo, hi) in enumerate(bounds):
        for z in range(lo, hi):
            finish(z)
        copy = pltpu.make_async_copy(state.at[:, lo:hi], new_ref.at[:, lo:hi], out_sems.at[i])
        copy.start()
        stores.append(copy)
    for copy in stores:
        copy.wait()
    dsum_copy.wait()


def rest(history, dsum, counts, sums_e, means_a, profiles):
    _, fields, depth, width, _ = history.shape
    top = profiles.shape[1]
    vmem = pl.BlockSpec(memory_space=pltpu.VMEM)
    hbm = pl.BlockSpec(memory_space=pltpu.HBM)
    padded = pltpu.VMEM((top + 2 * PAD, LANES), jnp.float32)
    return pl.pallas_call(
        functools.partial(rest_kernel, cut(depth)),
        out_shape=(
            jax.ShapeDtypeStruct(dsum.shape, jnp.float32),
            jax.ShapeDtypeStruct((depth, fields, LANES), jnp.float32),
            jax.ShapeDtypeStruct(history.shape[1:], jnp.float32),
        ),
        in_specs=[vmem] * 6,
        out_specs=(hbm, vmem, hbm),
        scratch_shapes=[
            pltpu.VMEM(history.shape[1:], jnp.float32),
            pltpu.VMEM(sums_e.shape[1:], jnp.float32),
            padded,
            padded,
            pltpu.VMEM((top, LANES), jnp.float32),
            pltpu.VMEM((top, LANES), jnp.float32),
            pltpu.SemaphoreType.DMA((CHUNKS,)),
            pltpu.SemaphoreType.DMA,
        ],
        compiler_params=pltpu.CompilerParams(vmem_limit_bytes=8 * 2**20),
        name="rest",
    )(history, dsum, counts, sums_e, means_a, profiles)


def on_device(dynamics, adjacency, cloud_state, span_source, substeps):
    devices = lax.axis_size("dev")
    carried = first(dynamics, adjacency, cloud_state, span_source, substeps, devices)
    dynamics_summed, tendency, cloud_new = rest(*carried)
    return dynamics_summed, jnp.transpose(tendency, (1, 0, 2)), cloud_new


def solution(mesh):
    in_specs = (
        P(None, None, "dev"),
        P(None, "dev"),
        P(None, None, None, "dev"),
        P("dev"),
        P("dev"),
    )
    out_specs = (P(None, None, "dev"), P(None, None, "dev"), P(None, None, None, "dev"))
    return jax.shard_map(on_device, mesh=mesh, in_specs=in_specs, out_specs=out_specs, check_vma=False)
```

```python
import functools

import jax
import jax.numpy as jnp
from jax import lax
from jax.experimental import pallas as pl
from jax.experimental.pallas import tpu as pltpu
from jax.sharding import PartitionSpec as P

LANES = 128
ROWS = 8
PAD = 8
CHUNKS = 6
AHEAD = 7


def odious(node):
    return ((node ^ (node >> 1) ^ (node >> 2) ^ (node >> 3)) & 1) == 1


def edge_of(node):
    return jnp.where(
        (node == 1) | (node == 2), 0, jnp.where((node == 7) | (node == 11), 1, jnp.where((node == 14) | (node == 13), 2, 3))
    )


def which_of(node):
    return jnp.where((node == 2) | (node == 11) | (node == 13) | (node == 4), 1, 0)


def lanes(shape=(ROWS, LANES)):
    return lax.broadcasted_iota(jnp.int32, shape, len(shape) - 1)


def total_of(parts):
    while len(parts) > 1:
        parts = [a + b for a, b in zip(parts[::2], parts[1::2])] + ([parts[-1]] if len(parts) % 2 else [])
    return parts[0]


def mean_of(sums, width):
    blocks = []
    for start in range(0, sums.shape[0], ROWS * ROWS):
        blocks.append(total_of([sums[pl.ds(start + j, ROWS, stride=ROWS), :] for j in range(ROWS)]))
    return jnp.concatenate(blocks, axis=0) * (1.0 / width)


def spread(ref, values, depth):
    top = values.shape[0]
    ref[PAD : PAD + top, :] = values
    ref[PAD - 1 : PAD, :] = values[0:1]
    ref[PAD + depth : PAD + depth + 1, :] = values[depth - 1 : depth]
    return 8.0 * values + ref[PAD - 1 : PAD - 1 + top, :] + ref[PAD + 1 : PAD + 1 + top, :]


def saturation_of(top, depth):
    height = lax.broadcasted_iota(jnp.int32, (top, LANES), 0).astype(jnp.float32)
    return 0.8 * jnp.exp(-2.0 * height / depth)


def sweep(src, dst, which, active, bias, sums, limit, between=(), emit=None):
    depth = src.shape[1]
    parts = src.shape[2] // ROWS

    def load(z):
        return [src[which, z, k * ROWS : (k + 1) * ROWS, :] for k in range(parts)]

    def level(z, before, here):
        after = load(min(z + 1, depth - 1))
        left = pltpu.roll(here[parts - 1], 1, axis=0)
        right = pltpu.roll(here[0], ROWS - 1, axis=0)
        if bias is not None:
            shift = jnp.broadcast_to(bias[z : z + 1, :], (ROWS, LANES))
        stepped = []
        for k in range(parts):
            beside = (here[k - 1] if k > 0 else left) + (here[k + 1] if k < parts - 1 else right)
            value = 6.0 * here[k] + (beside + (before[k] + after[k]))
            if bias is not None:
                value = value + shift
            if limit:
                value = jnp.minimum(value, 0.25 * value)
            if active is not None:
                value = jnp.where(active, value, here[k])
            stepped.append(value)
            if emit is None:
                dst[which, z, k * ROWS : (k + 1) * ROWS, :] = value
        if emit is not None:
            emit(z, stepped)
        if sums is not None:
            sums[z * ROWS : (z + 1) * ROWS, :] = total_of(stepped)
        return here, after

    before = here = load(0)
    between = list(between)
    for z in range(depth):
        before, here = level(z, before, here)
        if between:
            between.pop(0)()
    for piece in between:
        piece()


def advance(scale, sums, terms, bias, pad_e, pad_a, now, later, width, depth, active=None):
    top = bias.shape[0]
    blocks = [(at, at + ROWS) for at in range(0, top, ROWS)]

    def spread_of(pad, lo, hi):
        return 8.0 * pad[PAD + lo : PAD + hi, :] + pad[PAD - 1 + lo : PAD - 1 + hi, :] + pad[PAD + 1 + lo : PAD + 1 + hi, :]

    def ends(pad):
        pad[PAD - 1 : PAD, :] = pad[PAD : PAD + 1, :]
        pad[PAD + depth : PAD + depth + 1, :] = pad[PAD + depth - 1 : PAD + depth, :]

    def mean_e(lo, hi):
        rows = [sums[pl.ds(lo * ROWS + j, ROWS, stride=ROWS), :] for j in range(ROWS)]
        pad_e[PAD + lo : PAD + hi, :] = total_of(rows) * (1.0 / width)

    def bias_e(lo, hi):
        bias[lo:hi, :] = scale * terms[3, lo:hi, :] - 0.3 * spread_of(pad_e, lo, hi)

    def relaxed_a(lo, hi):
        pad_a[PAD + lo : PAD + hi, :] = 0.7 * now[lo:hi, :] + terms[2, lo:hi, :]

    def mean_a(lo, hi):
        value = 0.1 * spread_of(pad_a, lo, hi)
        if active is not None:
            value = jnp.where(active, value, now[lo:hi, :])
        later[lo:hi, :] = value

    pieces = [functools.partial(mean_e, *block) for block in blocks] + [functools.partial(ends, pad_e)]
    pieces += [functools.partial(bias_e, *block) for block in blocks]
    pieces += [functools.partial(relaxed_a, *block) for block in blocks] + [functools.partial(ends, pad_a)]
    return pieces + [functools.partial(mean_a, *block) for block in blocks]


def split_dot(values, weights):
    upper = values.astype(jnp.bfloat16)
    lower = (values - upper.astype(jnp.float32)).astype(jnp.bfloat16)
    return jnp.dot(upper, weights, preferred_element_type=jnp.float32) + jnp.dot(lower, weights, preferred_element_type=jnp.float32)


def partner_places(me, devices, adjacency, elements, half):
    across = jnp.broadcast_to(adjacency[0:1, :], (ROWS, LANES))
    facing = jnp.broadcast_to(adjacency[1:2, :], (ROWS, LANES))
    block = (across // elements - me + devices) % devices
    part = jnp.where(block == 0, 0, jnp.where(block == 1, 2, 1))
    places = []
    for t in range(2):
        other = ((2, 1), (11, 7), (13, 14), (4, 8))
        node = jnp.where(
            facing == 0, other[0][t], jnp.where(facing == 1, other[1][t], jnp.where(facing == 2, other[2][t], other[3][t]))
        )
        place = (across % elements) * 16 + node
        in_pair = place % 256
        lane = jnp.where(in_pair < LANES, in_pair, (in_pair - LANES + 8) % LANES)
        places.append(part * half + (place // 256) * LANES + lane)
    return places


def packed_nodes(index):
    lane = index % LANES
    direct = odious(lane % 16)
    moved = (lane + LANES - 8) % LANES
    element = jnp.where(direct, lane // 16, 8 + moved // 16) + (index // LANES) * 16
    return element, jnp.where(direct, lane % 16, moved % 16)


def edge_weights(places, half):
    landing = []
    for v in range(half // LANES):
        element, node = packed_nodes(lanes() + v * LANES)
        index = 4 * element + edge_of(node)
        picked = [jnp.take_along_axis(p, index, axis=1, mode="promise_in_bounds") for p in places]
        landing.append(jnp.where(which_of(node) == 0, picked[0], picked[1])[0:1])
    landing = jnp.concatenate(landing, axis=1)
    row = lax.broadcasted_iota(jnp.int32, (3 * half, half), 0)
    return jnp.where(row == landing, 1.0, 0.0).astype(jnp.bfloat16)


def quarter_weights(element, node, keep):
    column = 4 * element + 2 * (node // 8) + (node % 4) // 2
    here = (column == lax.broadcasted_iota(jnp.int32, column.shape, 1)) & keep
    return jnp.where(here, 0.25, 0.0).astype(jnp.bfloat16)


def first_kernel(
    devices, span, bounds, dyn_hbm, adj_hbm, cloud_hbm, source_hbm, sub_hbm,
    early, state, dsum_ref, count_ref, sums_e, mean_a, profiles,
    loaded, dyn, adj, source_ref, sub_ref, edges, halo, outgoing, merged, arrived_y, arrived_z, arrived_x,
    sums, padded, padded_a, bias, bias_a,
    local_sems, in_sems, halo_send, halo_recv, leg_send, leg_recv,
):
    me = lax.axis_index("dev")
    strides = (devices // 4, devices // 16)
    member = me % ROWS
    above = (me + 1) % devices
    below = (me + devices - 1) % devices

    def along(stride, step):
        at = (me // stride) % 4
        to = (at + step) % 4
        return to, me + (to - at) * stride

    fields, levels, nodes = dyn.shape
    half = nodes // 2
    depth, width = loaded.shape[1], loaded.shape[2]
    parts = width // ROWS
    top = profiles.shape[1]

    barrier = pltpu.get_barrier_semaphore()

    def greet(device):
        pl.semaphore_signal(barrier, inc=1, device_id=(device,), device_id_type=pl.DeviceIdType.MESH)

    greet(above)
    greet(below)
    for stride in strides:
        for step in range(1, 4):
            greet(along(stride, step)[1])
    for step in range(1, ROWS):
        greet(me - member + (member + step) % ROWS)

    local = []
    for i, (src, dst) in enumerate(((dyn_hbm, dyn), (source_hbm, source_ref), (sub_hbm, sub_ref), (adj_hbm, adj))):
        local.append(pltpu.make_async_copy(src, dst, local_sems.at[i]))
        local[-1].start()
    loads = []
    for i, (lo, hi) in enumerate(bounds):
        loads.append(pltpu.make_async_copy(cloud_hbm.at[:, lo:hi], loaded.at[:, lo:hi], in_sems.at[i]))
        loads[-1].start()

    local[0].wait()
    on_edge = odious(lanes((levels, LANES)) % 16)
    for f in range(fields):
        for j in range(2):
            direct = dyn[f, :, 2 * j * LANES : (2 * j + 1) * LANES]
            later = dyn[f, :, (2 * j + 1) * LANES : (2 * j + 2) * LANES]
            edges[f, :, j * LANES : (j + 1) * LANES] = jnp.where(on_edge, direct, pltpu.roll(later, 8, axis=1))

    local[1].wait()
    local[2].wait()
    slot = lanes((1, LANES))
    counts = jnp.zeros((1, LANES), jnp.int32)
    for i in range(LANES // span):
        counts = jnp.where(slot // span == i, sub_ref[0:1, i : i + 1], counts)
    source = source_ref[...]
    target = lax.broadcasted_iota(jnp.int32, (devices, LANES), 0)
    to_device = jnp.where(source // LANES == target, counts, 0).astype(jnp.float32).astype(jnp.bfloat16)
    row = lax.broadcasted_iota(jnp.int32, (LANES, LANES), 0)
    to_lane = jnp.where(source % LANES == row, 1.0, 0.0).astype(jnp.bfloat16)
    message = lax.dot_general(to_device, to_lane, (((1,), (1,)), ((), ())), preferred_element_type=jnp.float32)
    outgoing[...] = message.astype(jnp.int32).reshape(outgoing.shape)

    pl.semaphore_wait(barrier, 2 + 3 + 3 + ROWS - 1)

    def send(src, dst, send_sem, recv_sem, device):
        copy = pltpu.make_async_remote_copy(
            src_ref=src, dst_ref=dst, send_sem=send_sem, recv_sem=recv_sem, device_id=(device,), device_id_type=pl.DeviceIdType.MESH
        )
        copy.start()
        return copy

    rows_y = outgoing.shape[0] // 4
    leg_y, leg_z, leg_x = [], [], []
    for step in range(1, 4):
        to, device = along(strides[0], step)
        leg_y.append(send(outgoing.at[pl.ds(to * rows_y, rows_y)], arrived_y.at[step], leg_send.at[step], leg_recv.at[step], device))
    up = send(edges, halo.at[0], halo_send.at[0], halo_recv.at[0], above)
    down = send(edges, halo.at[1], halo_send.at[1], halo_recv.at[1], below)

    local[3].wait()
    weights = edge_weights(partner_places(me, devices, adj, nodes // 16, half), half)
    row = lax.broadcasted_iota(jnp.int32, (nodes, LANES), 0)
    own_weights = quarter_weights(row // 16, row % 16, ~odious(row % 16))
    pool_weights = quarter_weights(*packed_nodes(lax.broadcasted_iota(jnp.int32, (half, LANES), 0)), True)
    rows = fields * levels
    force_own = split_dot(dyn[...].reshape(rows, nodes), own_weights)
    own_edges = edges[...].reshape(rows, half)
    opposite_own = split_dot(own_edges, weights[:half])

    def begin(z, carry):
        all_a, all_e = [], []
        for k in range(parts):
            u0 = loaded[0, z, pl.ds(k, ROWS, stride=parts), :]
            u1 = loaded[1, z, pl.ds(k, ROWS, stride=parts), :]
            all_a.append(u0 + u1)
            all_e.append(u1 - 0.5 * u0)
        for k in range(parts):
            loaded[0, z, k * ROWS : (k + 1) * ROWS, :] = all_a[k]
            loaded[1, z, k * ROWS : (k + 1) * ROWS, :] = all_e[k]
        at = pl.multiple_of(z * ROWS, ROWS)
        sums[0, pl.ds(at, ROWS), :] = total_of(all_a)
        sums[1, pl.ds(at, ROWS), :] = total_of(all_e)
        return carry

    for (lo, hi), copy in zip(bounds, loads):
        copy.wait()
        lax.fori_loop(lo, hi, begin, 0, unroll=2)

    start_a = mean_of(sums.at[0], width)
    start_e = mean_of(sums.at[1], width)
    saturation = saturation_of(top, depth)
    bias_a[...] = -spread(padded, start_a, depth)
    sweep(loaded, early, 0, None, bias_a, None, False)

    for copy in leg_y:
        copy.wait_recv()
    at_y = (me // strides[0]) % 4
    merged[...] = outgoing[pl.ds(at_y * rows_y, rows_y)] + arrived_y[1] + arrived_y[2] + arrived_y[3]
    for step in range(1, 4):
        to, device = along(strides[1], step)
        leg_z.append(send(merged.at[to], arrived_z.at[step], leg_send.at[3 + step], leg_recv.at[3 + step], device))

    up.wait()
    down.wait()
    values = jnp.concatenate([halo[i].reshape(rows, half) for i in range(2)], axis=1)
    averaged = 0.5 * (own_edges + (opposite_own + split_dot(values, weights[half:])))
    force = force_own + split_dot(averaged, pool_weights)
    force_0 = force[0:top]
    force_1 = force[levels : levels + top]
    force_e = force_1 - 0.5 * force_0
    force_a = force_0 + force_1
    bias[...] = spread(padded, 0.3 * (force_e - start_e), depth) - 10.0 * saturation
    sweep(loaded, early, 1, None, bias, sums_e.at[0], True)

    profiles[0] = start_a
    profiles[1] = start_e
    profiles[2] = 0.3 * force_a
    profiles[3] = spread(padded, saturation + 0.3 * (force_e - saturation), depth) - 10.0 * saturation
    mean_a[0] = 0.1 * spread(padded, 0.7 * start_a + 0.3 * force_a, depth)

    def onward(source, before, scale):
        pieces = advance(
            scale, sums_e.at[before], profiles, bias, padded, padded_a, mean_a.at[before], mean_a.at[1], width, depth
        )
        sweep(source, state, 0, None, None, None, False, pieces)
        sweep(source, state, 1, None, bias, sums_e.at[1], True)
        return scale * 10.0

    onward(early, 0, 10.0)
    for copy in leg_z:
        copy.wait_recv()
    at_z = (me // strides[1]) % 4
    arrived_x[0] = merged[at_z] + arrived_z[1] + arrived_z[2] + arrived_z[3]
    for step in range(1, ROWS):
        device = me - member + (member + step) % ROWS
        leg_x.append(send(arrived_x.at[0], arrived_x.at[step], leg_send.at[6 + step], leg_recv.at[6 + step], device))
    lax.fori_loop(2, AHEAD, lambda step, scale: onward(state, 1, scale), jnp.float32(100.0))

    averaged = averaged.reshape(fields, levels, half)
    for f in range(fields):
        for j in range(2):
            part = averaged[f, :, j * LANES : (j + 1) * LANES]
            for v, moved in ((2 * j, part), (2 * j + 1, pltpu.roll(part, LANES - 8, axis=1))):
                at = slice(v * LANES, (v + 1) * LANES)
                dsum_ref[f, :, at] = jnp.where(on_edge, moved, dyn[f, :, at])

    for copy in leg_x:
        copy.wait_recv()
    mine = total_of([arrived_x[i, pl.ds(member, 1), :] for i in range(ROWS)])
    count_ref[...] = jnp.broadcast_to(mine, (ROWS, LANES))
    for copy in leg_y + leg_z + leg_x:
        copy.wait_send()


def cut(depth):
    cuts = [round(i * depth / CHUNKS) for i in range(CHUNKS + 1)]
    return tuple(zip(cuts[:-1], cuts[1:]))


def first(dynamics, adjacency, cloud_state, span_source, substeps, devices):
    fields, levels, nodes = dynamics.shape
    depth, width = cloud_state.shape[1], cloud_state.shape[2]
    top = -(-depth // ROWS) * ROWS
    tiles = devices // ROWS
    span = span_source.shape[0] // substeps.shape[0]
    vmem = pl.BlockSpec(memory_space=pltpu.VMEM)
    hbm = pl.BlockSpec(memory_space=pltpu.HBM)
    profile = pltpu.VMEM((top, LANES), jnp.float32)
    return pl.pallas_call(
        functools.partial(first_kernel, devices, span, cut(depth)),
        out_shape=(
            jax.ShapeDtypeStruct(cloud_state.shape, jnp.float32),
            jax.ShapeDtypeStruct(cloud_state.shape, jnp.float32),
            jax.ShapeDtypeStruct(dynamics.shape, jnp.float32),
            jax.ShapeDtypeStruct((ROWS, LANES), jnp.int32),
            jax.ShapeDtypeStruct((2, top * ROWS, LANES), jnp.float32),
            jax.ShapeDtypeStruct((2, top, LANES), jnp.float32),
            jax.ShapeDtypeStruct((4, top, LANES), jnp.float32),
        ),
        in_specs=[hbm] * 5,
        out_specs=(vmem,) * 7,
        scratch_shapes=[
            pltpu.VMEM(cloud_state.shape, jnp.float32),
            pltpu.VMEM(dynamics.shape, jnp.float32),
            pltpu.VMEM(adjacency.shape, jnp.int32),
            pltpu.VMEM((1, LANES), jnp.int32),
            pltpu.VMEM((1, substeps.shape[0]), jnp.int32),
            pltpu.VMEM((fields, levels, nodes // 2), jnp.float32),
            pltpu.VMEM((2, fields, levels, nodes // 2), jnp.float32),
            pltpu.VMEM((tiles, ROWS, LANES), jnp.int32),
            pltpu.VMEM((tiles // 4, ROWS, LANES), jnp.int32),
            pltpu.VMEM((4, tiles // 4, ROWS, LANES), jnp.int32),
            pltpu.VMEM((4, ROWS, LANES), jnp.int32),
            pltpu.VMEM((ROWS, ROWS, LANES), jnp.int32),
            pltpu.VMEM((2, top * ROWS, LANES), jnp.float32),
            pltpu.VMEM((top + 2 * PAD, LANES), jnp.float32),
            pltpu.VMEM((top + 2 * PAD, LANES), jnp.float32),
            profile,
            profile,
            pltpu.SemaphoreType.DMA((4,)),
            pltpu.SemaphoreType.DMA((CHUNKS,)),
            pltpu.SemaphoreType.DMA((2,)),
            pltpu.SemaphoreType.DMA((2,)),
            pltpu.SemaphoreType.DMA((14,)),
            pltpu.SemaphoreType.DMA((14,)),
        ],
        compiler_params=pltpu.CompilerParams(collective_id=0, has_side_effects=True, vmem_limit_bytes=10 * 2**20),
        name="first",
    )(*[
        pltpu.with_memory_space_constraint(x, pltpu.HBM)
        for x in (dynamics, adjacency, cloud_state, span_source.reshape(1, -1), substeps.reshape(1, -1))
    ])


def rest_kernel(
    bounds, early, ahead, dsum_ref, count_ref, sums_e, means_a, profiles, dsum_out, tend_ref, new_ref,
    state, sums, padded, padded_a, mean_a, bias, add, out_sems, dsum_sem,
):
    depth, width = state.shape[1], state.shape[2]
    parts = width // ROWS
    top = bias.shape[0]
    dsum_copy = pltpu.make_async_copy(dsum_ref, dsum_out, dsum_sem)
    dsum_copy.start()

    counts = count_ref[...]
    least = jnp.min(counts)
    most = jnp.max(counts)
    saturation = saturation_of(top, depth)

    def substep(src, source_sums, source_mean, scale, active):
        pieces = advance(scale, source_sums, profiles, bias, padded, padded_a, source_mean, mean_a, width, depth, active)
        sweep(src, state, 0, active, None, None, False, pieces)
        sweep(src, state, 1, active, bias, sums, True)
        return scale * 10.0

    def plain(step, scale):
        return substep(state, sums, mean_a, scale, None)

    def masked(step, scale):
        return substep(state, sums, mean_a, scale, counts > step)

    @pl.when(least > AHEAD)
    def _():
        substep(ahead, sums_e.at[1], means_a.at[1], 10.0**AHEAD, None)

    @pl.when(least <= AHEAD)
    def _():
        substep(early, sums_e.at[0], means_a.at[0], 10.0, counts > 1)

    shrink = jnp.ones((ROWS, LANES), jnp.float32)
    for step in range(12):
        shrink = jnp.where(counts > step, shrink * 0.1, shrink)
    shrink_0 = (2.0 / 3.0) * shrink
    copies = [
        pltpu.make_async_copy(state.at[:, lo:hi], new_ref.at[:, lo:hi], out_sems.at[i]) for i, (lo, hi) in enumerate(bounds)
    ]

    def finish(z, e):
        add_0 = jnp.broadcast_to(add[z : z + 1, :], (ROWS, LANES))
        add_a = jnp.broadcast_to(mean_a[z : z + 1, :], (ROWS, LANES))
        new_0, new_1 = [], []
        for k in range(parts):
            a = state[0, z, k * ROWS : (k + 1) * ROWS, :]
            u0 = (a - e[k]) * shrink_0 + add_0
            new_0.append(u0)
            new_1.append((a * shrink + add_a) - u0)
        for k in range(parts):
            state[0, z, pl.ds(k, ROWS, stride=parts), :] = new_0[k]
            state[1, z, pl.ds(k, ROWS, stride=parts), :] = new_1[k]
        for (_, hi), copy in zip(bounds, copies):
            if hi == z + 1:
                copy.start()

    def set_add():
        add[...] = (2.0 / 3.0) * (mean_a[...] - saturation)

    done = jnp.where(least > AHEAD, AHEAD + 1, 2)

    @pl.when(most > done)
    def _():
        scale = jnp.where(least > AHEAD, jnp.float32(10.0 ** (AHEAD + 1)), jnp.float32(100.0))
        middle = jnp.minimum(jnp.maximum(least, done), most - 1)
        scale = lax.fori_loop(done, middle, plain, scale)
        scale = lax.fori_loop(middle, most - 1, masked, scale)
        active = counts > most - 1
        pieces = advance(scale, sums, profiles, bias, padded, padded_a, mean_a, mean_a, width, depth, active)
        sweep(state, state, 0, active, None, None, False, pieces + [set_add])
        sweep(state, state, 1, active, bias, sums, True, (), finish)

    @pl.when(most <= done)
    def _():
        set_add()
        for z in range(depth):
            finish(z, [state[1, z, k * ROWS : (k + 1) * ROWS, :] for k in range(parts)])

    new_a = mean_a[...]
    new_e = mean_of(sums, width) * shrink[0:1] + saturation
    old_a = profiles[0]
    old_e = profiles[1]
    tend_0 = (2.0 / 3.0) * ((new_a - new_e) - (old_a - old_e))
    tend_1 = (new_a - old_a) - tend_0
    tend_ref[:, 0, :] = tend_0[0:depth]
    tend_ref[:, 1, :] = tend_1[0:depth]
    for copy in copies:
        copy.wait()
    dsum_copy.wait()


def rest(early, ahead, dsum, counts, sums_e, means_a, profiles):
    fields, depth, width, _ = early.shape
    top = profiles.shape[1]
    vmem = pl.BlockSpec(memory_space=pltpu.VMEM)
    hbm = pl.BlockSpec(memory_space=pltpu.HBM)
    padded = pltpu.VMEM((top + 2 * PAD, LANES), jnp.float32)
    return pl.pallas_call(
        functools.partial(rest_kernel, cut(depth)),
        out_shape=(
            jax.ShapeDtypeStruct(dsum.shape, jnp.float32),
            jax.ShapeDtypeStruct((depth, fields, LANES), jnp.float32),
            jax.ShapeDtypeStruct(early.shape, jnp.float32),
        ),
        in_specs=[vmem] * 7,
        out_specs=(hbm, vmem, hbm),
        scratch_shapes=[
            pltpu.VMEM(early.shape, jnp.float32),
            pltpu.VMEM(sums_e.shape[1:], jnp.float32),
            padded,
            padded,
            pltpu.VMEM((top, LANES), jnp.float32),
            pltpu.VMEM((top, LANES), jnp.float32),
            pltpu.VMEM((top, LANES), jnp.float32),
            pltpu.SemaphoreType.DMA((CHUNKS,)),
            pltpu.SemaphoreType.DMA,
        ],
        compiler_params=pltpu.CompilerParams(vmem_limit_bytes=8 * 2**20),
        name="rest",
    )(early, ahead, dsum, counts, sums_e, means_a, profiles)


def on_device(dynamics, adjacency, cloud_state, span_source, substeps):
    devices = lax.axis_size("dev")
    carried = first(dynamics, adjacency, cloud_state, span_source, substeps, devices)
    dynamics_summed, tendency, cloud_new = rest(*carried)
    return dynamics_summed, jnp.transpose(tendency, (1, 0, 2)), cloud_new


def solution(mesh):
    in_specs = (
        P(None, None, "dev"),
        P(None, "dev"),
        P(None, None, None, "dev"),
        P("dev"),
        P("dev"),
    )
    out_specs = (P(None, None, "dev"), P(None, None, "dev"), P(None, None, None, "dev"))
    return jax.shard_map(on_device, mesh=mesh, in_specs=in_specs, out_specs=out_specs, check_vma=False)
```

```python
import functools

import jax
import jax.numpy as jnp
from jax import lax
from jax.experimental import pallas as pl
from jax.experimental.pallas import tpu as pltpu
from jax.sharding import PartitionSpec as P

LANES = 128
ROWS = 8
PAD = 8
CHUNKS = 6
AHEAD = 7
EARLY_CHUNKS = 2


def odious(node):
    return ((node ^ (node >> 1) ^ (node >> 2) ^ (node >> 3)) & 1) == 1


def edge_of(node):
    return jnp.where(
        (node == 1) | (node == 2), 0, jnp.where((node == 7) | (node == 11), 1, jnp.where((node == 14) | (node == 13), 2, 3))
    )


def which_of(node):
    return jnp.where((node == 2) | (node == 11) | (node == 13) | (node == 4), 1, 0)


def lanes(shape=(ROWS, LANES)):
    return lax.broadcasted_iota(jnp.int32, shape, len(shape) - 1)


def total_of(parts):
    while len(parts) > 1:
        parts = [a + b for a, b in zip(parts[::2], parts[1::2])] + ([parts[-1]] if len(parts) % 2 else [])
    return parts[0]


def mean_of(sums, width):
    blocks = []
    for start in range(0, sums.shape[0], ROWS * ROWS):
        blocks.append(total_of([sums[pl.ds(start + j, ROWS, stride=ROWS), :] for j in range(ROWS)]))
    return jnp.concatenate(blocks, axis=0) * (1.0 / width)


def spread(ref, values, depth):
    top = values.shape[0]
    ref[PAD : PAD + top, :] = values
    ref[PAD - 1 : PAD, :] = values[0:1]
    ref[PAD + depth : PAD + depth + 1, :] = values[depth - 1 : depth]
    return 8.0 * values + ref[PAD - 1 : PAD - 1 + top, :] + ref[PAD + 1 : PAD + 1 + top, :]


def saturation_of(top, depth):
    height = lax.broadcasted_iota(jnp.int32, (top, LANES), 0).astype(jnp.float32)
    return 0.8 * jnp.exp(-2.0 * height / depth)


def sweep(src, dst, which, active, bias, sums, limit, between=(), emit=None):
    depth = src.shape[1]
    parts = src.shape[2] // ROWS

    def load(z):
        return [src[which, z, k * ROWS : (k + 1) * ROWS, :] for k in range(parts)]

    def level(z, before, here):
        after = load(min(z + 1, depth - 1))
        left = pltpu.roll(here[parts - 1], 1, axis=0)
        right = pltpu.roll(here[0], ROWS - 1, axis=0)
        if bias is not None:
            shift = jnp.broadcast_to(bias[z : z + 1, :], (ROWS, LANES))
        stepped = []
        for k in range(parts):
            beside = (here[k - 1] if k > 0 else left) + (here[k + 1] if k < parts - 1 else right)
            value = 6.0 * here[k] + (beside + (before[k] + after[k]))
            if bias is not None:
                value = value + shift
            if limit:
                value = jnp.minimum(value, 0.25 * value)
            if active is not None:
                value = jnp.where(active, value, here[k])
            stepped.append(value)
            if emit is None:
                dst[which, z, k * ROWS : (k + 1) * ROWS, :] = value
        if emit is not None:
            emit(z, stepped)
        if sums is not None:
            sums[z * ROWS : (z + 1) * ROWS, :] = total_of(stepped)
        return here, after

    before = here = load(0)
    between = list(between)
    for z in range(depth):
        before, here = level(z, before, here)
        if between:
            between.pop(0)()
    for piece in between:
        piece()


def advance(scale, sums, terms, bias, pad_e, pad_a, now, later, width, depth, active=None):
    top = bias.shape[0]
    blocks = [(at, at + ROWS) for at in range(0, top, ROWS)]

    def spread_of(pad, lo, hi):
        return 8.0 * pad[PAD + lo : PAD + hi, :] + pad[PAD - 1 + lo : PAD - 1 + hi, :] + pad[PAD + 1 + lo : PAD + 1 + hi, :]

    def ends(pad):
        pad[PAD - 1 : PAD, :] = pad[PAD : PAD + 1, :]
        pad[PAD + depth : PAD + depth + 1, :] = pad[PAD + depth - 1 : PAD + depth, :]

    def mean_e(lo, hi):
        rows = [sums[pl.ds(lo * ROWS + j, ROWS, stride=ROWS), :] for j in range(ROWS)]
        pad_e[PAD + lo : PAD + hi, :] = total_of(rows) * (1.0 / width)

    def bias_e(lo, hi):
        bias[lo:hi, :] = scale * terms[3, lo:hi, :] - 0.3 * spread_of(pad_e, lo, hi)

    def relaxed_a(lo, hi):
        pad_a[PAD + lo : PAD + hi, :] = 0.7 * now[lo:hi, :] + terms[2, lo:hi, :]

    def mean_a(lo, hi):
        value = 0.1 * spread_of(pad_a, lo, hi)
        if active is not None:
            value = jnp.where(active, value, now[lo:hi, :])
        later[lo:hi, :] = value

    pieces = [functools.partial(mean_e, *block) for block in blocks] + [functools.partial(ends, pad_e)]
    pieces += [functools.partial(bias_e, *block) for block in blocks]
    pieces += [functools.partial(relaxed_a, *block) for block in blocks] + [functools.partial(ends, pad_a)]
    return pieces + [functools.partial(mean_a, *block) for block in blocks]


def split_dot(values, weights):
    upper = values.astype(jnp.bfloat16)
    lower = (values - upper.astype(jnp.float32)).astype(jnp.bfloat16)
    return jnp.dot(upper, weights, preferred_element_type=jnp.float32) + jnp.dot(lower, weights, preferred_element_type=jnp.float32)


def partner_places(me, devices, adjacency, elements, half):
    across = jnp.broadcast_to(adjacency[0:1, :], (ROWS, LANES))
    facing = jnp.broadcast_to(adjacency[1:2, :], (ROWS, LANES))
    block = (across // elements - me + devices) % devices
    part = jnp.where(block == 0, 0, jnp.where(block == 1, 2, 1))
    places = []
    for t in range(2):
        other = ((2, 1), (11, 7), (13, 14), (4, 8))
        node = jnp.where(
            facing == 0, other[0][t], jnp.where(facing == 1, other[1][t], jnp.where(facing == 2, other[2][t], other[3][t]))
        )
        place = (across % elements) * 16 + node
        in_pair = place % 256
        lane = jnp.where(in_pair < LANES, in_pair, (in_pair - LANES + 8) % LANES)
        places.append(part * half + (place // 256) * LANES + lane)
    return places


def packed_nodes(index):
    lane = index % LANES
    direct = odious(lane % 16)
    moved = (lane + LANES - 8) % LANES
    element = jnp.where(direct, lane // 16, 8 + moved // 16) + (index // LANES) * 16
    return element, jnp.where(direct, lane % 16, moved % 16)


def edge_weights(places, half):
    landing = []
    for v in range(half // LANES):
        element, node = packed_nodes(lanes() + v * LANES)
        index = 4 * element + edge_of(node)
        picked = [jnp.take_along_axis(p, index, axis=1, mode="promise_in_bounds") for p in places]
        landing.append(jnp.where(which_of(node) == 0, picked[0], picked[1])[0:1])
    landing = jnp.concatenate(landing, axis=1)
    row = lax.broadcasted_iota(jnp.int32, (3 * half, half), 0)
    return jnp.where(row == landing, 1.0, 0.0).astype(jnp.bfloat16)


def quarter_weights(element, node, keep):
    column = 4 * element + 2 * (node // 8) + (node % 4) // 2
    here = (column == lax.broadcasted_iota(jnp.int32, column.shape, 1)) & keep
    return jnp.where(here, 0.25, 0.0).astype(jnp.bfloat16)


def first_kernel(
    devices, span, bounds, dyn_hbm, adj_hbm, cloud_hbm, source_hbm, sub_hbm,
    early, state, dsum_ref, count_ref, sums_e, mean_a, profiles,
    loaded, dyn, adj, source_ref, sub_ref, edges, halo, outgoing, merged, arrived_y, arrived_z, arrived_x,
    sums, padded, padded_a, bias, bias_a,
    local_sems, in_sems, halo_send, halo_recv, leg_send, leg_recv,
):
    me = lax.axis_index("dev")
    strides = (devices // 4, devices // 16)
    member = me % ROWS
    above = (me + 1) % devices
    below = (me + devices - 1) % devices

    def along(stride, step):
        at = (me // stride) % 4
        to = (at + step) % 4
        return to, me + (to - at) * stride

    fields, levels, nodes = dyn.shape
    half = nodes // 2
    depth, width = loaded.shape[1], loaded.shape[2]
    parts = width // ROWS
    top = profiles.shape[1]

    barrier = pltpu.get_barrier_semaphore()

    def greet(device):
        pl.semaphore_signal(barrier, inc=1, device_id=(device,), device_id_type=pl.DeviceIdType.MESH)

    greet(above)
    greet(below)
    for stride in strides:
        for step in range(1, 4):
            greet(along(stride, step)[1])
    for step in range(1, ROWS):
        greet(me - member + (member + step) % ROWS)

    local = []
    for i, (src, dst) in enumerate(((dyn_hbm, dyn), (source_hbm, source_ref), (sub_hbm, sub_ref), (adj_hbm, adj))):
        local.append(pltpu.make_async_copy(src, dst, local_sems.at[i]))
        local[-1].start()
    loads = []
    for i, (lo, hi) in enumerate(bounds):
        loads.append(pltpu.make_async_copy(cloud_hbm.at[:, lo:hi], loaded.at[:, lo:hi], in_sems.at[i]))
        loads[-1].start()

    local[0].wait()
    on_edge = odious(lanes((levels, LANES)) % 16)
    for f in range(fields):
        for j in range(2):
            direct = dyn[f, :, 2 * j * LANES : (2 * j + 1) * LANES]
            later = dyn[f, :, (2 * j + 1) * LANES : (2 * j + 2) * LANES]
            edges[f, :, j * LANES : (j + 1) * LANES] = jnp.where(on_edge, direct, pltpu.roll(later, 8, axis=1))

    local[1].wait()
    local[2].wait()
    slot = lanes((1, LANES))
    counts = jnp.zeros((1, LANES), jnp.int32)
    for i in range(LANES // span):
        counts = jnp.where(slot // span == i, sub_ref[0:1, i : i + 1], counts)
    source = source_ref[...]
    target = lax.broadcasted_iota(jnp.int32, (devices, LANES), 0)
    to_device = jnp.where(source // LANES == target, counts, 0).astype(jnp.float32).astype(jnp.bfloat16)
    row = lax.broadcasted_iota(jnp.int32, (LANES, LANES), 0)
    to_lane = jnp.where(source % LANES == row, 1.0, 0.0).astype(jnp.bfloat16)
    message = lax.dot_general(to_device, to_lane, (((1,), (1,)), ((), ())), preferred_element_type=jnp.float32)
    outgoing[...] = message.astype(jnp.int32).reshape(outgoing.shape)

    local[3].wait()
    weights = edge_weights(partner_places(me, devices, adj, nodes // 16, half), half)
    row = lax.broadcasted_iota(jnp.int32, (nodes, LANES), 0)
    own_weights = quarter_weights(row // 16, row % 16, ~odious(row % 16))
    pool_weights = quarter_weights(*packed_nodes(lax.broadcasted_iota(jnp.int32, (half, LANES), 0)), True)
    rows = fields * levels
    force_own = split_dot(dyn[...].reshape(rows, nodes), own_weights)
    own_edges = edges[...].reshape(rows, half)
    opposite_own = split_dot(own_edges, weights[:half])

    def begin(z, carry):
        all_a, all_e = [], []
        for k in range(parts):
            u0 = loaded[0, z, pl.ds(k, ROWS, stride=parts), :]
            u1 = loaded[1, z, pl.ds(k, ROWS, stride=parts), :]
            all_a.append(u0 + u1)
            all_e.append(u1 - 0.5 * u0)
        for k in range(parts):
            loaded[0, z, k * ROWS : (k + 1) * ROWS, :] = all_a[k]
            loaded[1, z, k * ROWS : (k + 1) * ROWS, :] = all_e[k]
        at = pl.multiple_of(z * ROWS, ROWS)
        sums[0, pl.ds(at, ROWS), :] = total_of(all_a)
        sums[1, pl.ds(at, ROWS), :] = total_of(all_e)
        return carry

    def begin_part(part):
        for (lo, hi), copy in list(zip(bounds, loads))[part]:
            copy.wait()
            lax.fori_loop(lo, hi, begin, 0, unroll=2)

    begin_part(slice(0, EARLY_CHUNKS))

    pl.semaphore_wait(barrier, 2 + 3 + 3 + ROWS - 1)

    def send(src, dst, send_sem, recv_sem, device):
        copy = pltpu.make_async_remote_copy(
            src_ref=src, dst_ref=dst, send_sem=send_sem, recv_sem=recv_sem, device_id=(device,), device_id_type=pl.DeviceIdType.MESH
        )
        copy.start()
        return copy

    rows_y = outgoing.shape[0] // 4
    leg_y, leg_z, leg_x = [], [], []
    for step in range(1, 4):
        to, device = along(strides[0], step)
        leg_y.append(send(outgoing.at[pl.ds(to * rows_y, rows_y)], arrived_y.at[step], leg_send.at[step], leg_recv.at[step], device))
    up = send(edges, halo.at[0], halo_send.at[0], halo_recv.at[0], above)
    down = send(edges, halo.at[1], halo_send.at[1], halo_recv.at[1], below)

    begin_part(slice(EARLY_CHUNKS, CHUNKS))

    start_a = mean_of(sums.at[0], width)
    start_e = mean_of(sums.at[1], width)
    saturation = saturation_of(top, depth)
    bias_a[...] = -spread(padded, start_a, depth)
    sweep(loaded, early, 0, None, bias_a, None, False)
    sweep(early, state, 0, None, None, None, False)

    for copy in leg_y:
        copy.wait_recv()
    at_y = (me // strides[0]) % 4
    merged[...] = outgoing[pl.ds(at_y * rows_y, rows_y)] + arrived_y[1] + arrived_y[2] + arrived_y[3]
    for step in range(1, 4):
        to, device = along(strides[1], step)
        leg_z.append(send(merged.at[to], arrived_z.at[step], leg_send.at[3 + step], leg_recv.at[3 + step], device))

    def further(step, carry):
        sweep(state, state, 0, None, None, None, False)
        return carry

    lax.fori_loop(2, AHEAD, further, 0)

    up.wait()
    down.wait()
    values = jnp.concatenate([halo[i].reshape(rows, half) for i in range(2)], axis=1)
    averaged = 0.5 * (own_edges + (opposite_own + split_dot(values, weights[half:])))
    force = force_own + split_dot(averaged, pool_weights)
    force_0 = force[0:top]
    force_1 = force[levels : levels + top]
    force_e = force_1 - 0.5 * force_0
    force_a = force_0 + force_1
    bias[...] = spread(padded, 0.3 * (force_e - start_e), depth) - 10.0 * saturation
    sweep(loaded, early, 1, None, bias, sums_e.at[0], True)

    profiles[0] = start_a
    profiles[1] = start_e
    profiles[2] = 0.3 * force_a
    profiles[3] = spread(padded, saturation + 0.3 * (force_e - saturation), depth) - 10.0 * saturation
    mean_a[0] = 0.1 * spread(padded, 0.7 * start_a + 0.3 * force_a, depth)

    def onward(source, before, scale):
        pieces = advance(
            scale, sums_e.at[before], profiles, bias, padded, padded_a, mean_a.at[before], mean_a.at[1], width, depth
        )
        for piece in pieces:
            piece()
        sweep(source, state, 1, None, bias, sums_e.at[1], True)
        return scale * 10.0

    onward(early, 0, 10.0)
    for copy in leg_z:
        copy.wait_recv()
    at_z = (me // strides[1]) % 4
    arrived_x[0] = merged[at_z] + arrived_z[1] + arrived_z[2] + arrived_z[3]
    for step in range(1, ROWS):
        device = me - member + (member + step) % ROWS
        leg_x.append(send(arrived_x.at[0], arrived_x.at[step], leg_send.at[6 + step], leg_recv.at[6 + step], device))
    lax.fori_loop(2, AHEAD, lambda step, scale: onward(state, 1, scale), jnp.float32(100.0))

    averaged = averaged.reshape(fields, levels, half)
    for f in range(fields):
        for j in range(2):
            part = averaged[f, :, j * LANES : (j + 1) * LANES]
            for v, moved in ((2 * j, part), (2 * j + 1, pltpu.roll(part, LANES - 8, axis=1))):
                at = slice(v * LANES, (v + 1) * LANES)
                dsum_ref[f, :, at] = jnp.where(on_edge, moved, dyn[f, :, at])

    for copy in leg_x:
        copy.wait_recv()
    mine = total_of([arrived_x[i, pl.ds(member, 1), :] for i in range(ROWS)])
    count_ref[...] = jnp.broadcast_to(mine, (ROWS, LANES))
    for copy in leg_y + leg_z + leg_x:
        copy.wait_send()


def cut(depth):
    cuts = [round(i * depth / CHUNKS) for i in range(CHUNKS + 1)]
    return tuple(zip(cuts[:-1], cuts[1:]))


def first(dynamics, adjacency, cloud_state, span_source, substeps, devices):
    fields, levels, nodes = dynamics.shape
    depth, width = cloud_state.shape[1], cloud_state.shape[2]
    top = -(-depth // ROWS) * ROWS
    tiles = devices // ROWS
    span = span_source.shape[0] // substeps.shape[0]
    vmem = pl.BlockSpec(memory_space=pltpu.VMEM)
    hbm = pl.BlockSpec(memory_space=pltpu.HBM)
    profile = pltpu.VMEM((top, LANES), jnp.float32)
    return pl.pallas_call(
        functools.partial(first_kernel, devices, span, cut(depth)),
        out_shape=(
            jax.ShapeDtypeStruct(cloud_state.shape, jnp.float32),
            jax.ShapeDtypeStruct(cloud_state.shape, jnp.float32),
            jax.ShapeDtypeStruct(dynamics.shape, jnp.float32),
            jax.ShapeDtypeStruct((ROWS, LANES), jnp.int32),
            jax.ShapeDtypeStruct((2, top * ROWS, LANES), jnp.float32),
            jax.ShapeDtypeStruct((2, top, LANES), jnp.float32),
            jax.ShapeDtypeStruct((4, top, LANES), jnp.float32),
        ),
        in_specs=[hbm] * 5,
        out_specs=(vmem,) * 7,
        scratch_shapes=[
            pltpu.VMEM(cloud_state.shape, jnp.float32),
            pltpu.VMEM(dynamics.shape, jnp.float32),
            pltpu.VMEM(adjacency.shape, jnp.int32),
            pltpu.VMEM((1, LANES), jnp.int32),
            pltpu.VMEM((1, substeps.shape[0]), jnp.int32),
            pltpu.VMEM((fields, levels, nodes // 2), jnp.float32),
            pltpu.VMEM((2, fields, levels, nodes // 2), jnp.float32),
            pltpu.VMEM((tiles, ROWS, LANES), jnp.int32),
            pltpu.VMEM((tiles // 4, ROWS, LANES), jnp.int32),
            pltpu.VMEM((4, tiles // 4, ROWS, LANES), jnp.int32),
            pltpu.VMEM((4, ROWS, LANES), jnp.int32),
            pltpu.VMEM((ROWS, ROWS, LANES), jnp.int32),
            pltpu.VMEM((2, top * ROWS, LANES), jnp.float32),
            pltpu.VMEM((top + 2 * PAD, LANES), jnp.float32),
            pltpu.VMEM((top + 2 * PAD, LANES), jnp.float32),
            profile,
            profile,
            pltpu.SemaphoreType.DMA((4,)),
            pltpu.SemaphoreType.DMA((CHUNKS,)),
            pltpu.SemaphoreType.DMA((2,)),
            pltpu.SemaphoreType.DMA((2,)),
            pltpu.SemaphoreType.DMA((14,)),
            pltpu.SemaphoreType.DMA((14,)),
        ],
        compiler_params=pltpu.CompilerParams(collective_id=0, has_side_effects=True, vmem_limit_bytes=10 * 2**20),
        name="first",
    )(*[
        pltpu.with_memory_space_constraint(x, pltpu.HBM)
        for x in (dynamics, adjacency, cloud_state, span_source.reshape(1, -1), substeps.reshape(1, -1))
    ])


def rest_kernel(
    bounds, early, ahead, dsum_ref, count_ref, sums_e, means_a, profiles, dsum_out, tend_ref, new_ref,
    state, sums, padded, padded_a, mean_a, bias, add, out_sems, dsum_sem,
):
    depth, width = state.shape[1], state.shape[2]
    parts = width // ROWS
    top = bias.shape[0]
    dsum_copy = pltpu.make_async_copy(dsum_ref, dsum_out, dsum_sem)
    dsum_copy.start()

    counts = count_ref[...]
    least = jnp.min(counts)
    most = jnp.max(counts)
    saturation = saturation_of(top, depth)

    def substep(src, source_sums, source_mean, scale, active):
        pieces = advance(scale, source_sums, profiles, bias, padded, padded_a, source_mean, mean_a, width, depth, active)
        sweep(src, state, 0, active, None, None, False, pieces)
        sweep(src, state, 1, active, bias, sums, True)
        return scale * 10.0

    def plain(step, scale):
        return substep(state, sums, mean_a, scale, None)

    def masked(step, scale):
        return substep(state, sums, mean_a, scale, counts > step)

    @pl.when(least > AHEAD)
    def _():
        substep(ahead, sums_e.at[1], means_a.at[1], 10.0**AHEAD, None)

    @pl.when(least <= AHEAD)
    def _():
        substep(early, sums_e.at[0], means_a.at[0], 10.0, counts > 1)

    shrink = jnp.ones((ROWS, LANES), jnp.float32)
    for step in range(12):
        shrink = jnp.where(counts > step, shrink * 0.1, shrink)
    shrink_0 = (2.0 / 3.0) * shrink
    copies = [
        pltpu.make_async_copy(state.at[:, lo:hi], new_ref.at[:, lo:hi], out_sems.at[i]) for i, (lo, hi) in enumerate(bounds)
    ]

    def finish(z, e):
        add_0 = jnp.broadcast_to(add[z : z + 1, :], (ROWS, LANES))
        add_a = jnp.broadcast_to(mean_a[z : z + 1, :], (ROWS, LANES))
        new_0, new_1 = [], []
        for k in range(parts):
            a = state[0, z, k * ROWS : (k + 1) * ROWS, :]
            u0 = (a - e[k]) * shrink_0 + add_0
            new_0.append(u0)
            new_1.append((a * shrink + add_a) - u0)
        for k in range(parts):
            state[0, z, pl.ds(k, ROWS, stride=parts), :] = new_0[k]
            state[1, z, pl.ds(k, ROWS, stride=parts), :] = new_1[k]
        for (_, hi), copy in zip(bounds, copies):
            if hi == z + 1:
                copy.start()

    def set_add():
        add[...] = (2.0 / 3.0) * (mean_a[...] - saturation)

    done = jnp.where(least > AHEAD, AHEAD + 1, 2)

    @pl.when(most > done)
    def _():
        scale = jnp.where(least > AHEAD, jnp.float32(10.0 ** (AHEAD + 1)), jnp.float32(100.0))
        middle = jnp.minimum(jnp.maximum(least, done), most - 1)
        scale = lax.fori_loop(done, middle, plain, scale)
        scale = lax.fori_loop(middle, most - 1, masked, scale)
        active = counts > most - 1
        pieces = advance(scale, sums, profiles, bias, padded, padded_a, mean_a, mean_a, width, depth, active)
        sweep(state, state, 0, active, None, None, False, pieces + [set_add])
        sweep(state, state, 1, active, bias, sums, True, (), finish)

    @pl.when(most <= done)
    def _():
        set_add()
        for z in range(depth):
            finish(z, [state[1, z, k * ROWS : (k + 1) * ROWS, :] for k in range(parts)])

    new_a = mean_a[...]
    new_e = mean_of(sums, width) * shrink[0:1] + saturation
    old_a = profiles[0]
    old_e = profiles[1]
    tend_0 = (2.0 / 3.0) * ((new_a - new_e) - (old_a - old_e))
    tend_1 = (new_a - old_a) - tend_0
    tend_ref[:, 0, :] = tend_0[0:depth]
    tend_ref[:, 1, :] = tend_1[0:depth]
    for copy in copies:
        copy.wait()
    dsum_copy.wait()


def rest(early, ahead, dsum, counts, sums_e, means_a, profiles):
    fields, depth, width, _ = early.shape
    top = profiles.shape[1]
    vmem = pl.BlockSpec(memory_space=pltpu.VMEM)
    hbm = pl.BlockSpec(memory_space=pltpu.HBM)
    padded = pltpu.VMEM((top + 2 * PAD, LANES), jnp.float32)
    return pl.pallas_call(
        functools.partial(rest_kernel, cut(depth)),
        out_shape=(
            jax.ShapeDtypeStruct(dsum.shape, jnp.float32),
            jax.ShapeDtypeStruct((depth, fields, LANES), jnp.float32),
            jax.ShapeDtypeStruct(early.shape, jnp.float32),
        ),
        in_specs=[vmem] * 7,
        out_specs=(hbm, vmem, hbm),
        scratch_shapes=[
            pltpu.VMEM(early.shape, jnp.float32),
            pltpu.VMEM(sums_e.shape[1:], jnp.float32),
            padded,
            padded,
            pltpu.VMEM((top, LANES), jnp.float32),
            pltpu.VMEM((top, LANES), jnp.float32),
            pltpu.VMEM((top, LANES), jnp.float32),
            pltpu.SemaphoreType.DMA((CHUNKS,)),
            pltpu.SemaphoreType.DMA,
        ],
        compiler_params=pltpu.CompilerParams(vmem_limit_bytes=8 * 2**20),
        name="rest",
    )(early, ahead, dsum, counts, sums_e, means_a, profiles)


def on_device(dynamics, adjacency, cloud_state, span_source, substeps):
    devices = lax.axis_size("dev")
    carried = first(dynamics, adjacency, cloud_state, span_source, substeps, devices)
    dynamics_summed, tendency, cloud_new = rest(*carried)
    return dynamics_summed, jnp.transpose(tendency, (1, 0, 2)), cloud_new


def solution(mesh):
    in_specs = (
        P(None, None, "dev"),
        P(None, "dev"),
        P(None, None, None, "dev"),
        P("dev"),
        P("dev"),
    )
    out_specs = (P(None, None, "dev"), P(None, None, "dev"), P(None, None, None, "dev"))
    return jax.shard_map(on_device, mesh=mesh, in_specs=in_specs, out_specs=out_specs, check_vma=False)
```

```python
import functools

import jax
import jax.numpy as jnp
from jax import lax
from jax.experimental import pallas as pl
from jax.experimental.pallas import tpu as pltpu
from jax.sharding import PartitionSpec as P

LANES = 128
ROWS = 8
PAD = 8
CHUNKS = 6
AHEAD = 8
EARLY_CHUNKS = 2


def odious(node):
    return ((node ^ (node >> 1) ^ (node >> 2) ^ (node >> 3)) & 1) == 1


def edge_of(node):
    return jnp.where(
        (node == 1) | (node == 2), 0, jnp.where((node == 7) | (node == 11), 1, jnp.where((node == 14) | (node == 13), 2, 3))
    )


def which_of(node):
    return jnp.where((node == 2) | (node == 11) | (node == 13) | (node == 4), 1, 0)


def lanes(shape=(ROWS, LANES)):
    return lax.broadcasted_iota(jnp.int32, shape, len(shape) - 1)


def total_of(parts):
    while len(parts) > 1:
        parts = [a + b for a, b in zip(parts[::2], parts[1::2])] + ([parts[-1]] if len(parts) % 2 else [])
    return parts[0]


def mean_of(sums, width):
    blocks = []
    for start in range(0, sums.shape[0], ROWS * ROWS):
        blocks.append(total_of([sums[pl.ds(start + j, ROWS, stride=ROWS), :] for j in range(ROWS)]))
    return jnp.concatenate(blocks, axis=0) * (1.0 / width)


def spread(ref, values, depth):
    top = values.shape[0]
    ref[PAD : PAD + top, :] = values
    ref[PAD - 1 : PAD, :] = values[0:1]
    ref[PAD + depth : PAD + depth + 1, :] = values[depth - 1 : depth]
    return 8.0 * values + ref[PAD - 1 : PAD - 1 + top, :] + ref[PAD + 1 : PAD + 1 + top, :]


def saturation_of(top, depth):
    height = lax.broadcasted_iota(jnp.int32, (top, LANES), 0).astype(jnp.float32)
    return 0.8 * jnp.exp(-2.0 * height / depth)


def sweep(src, dst, which, active, bias, sums, limit, between=(), emit=None):
    depth = src.shape[1]
    parts = src.shape[2] // ROWS

    def load(z):
        return [src[which, z, k * ROWS : (k + 1) * ROWS, :] for k in range(parts)]

    def level(z, before, here):
        after = load(min(z + 1, depth - 1))
        left = pltpu.roll(here[parts - 1], 1, axis=0)
        right = pltpu.roll(here[0], ROWS - 1, axis=0)
        if bias is not None:
            shift = jnp.broadcast_to(bias[z : z + 1, :], (ROWS, LANES))
        stepped = []
        for k in range(parts):
            beside = (here[k - 1] if k > 0 else left) + (here[k + 1] if k < parts - 1 else right)
            value = 6.0 * here[k] + (beside + (before[k] + after[k]))
            if bias is not None:
                value = value + shift
            if limit:
                value = jnp.minimum(value, 0.25 * value)
            if active is not None:
                value = jnp.where(active, value, here[k])
            stepped.append(value)
            if emit is None:
                dst[which, z, k * ROWS : (k + 1) * ROWS, :] = value
        if emit is not None:
            emit(z, stepped)
        if sums is not None:
            sums[z * ROWS : (z + 1) * ROWS, :] = total_of(stepped)
        return here, after

    before = here = load(0)
    between = list(between)
    for z in range(depth):
        before, here = level(z, before, here)
        if between:
            between.pop(0)()
    for piece in between:
        piece()


def advance(scale, sums, terms, bias, pad_e, pad_a, now, later, width, depth, active=None):
    top = bias.shape[0]
    blocks = [(at, at + ROWS) for at in range(0, top, ROWS)]

    def spread_of(pad, lo, hi):
        return 8.0 * pad[PAD + lo : PAD + hi, :] + pad[PAD - 1 + lo : PAD - 1 + hi, :] + pad[PAD + 1 + lo : PAD + 1 + hi, :]

    def ends(pad):
        pad[PAD - 1 : PAD, :] = pad[PAD : PAD + 1, :]
        pad[PAD + depth : PAD + depth + 1, :] = pad[PAD + depth - 1 : PAD + depth, :]

    def mean_e(lo, hi):
        rows = [sums[pl.ds(lo * ROWS + j, ROWS, stride=ROWS), :] for j in range(ROWS)]
        pad_e[PAD + lo : PAD + hi, :] = total_of(rows) * (1.0 / width)

    def bias_e(lo, hi):
        bias[lo:hi, :] = scale * terms[3, lo:hi, :] - 0.3 * spread_of(pad_e, lo, hi)

    def relaxed_a(lo, hi):
        pad_a[PAD + lo : PAD + hi, :] = 0.7 * now[lo:hi, :] + terms[2, lo:hi, :]

    def mean_a(lo, hi):
        value = 0.1 * spread_of(pad_a, lo, hi)
        if active is not None:
            value = jnp.where(active, value, now[lo:hi, :])
        later[lo:hi, :] = value

    pieces = [functools.partial(mean_e, *block) for block in blocks] + [functools.partial(ends, pad_e)]
    pieces += [functools.partial(bias_e, *block) for block in blocks]
    pieces += [functools.partial(relaxed_a, *block) for block in blocks] + [functools.partial(ends, pad_a)]
    return pieces + [functools.partial(mean_a, *block) for block in blocks]


def split_dot(values, weights):
    upper = values.astype(jnp.bfloat16)
    lower = (values - upper.astype(jnp.float32)).astype(jnp.bfloat16)
    return jnp.dot(upper, weights, preferred_element_type=jnp.float32) + jnp.dot(lower, weights, preferred_element_type=jnp.float32)


def partner_places(me, devices, adjacency, elements, half):
    across = jnp.broadcast_to(adjacency[0:1, :], (ROWS, LANES))
    facing = jnp.broadcast_to(adjacency[1:2, :], (ROWS, LANES))
    block = (across // elements - me + devices) % devices
    part = jnp.where(block == 0, 0, jnp.where(block == 1, 2, 1))
    places = []
    for t in range(2):
        other = ((2, 1), (11, 7), (13, 14), (4, 8))
        node = jnp.where(
            facing == 0, other[0][t], jnp.where(facing == 1, other[1][t], jnp.where(facing == 2, other[2][t], other[3][t]))
        )
        place = (across % elements) * 16 + node
        in_pair = place % 256
        lane = jnp.where(in_pair < LANES, in_pair, (in_pair - LANES + 8) % LANES)
        places.append(part * half + (place // 256) * LANES + lane)
    return places


def packed_nodes(index):
    lane = index % LANES
    direct = odious(lane % 16)
    moved = (lane + LANES - 8) % LANES
    element = jnp.where(direct, lane // 16, 8 + moved // 16) + (index // LANES) * 16
    return element, jnp.where(direct, lane % 16, moved % 16)


def edge_weights(places, half):
    landing = []
    for v in range(half // LANES):
        element, node = packed_nodes(lanes() + v * LANES)
        index = 4 * element + edge_of(node)
        picked = [jnp.take_along_axis(p, index, axis=1, mode="promise_in_bounds") for p in places]
        landing.append(jnp.where(which_of(node) == 0, picked[0], picked[1])[0:1])
    landing = jnp.concatenate(landing, axis=1)
    row = lax.broadcasted_iota(jnp.int32, (3 * half, half), 0)
    return jnp.where(row == landing, 1.0, 0.0).astype(jnp.bfloat16)


def quarter_weights(element, node, keep):
    column = 4 * element + 2 * (node // 8) + (node % 4) // 2
    here = (column == lax.broadcasted_iota(jnp.int32, column.shape, 1)) & keep
    return jnp.where(here, 0.25, 0.0).astype(jnp.bfloat16)


def first_kernel(
    devices, span, bounds, dyn_hbm, adj_hbm, cloud_hbm, source_hbm, sub_hbm,
    early, state, dsum_ref, count_ref, sums_e, mean_a, profiles,
    loaded, dyn, adj, source_ref, sub_ref, edges, halo, outgoing, merged, arrived_y, arrived_z, arrived_x,
    sums, padded, padded_a, bias, bias_a,
    local_sems, in_sems, halo_send, halo_recv, leg_send, leg_recv,
):
    me = lax.axis_index("dev")
    strides = (devices // 4, devices // 16)
    member = me % ROWS
    above = (me + 1) % devices
    below = (me + devices - 1) % devices

    def along(stride, step):
        at = (me // stride) % 4
        to = (at + step) % 4
        return to, me + (to - at) * stride

    fields, levels, nodes = dyn.shape
    half = nodes // 2
    depth, width = loaded.shape[1], loaded.shape[2]
    parts = width // ROWS
    top = profiles.shape[1]

    barrier = pltpu.get_barrier_semaphore()

    def greet(device):
        pl.semaphore_signal(barrier, inc=1, device_id=(device,), device_id_type=pl.DeviceIdType.MESH)

    for stride in strides:
        for step in range(1, 4):
            greet(along(stride, step)[1])
    greet(above)
    greet(below)
    for step in range(1, ROWS):
        greet(me - member + (member + step) % ROWS)

    local = []
    for i, (src, dst) in enumerate(((dyn_hbm, dyn), (source_hbm, source_ref), (sub_hbm, sub_ref), (adj_hbm, adj))):
        local.append(pltpu.make_async_copy(src, dst, local_sems.at[i]))
        local[-1].start()
    loads = []
    for i, (lo, hi) in enumerate(bounds):
        loads.append(pltpu.make_async_copy(cloud_hbm.at[:, lo:hi], loaded.at[:, lo:hi], in_sems.at[i]))
        loads[-1].start()

    local[0].wait()
    on_edge = odious(lanes((levels, LANES)) % 16)
    for f in range(fields):
        for j in range(2):
            direct = dyn[f, :, 2 * j * LANES : (2 * j + 1) * LANES]
            later = dyn[f, :, (2 * j + 1) * LANES : (2 * j + 2) * LANES]
            edges[f, :, j * LANES : (j + 1) * LANES] = jnp.where(on_edge, direct, pltpu.roll(later, 8, axis=1))

    local[1].wait()
    local[2].wait()
    slot = lanes((1, LANES))
    counts = jnp.zeros((1, LANES), jnp.int32)
    for i in range(LANES // span):
        counts = jnp.where(slot // span == i, sub_ref[0:1, i : i + 1], counts)
    source = source_ref[...]
    target = lax.broadcasted_iota(jnp.int32, (devices, LANES), 0)
    to_device = jnp.where(source // LANES == target, counts, 0).astype(jnp.float32).astype(jnp.bfloat16)
    row = lax.broadcasted_iota(jnp.int32, (LANES, LANES), 0)
    to_lane = jnp.where(source % LANES == row, 1.0, 0.0).astype(jnp.bfloat16)
    message = lax.dot_general(to_device, to_lane, (((1,), (1,)), ((), ())), preferred_element_type=jnp.float32)
    outgoing[...] = message.astype(jnp.int32).reshape(outgoing.shape)

    local[3].wait()
    weights = edge_weights(partner_places(me, devices, adj, nodes // 16, half), half)
    row = lax.broadcasted_iota(jnp.int32, (nodes, LANES), 0)
    own_weights = quarter_weights(row // 16, row % 16, ~odious(row % 16))
    pool_weights = quarter_weights(*packed_nodes(lax.broadcasted_iota(jnp.int32, (half, LANES), 0)), True)
    rows = fields * levels
    force_own = split_dot(dyn[...].reshape(rows, nodes), own_weights)
    own_edges = edges[...].reshape(rows, half)
    opposite_own = split_dot(own_edges, weights[:half])

    def begin(z, carry):
        all_a, all_e = [], []
        for k in range(parts):
            u0 = loaded[0, z, pl.ds(k, ROWS, stride=parts), :]
            u1 = loaded[1, z, pl.ds(k, ROWS, stride=parts), :]
            all_a.append(u0 + u1)
            all_e.append(u1 - 0.5 * u0)
        for k in range(parts):
            loaded[0, z, k * ROWS : (k + 1) * ROWS, :] = all_a[k]
            loaded[1, z, k * ROWS : (k + 1) * ROWS, :] = all_e[k]
        at = pl.multiple_of(z * ROWS, ROWS)
        sums[0, pl.ds(at, ROWS), :] = total_of(all_a)
        sums[1, pl.ds(at, ROWS), :] = total_of(all_e)
        return carry

    def begin_part(part):
        for (lo, hi), copy in list(zip(bounds, loads))[part]:
            copy.wait()
            lax.fori_loop(lo, hi, begin, 0, unroll=2)

    begin_part(slice(0, EARLY_CHUNKS))

    pl.semaphore_wait(barrier, 2 + 3 + 3 + ROWS - 1)

    def send(src, dst, send_sem, recv_sem, device):
        copy = pltpu.make_async_remote_copy(
            src_ref=src, dst_ref=dst, send_sem=send_sem, recv_sem=recv_sem, device_id=(device,), device_id_type=pl.DeviceIdType.MESH
        )
        copy.start()
        return copy

    rows_y = outgoing.shape[0] // 4
    leg_y, leg_z, leg_x = [], [], []
    for step in range(1, 4):
        to, device = along(strides[0], step)
        leg_y.append(send(outgoing.at[pl.ds(to * rows_y, rows_y)], arrived_y.at[step], leg_send.at[step], leg_recv.at[step], device))
    up = send(edges, halo.at[0], halo_send.at[0], halo_recv.at[0], above)
    down = send(edges, halo.at[1], halo_send.at[1], halo_recv.at[1], below)

    begin_part(slice(EARLY_CHUNKS, CHUNKS))

    start_a = mean_of(sums.at[0], width)
    start_e = mean_of(sums.at[1], width)
    saturation = saturation_of(top, depth)
    bias_a[...] = -spread(padded, start_a, depth)
    sweep(loaded, early, 0, None, bias_a, None, False)
    sweep(early, state, 0, None, None, None, False)

    for copy in leg_y:
        copy.wait_recv()
    at_y = (me // strides[0]) % 4
    merged[...] = outgoing[pl.ds(at_y * rows_y, rows_y)] + arrived_y[1] + arrived_y[2] + arrived_y[3]
    for step in range(1, 4):
        to, device = along(strides[1], step)
        leg_z.append(send(merged.at[to], arrived_z.at[step], leg_send.at[3 + step], leg_recv.at[3 + step], device))

    def further(step, carry):
        sweep(state, state, 0, None, None, None, False)
        return carry

    lax.fori_loop(2, AHEAD, further, 0)

    up.wait()
    down.wait()
    values = jnp.concatenate([halo[i].reshape(rows, half) for i in range(2)], axis=1)
    averaged = 0.5 * (own_edges + (opposite_own + split_dot(values, weights[half:])))
    force = force_own + split_dot(averaged, pool_weights)
    force_0 = force[0:top]
    force_1 = force[levels : levels + top]
    force_e = force_1 - 0.5 * force_0
    force_a = force_0 + force_1
    bias[...] = spread(padded, 0.3 * (force_e - start_e), depth) - 10.0 * saturation
    sweep(loaded, early, 1, None, bias, sums_e.at[0], True)

    profiles[0] = start_a
    profiles[1] = start_e
    profiles[2] = 0.3 * force_a
    profiles[3] = spread(padded, saturation + 0.3 * (force_e - saturation), depth) - 10.0 * saturation
    mean_a[0] = 0.1 * spread(padded, 0.7 * start_a + 0.3 * force_a, depth)

    def onward(source, before, scale):
        pieces = advance(
            scale, sums_e.at[before], profiles, bias, padded, padded_a, mean_a.at[before], mean_a.at[1], width, depth
        )
        for piece in pieces:
            piece()
        sweep(source, state, 1, None, bias, sums_e.at[1], True)
        return scale * 10.0

    onward(early, 0, 10.0)
    for copy in leg_z:
        copy.wait_recv()
    at_z = (me // strides[1]) % 4
    arrived_x[0] = merged[at_z] + arrived_z[1] + arrived_z[2] + arrived_z[3]
    for step in range(1, ROWS):
        device = me - member + (member + step) % ROWS
        leg_x.append(send(arrived_x.at[0], arrived_x.at[step], leg_send.at[6 + step], leg_recv.at[6 + step], device))
    lax.fori_loop(2, AHEAD, lambda step, scale: onward(state, 1, scale), jnp.float32(100.0))

    averaged = averaged.reshape(fields, levels, half)
    for f in range(fields):
        for j in range(2):
            part = averaged[f, :, j * LANES : (j + 1) * LANES]
            for v, moved in ((2 * j, part), (2 * j + 1, pltpu.roll(part, LANES - 8, axis=1))):
                at = slice(v * LANES, (v + 1) * LANES)
                dsum_ref[f, :, at] = jnp.where(on_edge, moved, dyn[f, :, at])

    for copy in leg_x:
        copy.wait_recv()
    mine = total_of([arrived_x[i, pl.ds(member, 1), :] for i in range(ROWS)])
    count_ref[...] = jnp.broadcast_to(mine, (ROWS, LANES))
    for copy in leg_y + leg_z + leg_x:
        copy.wait_send()


def cut(depth):
    cuts = [round(i * depth / CHUNKS) for i in range(CHUNKS + 1)]
    return tuple(zip(cuts[:-1], cuts[1:]))


def first(dynamics, adjacency, cloud_state, span_source, substeps, devices):
    fields, levels, nodes = dynamics.shape
    depth, width = cloud_state.shape[1], cloud_state.shape[2]
    top = -(-depth // ROWS) * ROWS
    tiles = devices // ROWS
    span = span_source.shape[0] // substeps.shape[0]
    vmem = pl.BlockSpec(memory_space=pltpu.VMEM)
    hbm = pl.BlockSpec(memory_space=pltpu.HBM)
    profile = pltpu.VMEM((top, LANES), jnp.float32)
    return pl.pallas_call(
        functools.partial(first_kernel, devices, span, cut(depth)),
        out_shape=(
            jax.ShapeDtypeStruct(cloud_state.shape, jnp.float32),
            jax.ShapeDtypeStruct(cloud_state.shape, jnp.float32),
            jax.ShapeDtypeStruct(dynamics.shape, jnp.float32),
            jax.ShapeDtypeStruct((ROWS, LANES), jnp.int32),
            jax.ShapeDtypeStruct((2, top * ROWS, LANES), jnp.float32),
            jax.ShapeDtypeStruct((2, top, LANES), jnp.float32),
            jax.ShapeDtypeStruct((4, top, LANES), jnp.float32),
        ),
        in_specs=[hbm] * 5,
        out_specs=(vmem,) * 7,
        scratch_shapes=[
            pltpu.VMEM(cloud_state.shape, jnp.float32),
            pltpu.VMEM(dynamics.shape, jnp.float32),
            pltpu.VMEM(adjacency.shape, jnp.int32),
            pltpu.VMEM((1, LANES), jnp.int32),
            pltpu.VMEM((1, substeps.shape[0]), jnp.int32),
            pltpu.VMEM((fields, levels, nodes // 2), jnp.float32),
            pltpu.VMEM((2, fields, levels, nodes // 2), jnp.float32),
            pltpu.VMEM((tiles, ROWS, LANES), jnp.int32),
            pltpu.VMEM((tiles // 4, ROWS, LANES), jnp.int32),
            pltpu.VMEM((4, tiles // 4, ROWS, LANES), jnp.int32),
            pltpu.VMEM((4, ROWS, LANES), jnp.int32),
            pltpu.VMEM((ROWS, ROWS, LANES), jnp.int32),
            pltpu.VMEM((2, top * ROWS, LANES), jnp.float32),
            pltpu.VMEM((top + 2 * PAD, LANES), jnp.float32),
            pltpu.VMEM((top + 2 * PAD, LANES), jnp.float32),
            profile,
            profile,
            pltpu.SemaphoreType.DMA((4,)),
            pltpu.SemaphoreType.DMA((CHUNKS,)),
            pltpu.SemaphoreType.DMA((2,)),
            pltpu.SemaphoreType.DMA((2,)),
            pltpu.SemaphoreType.DMA((14,)),
            pltpu.SemaphoreType.DMA((14,)),
        ],
        compiler_params=pltpu.CompilerParams(collective_id=0, has_side_effects=True, vmem_limit_bytes=10 * 2**20),
        name="first",
    )(*[
        pltpu.with_memory_space_constraint(x, pltpu.HBM)
        for x in (dynamics, adjacency, cloud_state, span_source.reshape(1, -1), substeps.reshape(1, -1))
    ])


def rest_kernel(
    bounds, early, ahead, dsum_ref, count_ref, sums_e, means_a, profiles, dsum_out, tend_ref, new_ref,
    state, sums, padded, padded_a, mean_a, bias, add, out_sems, dsum_sem,
):
    depth, width = state.shape[1], state.shape[2]
    parts = width // ROWS
    top = bias.shape[0]
    dsum_copy = pltpu.make_async_copy(dsum_ref, dsum_out, dsum_sem)
    dsum_copy.start()

    counts = count_ref[...]
    least = jnp.min(counts)
    most = jnp.max(counts)
    saturation = saturation_of(top, depth)

    def substep(src, source_sums, source_mean, scale, active):
        pieces = advance(scale, source_sums, profiles, bias, padded, padded_a, source_mean, mean_a, width, depth, active)
        sweep(src, state, 0, active, None, None, False, pieces)
        sweep(src, state, 1, active, bias, sums, True)
        return scale * 10.0

    def plain(step, scale):
        return substep(state, sums, mean_a, scale, None)

    def masked(step, scale):
        return substep(state, sums, mean_a, scale, counts > step)

    @pl.when(least > AHEAD)
    def _():
        substep(ahead, sums_e.at[1], means_a.at[1], 10.0**AHEAD, None)

    @pl.when((least <= AHEAD) & (most > 2))
    def _():
        substep(early, sums_e.at[0], means_a.at[0], 10.0, counts > 1)

    shrink = jnp.ones((ROWS, LANES), jnp.float32)
    for step in range(12):
        shrink = jnp.where(counts > step, shrink * 0.1, shrink)
    shrink_0 = (2.0 / 3.0) * shrink
    copies = [
        pltpu.make_async_copy(state.at[:, lo:hi], new_ref.at[:, lo:hi], out_sems.at[i]) for i, (lo, hi) in enumerate(bounds)
    ]

    def finish(z, e):
        add_0 = jnp.broadcast_to(add[z : z + 1, :], (ROWS, LANES))
        add_a = jnp.broadcast_to(mean_a[z : z + 1, :], (ROWS, LANES))
        new_0, new_1 = [], []
        for k in range(parts):
            a = state[0, z, k * ROWS : (k + 1) * ROWS, :]
            u0 = (a - e[k]) * shrink_0 + add_0
            new_0.append(u0)
            new_1.append((a * shrink + add_a) - u0)
        for k in range(parts):
            state[0, z, pl.ds(k, ROWS, stride=parts), :] = new_0[k]
            state[1, z, pl.ds(k, ROWS, stride=parts), :] = new_1[k]
        for (_, hi), copy in zip(bounds, copies):
            if hi == z + 1:
                copy.start()

    def set_add():
        add[...] = (2.0 / 3.0) * (mean_a[...] - saturation)

    done = jnp.where(least > AHEAD, AHEAD + 1, 2)

    def last_substep(src, source_sums, source_mean, scale, active):
        pieces = advance(scale, source_sums, profiles, bias, padded, padded_a, source_mean, mean_a, width, depth, active)
        sweep(src, state, 0, active, None, None, False, pieces + [set_add])
        sweep(src, state, 1, active, bias, sums, True, (), finish)

    @pl.when(most > done)
    def _():
        scale = jnp.where(least > AHEAD, jnp.float32(10.0 ** (AHEAD + 1)), jnp.float32(100.0))
        middle = jnp.minimum(jnp.maximum(least, done), most - 1)
        scale = lax.fori_loop(done, middle, plain, scale)
        scale = lax.fori_loop(middle, most - 1, masked, scale)
        last_substep(state, sums, mean_a, scale, counts > most - 1)

    @pl.when(most <= 2)
    def _():
        last_substep(early, sums_e.at[0], means_a.at[0], 10.0, counts > 1)

    @pl.when((most <= done) & (most > 2))
    def _():
        set_add()
        for z in range(depth):
            finish(z, [state[1, z, k * ROWS : (k + 1) * ROWS, :] for k in range(parts)])

    new_a = mean_a[...]
    new_e = mean_of(sums, width) * shrink[0:1] + saturation
    old_a = profiles[0]
    old_e = profiles[1]
    tend_0 = (2.0 / 3.0) * ((new_a - new_e) - (old_a - old_e))
    tend_1 = (new_a - old_a) - tend_0
    tend_ref[:, 0, :] = tend_0[0:depth]
    tend_ref[:, 1, :] = tend_1[0:depth]
    for copy in copies:
        copy.wait()
    dsum_copy.wait()


def rest(early, ahead, dsum, counts, sums_e, means_a, profiles):
    fields, depth, width, _ = early.shape
    top = profiles.shape[1]
    vmem = pl.BlockSpec(memory_space=pltpu.VMEM)
    hbm = pl.BlockSpec(memory_space=pltpu.HBM)
    padded = pltpu.VMEM((top + 2 * PAD, LANES), jnp.float32)
    return pl.pallas_call(
        functools.partial(rest_kernel, cut(depth)),
        out_shape=(
            jax.ShapeDtypeStruct(dsum.shape, jnp.float32),
            jax.ShapeDtypeStruct((depth, fields, LANES), jnp.float32),
            jax.ShapeDtypeStruct(early.shape, jnp.float32),
        ),
        in_specs=[vmem] * 7,
        out_specs=(hbm, vmem, hbm),
        scratch_shapes=[
            pltpu.VMEM(early.shape, jnp.float32),
            pltpu.VMEM(sums_e.shape[1:], jnp.float32),
            padded,
            padded,
            pltpu.VMEM((top, LANES), jnp.float32),
            pltpu.VMEM((top, LANES), jnp.float32),
            pltpu.VMEM((top, LANES), jnp.float32),
            pltpu.SemaphoreType.DMA((CHUNKS,)),
            pltpu.SemaphoreType.DMA,
        ],
        compiler_params=pltpu.CompilerParams(vmem_limit_bytes=8 * 2**20),
        name="rest",
    )(early, ahead, dsum, counts, sums_e, means_a, profiles)


def on_device(dynamics, adjacency, cloud_state, span_source, substeps):
    devices = lax.axis_size("dev")
    carried = first(dynamics, adjacency, cloud_state, span_source, substeps, devices)
    dynamics_summed, tendency, cloud_new = rest(*carried)
    return dynamics_summed, jnp.transpose(tendency, (1, 0, 2)), cloud_new


def solution(mesh):
    in_specs = (
        P(None, None, "dev"),
        P(None, "dev"),
        P(None, None, None, "dev"),
        P("dev"),
        P("dev"),
    )
    out_specs = (P(None, None, "dev"), P(None, None, "dev"), P(None, None, None, "dev"))
    return jax.shard_map(on_device, mesh=mesh, in_specs=in_specs, out_specs=out_specs, check_vma=False)
```

```python
import functools

import jax
import jax.numpy as jnp
from jax import lax
from jax.experimental import pallas as pl
from jax.experimental.pallas import tpu as pltpu
from jax.sharding import PartitionSpec as P

LANES = 128
ROWS = 8
PAD = 8
CHUNKS = 6
OUT_CHUNKS = 12
AHEAD = 8
EARLY_CHUNKS = 2


def odious(node):
    return ((node ^ (node >> 1) ^ (node >> 2) ^ (node >> 3)) & 1) == 1


def edge_of(node):
    return jnp.where(
        (node == 1) | (node == 2), 0, jnp.where((node == 7) | (node == 11), 1, jnp.where((node == 14) | (node == 13), 2, 3))
    )


def which_of(node):
    return jnp.where((node == 2) | (node == 11) | (node == 13) | (node == 4), 1, 0)


def lanes(shape=(ROWS, LANES)):
    return lax.broadcasted_iota(jnp.int32, shape, len(shape) - 1)


def total_of(parts):
    while len(parts) > 1:
        parts = [a + b for a, b in zip(parts[::2], parts[1::2])] + ([parts[-1]] if len(parts) % 2 else [])
    return parts[0]


def mean_of(sums, width):
    blocks = []
    for start in range(0, sums.shape[0], ROWS * ROWS):
        blocks.append(total_of([sums[pl.ds(start + j, ROWS, stride=ROWS), :] for j in range(ROWS)]))
    return jnp.concatenate(blocks, axis=0) * (1.0 / width)


def spread(ref, values, depth):
    top = values.shape[0]
    ref[PAD : PAD + top, :] = values
    ref[PAD - 1 : PAD, :] = values[0:1]
    ref[PAD + depth : PAD + depth + 1, :] = values[depth - 1 : depth]
    return 8.0 * values + ref[PAD - 1 : PAD - 1 + top, :] + ref[PAD + 1 : PAD + 1 + top, :]


def saturation_of(top, depth):
    height = lax.broadcasted_iota(jnp.int32, (top, LANES), 0).astype(jnp.float32)
    return 0.8 * jnp.exp(-2.0 * height / depth)


def sweep(src, dst, which, active, bias, sums, limit, between=(), emit=None):
    depth = src.shape[1]
    parts = src.shape[2] // ROWS

    def load(z):
        return [src[which, z, k * ROWS : (k + 1) * ROWS, :] for k in range(parts)]

    def level(z, before, here):
        after = load(min(z + 1, depth - 1))
        left = pltpu.roll(here[parts - 1], 1, axis=0)
        right = pltpu.roll(here[0], ROWS - 1, axis=0)
        if bias is not None:
            shift = jnp.broadcast_to(bias[z : z + 1, :], (ROWS, LANES))
        stepped = []
        for k in range(parts):
            beside = (here[k - 1] if k > 0 else left) + (here[k + 1] if k < parts - 1 else right)
            value = 6.0 * here[k] + (beside + (before[k] + after[k]))
            if bias is not None:
                value = value + shift
            if limit:
                value = jnp.minimum(value, 0.25 * value)
            if active is not None:
                value = jnp.where(active, value, here[k])
            stepped.append(value)
            if emit is None:
                dst[which, z, k * ROWS : (k + 1) * ROWS, :] = value
        if emit is not None:
            emit(z, stepped)
        if sums is not None:
            sums[z * ROWS : (z + 1) * ROWS, :] = total_of(stepped)
        return here, after

    before = here = load(0)
    between = list(between)
    for z in range(depth):
        before, here = level(z, before, here)
        if between:
            between.pop(0)()
    for piece in between:
        piece()


def advance(scale, sums, terms, bias, pad_e, pad_a, now, later, width, depth, active=None):
    top = bias.shape[0]
    blocks = [(at, at + ROWS) for at in range(0, top, ROWS)]

    def spread_of(pad, lo, hi):
        return 8.0 * pad[PAD + lo : PAD + hi, :] + pad[PAD - 1 + lo : PAD - 1 + hi, :] + pad[PAD + 1 + lo : PAD + 1 + hi, :]

    def ends(pad):
        pad[PAD - 1 : PAD, :] = pad[PAD : PAD + 1, :]
        pad[PAD + depth : PAD + depth + 1, :] = pad[PAD + depth - 1 : PAD + depth, :]

    def mean_e(lo, hi):
        rows = [sums[pl.ds(lo * ROWS + j, ROWS, stride=ROWS), :] for j in range(ROWS)]
        pad_e[PAD + lo : PAD + hi, :] = total_of(rows) * (1.0 / width)

    def bias_e(lo, hi):
        bias[lo:hi, :] = scale * terms[3, lo:hi, :] - 0.3 * spread_of(pad_e, lo, hi)

    def relaxed_a(lo, hi):
        pad_a[PAD + lo : PAD + hi, :] = 0.7 * now[lo:hi, :] + terms[2, lo:hi, :]

    def mean_a(lo, hi):
        value = 0.1 * spread_of(pad_a, lo, hi)
        if active is not None:
            value = jnp.where(active, value, now[lo:hi, :])
        later[lo:hi, :] = value

    pieces = [functools.partial(mean_e, *block) for block in blocks] + [functools.partial(ends, pad_e)]
    pieces += [functools.partial(bias_e, *block) for block in blocks]
    pieces += [functools.partial(relaxed_a, *block) for block in blocks] + [functools.partial(ends, pad_a)]
    return pieces + [functools.partial(mean_a, *block) for block in blocks]


def split_dot(values, weights):
    upper = values.astype(jnp.bfloat16)
    lower = (values - upper.astype(jnp.float32)).astype(jnp.bfloat16)
    return jnp.dot(upper, weights, preferred_element_type=jnp.float32) + jnp.dot(lower, weights, preferred_element_type=jnp.float32)


def partner_places(me, devices, adjacency, elements, half):
    across = jnp.broadcast_to(adjacency[0:1, :], (ROWS, LANES))
    facing = jnp.broadcast_to(adjacency[1:2, :], (ROWS, LANES))
    block = (across // elements - me + devices) % devices
    part = jnp.where(block == 0, 0, jnp.where(block == 1, 2, 1))
    places = []
    for t in range(2):
        other = ((2, 1), (11, 7), (13, 14), (4, 8))
        node = jnp.where(
            facing == 0, other[0][t], jnp.where(facing == 1, other[1][t], jnp.where(facing == 2, other[2][t], other[3][t]))
        )
        place = (across % elements) * 16 + node
        in_pair = place % 256
        lane = jnp.where(in_pair < LANES, in_pair, (in_pair - LANES + 8) % LANES)
        places.append(part * half + (place // 256) * LANES + lane)
    return places


def packed_nodes(index):
    lane = index % LANES
    direct = odious(lane % 16)
    moved = (lane + LANES - 8) % LANES
    element = jnp.where(direct, lane // 16, 8 + moved // 16) + (index // LANES) * 16
    return element, jnp.where(direct, lane % 16, moved % 16)


def edge_weights(places, half):
    landing = []
    for v in range(half // LANES):
        element, node = packed_nodes(lanes() + v * LANES)
        index = 4 * element + edge_of(node)
        picked = [jnp.take_along_axis(p, index, axis=1, mode="promise_in_bounds") for p in places]
        landing.append(jnp.where(which_of(node) == 0, picked[0], picked[1])[0:1])
    landing = jnp.concatenate(landing, axis=1)
    row = lax.broadcasted_iota(jnp.int32, (3 * half, half), 0)
    return jnp.where(row == landing, 1.0, 0.0).astype(jnp.bfloat16)


def quarter_weights(element, node, keep):
    column = 4 * element + 2 * (node // 8) + (node % 4) // 2
    here = (column == lax.broadcasted_iota(jnp.int32, column.shape, 1)) & keep
    return jnp.where(here, 0.25, 0.0).astype(jnp.bfloat16)


def first_kernel(
    devices, span, bounds, dyn_hbm, adj_hbm, cloud_hbm, source_hbm, sub_hbm,
    early, state, dsum_ref, count_ref, sums_e, mean_a, profiles,
    loaded, dyn, adj, source_ref, sub_ref, edges, halo, outgoing, merged, arrived_y, arrived_z, arrived_x,
    sums, padded, padded_a, bias, bias_a,
    local_sems, in_sems, halo_send, halo_recv, leg_send, leg_recv,
):
    me = lax.axis_index("dev")
    strides = (devices // 4, devices // 16)
    member = me % ROWS
    above = (me + 1) % devices
    below = (me + devices - 1) % devices

    def along(stride, step):
        at = (me // stride) % 4
        to = (at + step) % 4
        return to, me + (to - at) * stride

    fields, levels, nodes = dyn.shape
    half = nodes // 2
    depth, width = loaded.shape[1], loaded.shape[2]
    parts = width // ROWS
    top = profiles.shape[1]

    barrier = pltpu.get_barrier_semaphore()

    def greet(device):
        pl.semaphore_signal(barrier, inc=1, device_id=(device,), device_id_type=pl.DeviceIdType.MESH)

    for stride in strides:
        for step in range(1, 4):
            greet(along(stride, step)[1])
    greet(above)
    greet(below)
    for step in range(1, ROWS):
        greet(me - member + (member + step) % ROWS)

    local = []
    for i, (src, dst) in enumerate(((dyn_hbm, dyn), (source_hbm, source_ref), (sub_hbm, sub_ref), (adj_hbm, adj))):
        local.append(pltpu.make_async_copy(src, dst, local_sems.at[i]))
        local[-1].start()
    loads = []
    for i, (lo, hi) in enumerate(bounds):
        loads.append(pltpu.make_async_copy(cloud_hbm.at[:, lo:hi], loaded.at[:, lo:hi], in_sems.at[i]))
        loads[-1].start()

    local[0].wait()
    on_edge = odious(lanes((levels, LANES)) % 16)
    for f in range(fields):
        for j in range(2):
            direct = dyn[f, :, 2 * j * LANES : (2 * j + 1) * LANES]
            later = dyn[f, :, (2 * j + 1) * LANES : (2 * j + 2) * LANES]
            edges[f, :, j * LANES : (j + 1) * LANES] = jnp.where(on_edge, direct, pltpu.roll(later, 8, axis=1))

    local[1].wait()
    local[2].wait()
    slot = lanes((1, LANES))
    counts = jnp.zeros((1, LANES), jnp.int32)
    for i in range(LANES // span):
        counts = jnp.where(slot // span == i, sub_ref[0:1, i : i + 1], counts)
    source = source_ref[...]
    target = lax.broadcasted_iota(jnp.int32, (devices, LANES), 0)
    to_device = jnp.where(source // LANES == target, counts, 0).astype(jnp.float32).astype(jnp.bfloat16)
    row = lax.broadcasted_iota(jnp.int32, (LANES, LANES), 0)
    to_lane = jnp.where(source % LANES == row, 1.0, 0.0).astype(jnp.bfloat16)
    message = lax.dot_general(to_device, to_lane, (((1,), (1,)), ((), ())), preferred_element_type=jnp.float32)
    outgoing[...] = message.astype(jnp.int32).reshape(outgoing.shape)

    local[3].wait()
    weights = edge_weights(partner_places(me, devices, adj, nodes // 16, half), half)
    row = lax.broadcasted_iota(jnp.int32, (nodes, LANES), 0)
    own_weights = quarter_weights(row // 16, row % 16, ~odious(row % 16))
    pool_weights = quarter_weights(*packed_nodes(lax.broadcasted_iota(jnp.int32, (half, LANES), 0)), True)
    rows = fields * levels
    force_own = split_dot(dyn[...].reshape(rows, nodes), own_weights)
    own_edges = edges[...].reshape(rows, half)
    opposite_own = split_dot(own_edges, weights[:half])

    def begin(z, carry):
        all_a, all_e = [], []
        for k in range(parts):
            u0 = loaded[0, z, pl.ds(k, ROWS, stride=parts), :]
            u1 = loaded[1, z, pl.ds(k, ROWS, stride=parts), :]
            all_a.append(u0 + u1)
            all_e.append(u1 - 0.5 * u0)
        for k in range(parts):
            loaded[0, z, k * ROWS : (k + 1) * ROWS, :] = all_a[k]
            loaded[1, z, k * ROWS : (k + 1) * ROWS, :] = all_e[k]
        at = pl.multiple_of(z * ROWS, ROWS)
        sums[0, pl.ds(at, ROWS), :] = total_of(all_a)
        sums[1, pl.ds(at, ROWS), :] = total_of(all_e)
        return carry

    def begin_part(part):
        for (lo, hi), copy in list(zip(bounds, loads))[part]:
            copy.wait()
            lax.fori_loop(lo, hi, begin, 0, unroll=2)

    begin_part(slice(0, EARLY_CHUNKS))

    pl.semaphore_wait(barrier, 2 + 3 + 3 + ROWS - 1)

    def send(src, dst, send_sem, recv_sem, device):
        copy = pltpu.make_async_remote_copy(
            src_ref=src, dst_ref=dst, send_sem=send_sem, recv_sem=recv_sem, device_id=(device,), device_id_type=pl.DeviceIdType.MESH
        )
        copy.start()
        return copy

    rows_y = outgoing.shape[0] // 4
    leg_y, leg_z, leg_x = [], [], []
    for step in range(1, 4):
        to, device = along(strides[0], step)
        leg_y.append(send(outgoing.at[pl.ds(to * rows_y, rows_y)], arrived_y.at[step], leg_send.at[step], leg_recv.at[step], device))
    up = send(edges, halo.at[0], halo_send.at[0], halo_recv.at[0], above)
    down = send(edges, halo.at[1], halo_send.at[1], halo_recv.at[1], below)

    begin_part(slice(EARLY_CHUNKS, CHUNKS))

    start_a = mean_of(sums.at[0], width)
    start_e = mean_of(sums.at[1], width)
    saturation = saturation_of(top, depth)
    bias_a[...] = -spread(padded, start_a, depth)
    sweep(loaded, early, 0, None, bias_a, None, False)
    sweep(early, state, 0, None, None, None, False)

    for copy in leg_y:
        copy.wait_recv()
    at_y = (me // strides[0]) % 4
    merged[...] = outgoing[pl.ds(at_y * rows_y, rows_y)] + arrived_y[1] + arrived_y[2] + arrived_y[3]
    for step in range(1, 4):
        to, device = along(strides[1], step)
        leg_z.append(send(merged.at[to], arrived_z.at[step], leg_send.at[3 + step], leg_recv.at[3 + step], device))

    def further(step, carry):
        sweep(state, state, 0, None, None, None, False)
        return carry

    lax.fori_loop(2, AHEAD, further, 0)

    up.wait()
    down.wait()
    values = jnp.concatenate([halo[i].reshape(rows, half) for i in range(2)], axis=1)
    averaged = 0.5 * (own_edges + (opposite_own + split_dot(values, weights[half:])))
    force = force_own + split_dot(averaged, pool_weights)
    force_0 = force[0:top]
    force_1 = force[levels : levels + top]
    force_e = force_1 - 0.5 * force_0
    force_a = force_0 + force_1
    bias[...] = spread(padded, 0.3 * (force_e - start_e), depth) - 10.0 * saturation
    sweep(loaded, early, 1, None, bias, sums_e.at[0], True)

    profiles[0] = start_a
    profiles[1] = start_e
    profiles[2] = 0.3 * force_a
    profiles[3] = spread(padded, saturation + 0.3 * (force_e - saturation), depth) - 10.0 * saturation
    mean_a[0] = 0.1 * spread(padded, 0.7 * start_a + 0.3 * force_a, depth)

    def onward(source, before, scale):
        pieces = advance(
            scale, sums_e.at[before], profiles, bias, padded, padded_a, mean_a.at[before], mean_a.at[1], width, depth
        )
        for piece in pieces:
            piece()
        sweep(source, state, 1, None, bias, sums_e.at[1], True)
        return scale * 10.0

    onward(early, 0, 10.0)
    for copy in leg_z:
        copy.wait_recv()
    at_z = (me // strides[1]) % 4
    arrived_x[0] = merged[at_z] + arrived_z[1] + arrived_z[2] + arrived_z[3]
    for step in range(1, ROWS):
        device = me - member + (member + step) % ROWS
        leg_x.append(send(arrived_x.at[0], arrived_x.at[step], leg_send.at[6 + step], leg_recv.at[6 + step], device))
    lax.fori_loop(2, AHEAD, lambda step, scale: onward(state, 1, scale), jnp.float32(100.0))

    averaged = averaged.reshape(fields, levels, half)
    for f in range(fields):
        for j in range(2):
            part = averaged[f, :, j * LANES : (j + 1) * LANES]
            for v, moved in ((2 * j, part), (2 * j + 1, pltpu.roll(part, LANES - 8, axis=1))):
                at = slice(v * LANES, (v + 1) * LANES)
                dsum_ref[f, :, at] = jnp.where(on_edge, moved, dyn[f, :, at])

    for copy in leg_x:
        copy.wait_recv()
    mine = total_of([arrived_x[i, pl.ds(member, 1), :] for i in range(ROWS)])
    count_ref[...] = jnp.broadcast_to(mine, (ROWS, LANES))
    for copy in leg_y + leg_z + leg_x:
        copy.wait_send()


def cut(depth, parts):
    cuts = [round(i * depth / parts) for i in range(parts + 1)]
    return tuple(zip(cuts[:-1], cuts[1:]))


def first(dynamics, adjacency, cloud_state, span_source, substeps, devices):
    fields, levels, nodes = dynamics.shape
    depth, width = cloud_state.shape[1], cloud_state.shape[2]
    top = -(-depth // ROWS) * ROWS
    tiles = devices // ROWS
    span = span_source.shape[0] // substeps.shape[0]
    vmem = pl.BlockSpec(memory_space=pltpu.VMEM)
    hbm = pl.BlockSpec(memory_space=pltpu.HBM)
    profile = pltpu.VMEM((top, LANES), jnp.float32)
    return pl.pallas_call(
        functools.partial(first_kernel, devices, span, cut(depth, CHUNKS)),
        out_shape=(
            jax.ShapeDtypeStruct(cloud_state.shape, jnp.float32),
            jax.ShapeDtypeStruct(cloud_state.shape, jnp.float32),
            jax.ShapeDtypeStruct(dynamics.shape, jnp.float32),
            jax.ShapeDtypeStruct((ROWS, LANES), jnp.int32),
            jax.ShapeDtypeStruct((2, top * ROWS, LANES), jnp.float32),
            jax.ShapeDtypeStruct((2, top, LANES), jnp.float32),
            jax.ShapeDtypeStruct((4, top, LANES), jnp.float32),
        ),
        in_specs=[hbm] * 5,
        out_specs=(vmem,) * 7,
        scratch_shapes=[
            pltpu.VMEM(cloud_state.shape, jnp.float32),
            pltpu.VMEM(dynamics.shape, jnp.float32),
            pltpu.VMEM(adjacency.shape, jnp.int32),
            pltpu.VMEM((1, LANES), jnp.int32),
            pltpu.VMEM((1, substeps.shape[0]), jnp.int32),
            pltpu.VMEM((fields, levels, nodes // 2), jnp.float32),
            pltpu.VMEM((2, fields, levels, nodes // 2), jnp.float32),
            pltpu.VMEM((tiles, ROWS, LANES), jnp.int32),
            pltpu.VMEM((tiles // 4, ROWS, LANES), jnp.int32),
            pltpu.VMEM((4, tiles // 4, ROWS, LANES), jnp.int32),
            pltpu.VMEM((4, ROWS, LANES), jnp.int32),
            pltpu.VMEM((ROWS, ROWS, LANES), jnp.int32),
            pltpu.VMEM((2, top * ROWS, LANES), jnp.float32),
            pltpu.VMEM((top + 2 * PAD, LANES), jnp.float32),
            pltpu.VMEM((top + 2 * PAD, LANES), jnp.float32),
            profile,
            profile,
            pltpu.SemaphoreType.DMA((4,)),
            pltpu.SemaphoreType.DMA((CHUNKS,)),
            pltpu.SemaphoreType.DMA((2,)),
            pltpu.SemaphoreType.DMA((2,)),
            pltpu.SemaphoreType.DMA((14,)),
            pltpu.SemaphoreType.DMA((14,)),
        ],
        compiler_params=pltpu.CompilerParams(collective_id=0, has_side_effects=True, vmem_limit_bytes=10 * 2**20),
        name="first",
    )(*[
        pltpu.with_memory_space_constraint(x, pltpu.HBM)
        for x in (dynamics, adjacency, cloud_state, span_source.reshape(1, -1), substeps.reshape(1, -1))
    ])


def rest_kernel(
    bounds, early, ahead, dsum_ref, count_ref, sums_e, means_a, profiles, dsum_out, tend_ref, new_ref,
    state, sums, padded, padded_a, mean_a, bias, add, out_sems, dsum_sem,
):
    depth, width = state.shape[1], state.shape[2]
    parts = width // ROWS
    top = bias.shape[0]
    dsum_copy = pltpu.make_async_copy(dsum_ref, dsum_out, dsum_sem)
    dsum_copy.start()

    counts = count_ref[...]
    least = jnp.min(counts)
    most = jnp.max(counts)
    saturation = saturation_of(top, depth)

    def substep(src, source_sums, source_mean, scale, active):
        pieces = advance(scale, source_sums, profiles, bias, padded, padded_a, source_mean, mean_a, width, depth, active)
        sweep(src, state, 0, active, None, None, False, pieces)
        sweep(src, state, 1, active, bias, sums, True)
        return scale * 10.0

    def plain(step, scale):
        return substep(state, sums, mean_a, scale, None)

    def masked(step, scale):
        return substep(state, sums, mean_a, scale, counts > step)

    @pl.when(least > AHEAD)
    def _():
        substep(ahead, sums_e.at[1], means_a.at[1], 10.0**AHEAD, None)

    @pl.when((least <= AHEAD) & (most > 2))
    def _():
        substep(early, sums_e.at[0], means_a.at[0], 10.0, counts > 1)

    shrink = jnp.ones((ROWS, LANES), jnp.float32)
    for step in range(12):
        shrink = jnp.where(counts > step, shrink * 0.1, shrink)
    shrink_0 = (2.0 / 3.0) * shrink
    copies = [
        pltpu.make_async_copy(state.at[:, lo:hi], new_ref.at[:, lo:hi], out_sems.at[i]) for i, (lo, hi) in enumerate(bounds)
    ]

    def finish(z, e):
        add_0 = jnp.broadcast_to(add[z : z + 1, :], (ROWS, LANES))
        add_a = jnp.broadcast_to(mean_a[z : z + 1, :], (ROWS, LANES))
        new_0, new_1 = [], []
        for k in range(parts):
            a = state[0, z, k * ROWS : (k + 1) * ROWS, :]
            u0 = (a - e[k]) * shrink_0 + add_0
            new_0.append(u0)
            new_1.append((a * shrink + add_a) - u0)
        for k in range(parts):
            state[0, z, pl.ds(k, ROWS, stride=parts), :] = new_0[k]
            state[1, z, pl.ds(k, ROWS, stride=parts), :] = new_1[k]
        for (_, hi), copy in zip(bounds, copies):
            if hi == z + 1:
                copy.start()

    def set_add():
        add[...] = (2.0 / 3.0) * (mean_a[...] - saturation)

    done = jnp.where(least > AHEAD, AHEAD + 1, 2)

    def last_substep(src, source_sums, source_mean, scale, active):
        pieces = advance(scale, source_sums, profiles, bias, padded, padded_a, source_mean, mean_a, width, depth, active)
        sweep(src, state, 0, active, None, None, False, pieces + [set_add])
        sweep(src, state, 1, active, bias, sums, True, (), finish)

    @pl.when(most > done)
    def _():
        scale = jnp.where(least > AHEAD, jnp.float32(10.0 ** (AHEAD + 1)), jnp.float32(100.0))
        middle = jnp.minimum(jnp.maximum(least, done), most - 1)
        scale = lax.fori_loop(done, middle, plain, scale)
        scale = lax.fori_loop(middle, most - 1, masked, scale)
        last_substep(state, sums, mean_a, scale, counts > most - 1)

    @pl.when(most <= 2)
    def _():
        last_substep(early, sums_e.at[0], means_a.at[0], 10.0, counts > 1)

    @pl.when((most <= done) & (most > 2))
    def _():
        set_add()
        for z in range(depth):
            finish(z, [state[1, z, k * ROWS : (k + 1) * ROWS, :] for k in range(parts)])

    new_a = mean_a[...]
    new_e = mean_of(sums, width) * shrink[0:1] + saturation
    old_a = profiles[0]
    old_e = profiles[1]
    tend_0 = (2.0 / 3.0) * ((new_a - new_e) - (old_a - old_e))
    tend_1 = (new_a - old_a) - tend_0
    tend_ref[:, 0, :] = tend_0[0:depth]
    tend_ref[:, 1, :] = tend_1[0:depth]
    for copy in copies:
        copy.wait()
    dsum_copy.wait()


def rest(early, ahead, dsum, counts, sums_e, means_a, profiles):
    fields, depth, width, _ = early.shape
    top = profiles.shape[1]
    vmem = pl.BlockSpec(memory_space=pltpu.VMEM)
    hbm = pl.BlockSpec(memory_space=pltpu.HBM)
    padded = pltpu.VMEM((top + 2 * PAD, LANES), jnp.float32)
    return pl.pallas_call(
        functools.partial(rest_kernel, cut(depth, OUT_CHUNKS)),
        out_shape=(
            jax.ShapeDtypeStruct(dsum.shape, jnp.float32),
            jax.ShapeDtypeStruct((depth, fields, LANES), jnp.float32),
            jax.ShapeDtypeStruct(early.shape, jnp.float32),
        ),
        in_specs=[vmem] * 7,
        out_specs=(hbm, vmem, hbm),
        scratch_shapes=[
            pltpu.VMEM(early.shape, jnp.float32),
            pltpu.VMEM(sums_e.shape[1:], jnp.float32),
            padded,
            padded,
            pltpu.VMEM((top, LANES), jnp.float32),
            pltpu.VMEM((top, LANES), jnp.float32),
            pltpu.VMEM((top, LANES), jnp.float32),
            pltpu.SemaphoreType.DMA((OUT_CHUNKS,)),
            pltpu.SemaphoreType.DMA,
        ],
        compiler_params=pltpu.CompilerParams(vmem_limit_bytes=8 * 2**20),
        name="rest",
    )(early, ahead, dsum, counts, sums_e, means_a, profiles)


def on_device(dynamics, adjacency, cloud_state, span_source, substeps):
    devices = lax.axis_size("dev")
    carried = first(dynamics, adjacency, cloud_state, span_source, substeps, devices)
    dynamics_summed, tendency, cloud_new = rest(*carried)
    return dynamics_summed, jnp.transpose(tendency, (1, 0, 2)), cloud_new


def solution(mesh):
    in_specs = (
        P(None, None, "dev"),
        P(None, "dev"),
        P(None, None, None, "dev"),
        P("dev"),
        P("dev"),
    )
    out_specs = (P(None, None, "dev"), P(None, None, "dev"), P(None, None, None, "dev"))
    return jax.shard_map(on_device, mesh=mesh, in_specs=in_specs, out_specs=out_specs, check_vma=False)
```
